32 devices in a mesh: head: 4 (over z), blk: 2 (over x), dp: 4 (over y, core).
Axes of the slice: x: 2, y: 2, z: 4, core: 2. Of those that a mesh axis runs over, the one named last changes fastest.
Arguments:
- tokens: bfloat16 [4, 2048, 768], P('dp', ('blk', 'head')), may hold values from -6 to 6
- first_gain: bfloat16 [768], replicated, may hold values from 0.5 to 1.5
- query_weight: bfloat16 [768, 768], replicated, may hold values from -0.21875 to 0.21875
- key_weight: bfloat16 [768, 768], replicated, may hold values from -0.21875 to 0.21875
- value_weight: bfloat16 [768, 768], replicated, may hold values from -0.21875 to 0.21875
- output_weight: bfloat16 [768, 768], replicated, may hold values from -7 to 7
- bias_table: bfloat16 [32, 12], replicated, may hold values from -6 to 6
- second_gain: bfloat16 [768], replicated, may hold values from 0.5 to 1.5
- router_weight: bfloat16 [768, 8], replicated, may hold values from -0.109375 to 0.109375
- inner_weight: bfloat16 [8, 768, 3072], P(('head', 'blk'), None, 'dp'), may hold values from -0.21875 to 0.21875
- outer_weight: bfloat16 [8, 3072, 768], P(('head', 'blk'), 'dp'), may hold values from -1.5 to 1.5
- expert_index: int32 [4, 2048], P('dp', ('blk', 'head')), may hold values from 0 to 7, as said below
- capacity_slot: int32 [4, 2048], P('dp', ('blk', 'head')), may hold values from 0 to 63, as said below
- bucket_of_offset: int32 [4095], replicated, may hold values from 0 to 31
- upstream: bfloat16 [4, 2048, 768], P('dp', ('blk', 'head')), may hold values from -6 to 6
Outputs:
- layer_output: bfloat16 [4, 2048, 768], P('dp', ('blk', 'head'))
- tokens_grad: bfloat16 [4, 2048, 768], P('dp', ('blk', 'head'))
- first_gain_grad: float32 [768], replicated
- query_weight_grad: float32 [768, 768], replicated
- key_weight_grad: float32 [768, 768], replicated
- value_weight_grad: float32 [768, 768], replicated
- output_weight_grad: float32 [768, 768], replicated
- bias_table_grad: float32 [32, 12], replicated
- second_gain_grad: float32 [768], replicated
- router_weight_grad: float32 [768, 8], replicated
- inner_weight_grad: float32 [8, 768, 3072], P(('head', 'blk'), None, 'dp')
- outer_weight_grad: float32 [8, 3072, 768], P(('head', 'blk'), 'dp')
The draws below stay inside these ranges and needn't reach their ends.
Inputs may be any that keep to these rules, and one draw needn't show every extreme that they name: `expert_index`: within each aligned block of 256 tokens (one device's tokens), no expert is named more than 64 times. `capacity_slot`: within each aligned block of 256 tokens, tokens that name the same expert have distinct slots.
All inputs are finite; a program needn't handle non-finite values.
Results may differ from the reference program's by a relative error of at most 0.017.
The reference program's roundings to bfloat16 on the way count: a program that leaves them out, or rounds other values in their place, can miss the bound.
Values may be sent and summed in bfloat16 or wider, within the bound.
No kernel may reach another device: no remote copies, remote signals or barrier semaphores. Data moves between devices by JAX's collectives and lax.ppermute only.
A program may use at most 320 MiB of HBM per device.

```python
import jax
import jax.numpy as jnp
from jax import lax

D = 768
HEADS = 12
HEAD_DIM = 64
FF = 3072
BUCKETS = 32
TOK_DEV = 256
SEQ_LEN = 2048
SEQS = 4
EXPERTS = 8
CAP = 64


def routing(key):
    blocks = SEQS * SEQ_LEN // TOK_DEV
    slot_total = EXPERTS * CAP
    key_fav, key_pop, key_jit, key_mix = jax.random.split(key, 4)
    favored = jax.random.randint(key_fav, (), 0, EXPERTS)
    popular = jax.random.randint(key_pop, (EXPERTS,), 0, 4)
    jitter = jax.random.randint(key_jit, (blocks, slot_total), 0, 4096)
    owners = jnp.arange(slot_total, dtype=jnp.int32) // CAP
    ranking = jitter - popular[owners][None, :] * 1024 - jnp.where(owners == favored, 16384, 0)[None, :]
    scores = ranking * slot_total + jnp.arange(slot_total, dtype=jnp.int32)[None, :]
    chosen = jnp.argsort(scores, axis=1)[:, :TOK_DEV]
    shuffle_keys = jax.random.randint(key_mix, (blocks, TOK_DEV), 0, 1 << 20) * TOK_DEV + jnp.arange(TOK_DEV, dtype=jnp.int32)[None, :]
    shuffle = jnp.argsort(shuffle_keys, axis=1)
    picked = jnp.take_along_axis(chosen, shuffle, axis=1)
    return picked.reshape(SEQS, SEQ_LEN).astype(jnp.int32)


def draw_expert_index(key, part):
    picked = routing(key)
    return (picked // CAP).astype(jnp.int32)


def draw_capacity_slot(key, part):
    picked = routing(key)
    return (picked % CAP).astype(jnp.int32)


def with_ends(array, own_key, smallest, largest):
    longest = array.shape.index(max(array.shape))
    spots = []
    for shift in (0, 1):
        where = [jax.random.randint(jax.random.fold_in(own_key, axis), (), 0, length) for axis, length in enumerate(array.shape)]
        where[longest] = (where[longest] + shift) % array.shape[longest]
        spots.append(tuple(where))
    return array.at[spots[0]].set(smallest).at[spots[1]].set(largest)


def steps_of(key, dims, cuts, low, high):
    loudness = 1.0
    for dim, shards_of in cuts:
        draws = jax.random.uniform(jax.random.fold_in(jax.random.fold_in(key, 6), dim), (shards_of,), jnp.float32, low / len(cuts), high / len(cuts))
        loudness = loudness * jnp.repeat(jnp.exp(draws), dims[dim] // shards_of).reshape((-1,) + (1,) * (len(dims) - 1 - dim))
    return loudness


def normal_values(rng, extent, scale, bound, shards=(), kind=jnp.bfloat16):
    array = jax.random.normal(rng, extent, jnp.float32) * scale
    if len(shards) > 0:
        array = steps_of(rng, extent, shards, -0.22, 0.18) * array
    return jnp.clip(array, min=-bound, max=bound).astype(kind)


def setup_inputs(seed: int = 0) -> dict:
    key_list = jax.random.split(jax.random.key(seed), 16)
    tokens = normal_values(key_list[0], (SEQS, SEQ_LEN, D), 1.0, 6.0, ((0, 4), (1, 8)))
    first_gain = jnp.clip(1.0 + 0.1 * jax.random.normal(key_list[1], (D,), jnp.float32), 0.5, 1.5).astype(jnp.bfloat16)
    query_weight = normal_values(key_list[2], (D, D), D ** -0.5, 0.21875)
    key_weight = normal_values(key_list[3], (D, D), D ** -0.5, 0.21875)
    value_weight = normal_values(key_list[4], (D, D), D ** -0.5, 0.21875)
    output_weight = normal_values(key_list[5], (D, D), (0.025 * SEQ_LEN ** 0.5), 7.0)
    bias_table = normal_values(key_list[6], (BUCKETS, HEADS), 1.0, 6.0)
    second_gain = jnp.clip(1.0 + 0.1 * jax.random.normal(key_list[7], (D,), jnp.float32), 0.5, 1.5).astype(jnp.bfloat16)
    router_weight = normal_values(key_list[8], (D, EXPERTS), (4 * D) ** -0.5, 0.109375)
    inner_weight = normal_values(key_list[9], (EXPERTS, D, FF), D ** -0.5, 0.21875, ((0, 8), (2, 4)))
    outer_weight = normal_values(key_list[10], (EXPERTS, FF, D), (0.032 * EXPERTS), 1.5, ((0, 8), (1, 4)))
    expert_index = draw_expert_index(jax.random.fold_in(key_list[15], 71), 0)
    capacity_slot = draw_capacity_slot(jax.random.fold_in(key_list[15], 71), 0)
    bucket_of_offset = with_ends(jax.random.randint(key_list[13], (2 * SEQ_LEN - 1,), 0, BUCKETS), jax.random.fold_in(key_list[13], 1), 0, BUCKETS - 1).astype(jnp.int32)
    upstream = normal_values(key_list[14], (SEQS, SEQ_LEN, D), 1.0, 6.0, ((0, 4), (1, 8)))
    return {"tokens": tokens, "first_gain": first_gain, "query_weight": query_weight, "key_weight": key_weight, "value_weight": value_weight, "output_weight": output_weight, "bias_table": bias_table, "second_gain": second_gain, "router_weight": router_weight, "inner_weight": inner_weight, "outer_weight": outer_weight, "expert_index": expert_index, "capacity_slot": capacity_slot, "bucket_of_offset": bucket_of_offset, "upstream": upstream}


@jax.custom_vjp
def low(v):
    return lax.optimization_barrier(v.astype(jnp.bfloat16)).astype(jnp.float32)

@jax.custom_vjp
def low_back(v):
    return v

def low_keep(v):
    return (low(v), None)

def low_pass(kept, grad):
    return (grad,)

def back_keep(v):
    return (v, None)

def back_low(kept, grad):
    return (low(grad),)
low.defvjp(low_keep, low_pass)
low_back.defvjp(back_keep, back_low)
EPSILON = 1e-06
PRECISE = lax.Precision.HIGHEST

def rms_scale(values, gain_row):
    return values * lax.rsqrt(lax.optimization_barrier(jnp.mean(values * values, axis=-1, keepdims=True)) + EPSILON) * gain_row

def head_attention(query_head, key_head, value_head, bias_head):
    scores = low_back(jnp.dot(query_head, key_head.T, precision=PRECISE) * 0.125 + bias_head)
    weights = jnp.exp(scores)
    denominator = lax.optimization_barrier(jnp.sum(weights, axis=-1))
    numerator = low_back(jnp.dot(low(weights), value_head, precision=PRECISE))
    return numerator / denominator[:, None]

def sequence_block(sequence, first_gain, query_weight, key_weight, value_weight, output_weight, bias_table, bucket_of_offset):
    normed = low(rms_scale(sequence, first_gain))
    queries = low_back(low(jnp.dot(normed, query_weight, precision=PRECISE)))
    key_rows = low_back(low(jnp.dot(normed, key_weight, precision=PRECISE)))
    value_rows = low_back(low(jnp.dot(normed, value_weight, precision=PRECISE)))
    position = jnp.arange(SEQ_LEN, dtype=jnp.int32)
    offsets = (position[None, :] - position[:, None] + SEQ_LEN - 1).astype(jnp.int32)
    bucket_map = bucket_of_offset[offsets]

    def split_heads(values):
        return values.reshape(SEQ_LEN, HEADS, HEAD_DIM).transpose(1, 0, 2)

    def one_head(pieces):
        query_head, key_head, value_head, column = pieces
        return head_attention(query_head, key_head, value_head, column[bucket_map])
    attended = lax.map(jax.checkpoint(one_head), (split_heads(queries), split_heads(key_rows), split_heads(value_rows), bias_table.T))
    attended = low_back(low(attended.transpose(1, 0, 2).reshape(SEQ_LEN, D)))
    return sequence + low_back(jnp.dot(attended, output_weight, precision=PRECISE))

def expert_block(pieces):
    expert_rows, inner_mat, outer_mat = pieces
    hidden_pre = low_back(jnp.dot(expert_rows, inner_mat, precision=PRECISE))
    hidden_act = low(jax.nn.gelu(hidden_pre, approximate=True))
    return low_back(low(jnp.dot(hidden_act, outer_mat, precision=PRECISE)))

def forward(tokens, first_gain, query_weight, key_weight, value_weight, output_weight, bias_table, second_gain, router_weight, inner_weight, outer_weight, expert_index, capacity_slot, bucket_of_offset):

    def attend(sequence):
        return sequence_block(sequence, first_gain, query_weight, key_weight, value_weight, output_weight, bias_table, bucket_of_offset)
    residual = lax.map(jax.checkpoint(attend), tokens)
    flattened = residual.reshape(SEQS * SEQ_LEN, D)
    normed = low(rms_scale(flattened, second_gain))
    logits = low_back(jnp.dot(normed, router_weight, precision=PRECISE))
    router_probs = jax.nn.softmax(logits, axis=-1)
    chosen = expert_index.reshape(-1).astype(jnp.int32)
    chosen_mask = (chosen[:, None] == jnp.arange(EXPERTS, dtype=jnp.int32)[None, :]).astype(jnp.float32)
    gate_value = lax.optimization_barrier(jnp.sum(router_probs * chosen_mask, axis=-1))
    blocks = SEQS * SEQ_LEN // TOK_DEV
    block_of = (jnp.arange(SEQS * SEQ_LEN, dtype=jnp.int32) // TOK_DEV).astype(jnp.int32)
    slot_place = ((chosen * blocks + block_of) * CAP + capacity_slot.reshape(-1)).astype(jnp.int32)
    buffer = jnp.zeros((EXPERTS * blocks * CAP, D), jnp.float32).at[slot_place].set(low_back(normed))
    returned = lax.map(jax.checkpoint(expert_block), (buffer.reshape(EXPERTS, blocks * CAP, D), inner_weight, outer_weight))
    expert_out = returned.reshape(EXPERTS * blocks * CAP, D)[slot_place]
    layer_output = flattened + gate_value[:, None] * expert_out
    return layer_output.reshape(SEQS, SEQ_LEN, D)

def reference(tokens, first_gain, query_weight, key_weight, value_weight, output_weight, bias_table, second_gain, router_weight, inner_weight, outer_weight, expert_index, capacity_slot, bucket_of_offset, upstream):
    floats = (tokens.astype(jnp.float32), first_gain.astype(jnp.float32), query_weight.astype(jnp.float32), key_weight.astype(jnp.float32), value_weight.astype(jnp.float32), output_weight.astype(jnp.float32), bias_table.astype(jnp.float32), second_gain.astype(jnp.float32), router_weight.astype(jnp.float32), inner_weight.astype(jnp.float32), outer_weight.astype(jnp.float32))

    def wrapped(*values):
        return forward(*values, expert_index, capacity_slot, bucket_of_offset)
    layer_output, pullback = jax.vjp(wrapped, *floats)
    gradients = pullback(upstream.astype(jnp.float32))
    return (layer_output.astype(jnp.bfloat16), gradients[0].astype(jnp.bfloat16), gradients[1], gradients[2], gradients[3], gradients[4], gradients[5], gradients[6], gradients[7], gradients[8], gradients[9], gradients[10])
```

```python
import functools

import jax
import jax.numpy as jnp
from jax import lax
from jax.experimental import pallas as pl
from jax.experimental.pallas import tpu as pltpu
from jax.sharding import PartitionSpec as P

HEAD_DIM = 64


EPSILON = 1e-06
PRECISE = lax.Precision.HIGHEST


def rms_scale(values, gain_row):
    return (
        values * lax.rsqrt(jnp.mean(values * values, axis=-1, keepdims=True) + EPSILON) * gain_row
    )


def gelu_tanh(values):
    return jax.nn.gelu(values, approximate=True)


def round_low(values):
    return values.astype(jnp.bfloat16)


def contract_first(former, latter):
    return lax.dot_general(
        former, latter, (((0,), (0,)), ((), ())), preferred_element_type=jnp.float32
    )


def contract_last(former, latter):
    return lax.dot_general(
        former, latter, (((1,), (1,)), ((), ())), preferred_element_type=jnp.float32
    )


STRIP = 128
VMEM_BYTES = 60 * 2**20


def dot_nt(former, latter):
    return lax.dot_general(
        former, latter, (((1,), (1,)), ((), ())), preferred_element_type=jnp.float32
    )


def dot_nn(former, latter):
    return lax.dot_general(
        former, latter, (((1,), (0,)), ((), ())), preferred_element_type=jnp.float32
    )


def head_mask(shape, head):
    lane = lax.broadcasted_iota(jnp.int32, shape, 1)
    return (lane >= head * HEAD_DIM) & (lane < (head + 1) * HEAD_DIM)


def whole_block(shape):
    return pl.BlockSpec(shape, lambda i: (0,) * len(shape), pipeline_mode=pl.Buffered(1))


def over_chunks(count, body, initial):
    if count > 4:
        return lax.fori_loop(0, count, body, initial)
    running = initial
    for number in range(count):
        running = body(number, running)
    return running


def strips_kernel(window_ref, strips_ref, *, heads, span):
    breadth = window_ref.shape[1]
    for head in range(heads):
        spread = jnp.broadcast_to(window_ref[head : head + 1, :], (STRIP, breadth))
        turned = pltpu.roll(spread, breadth - (STRIP - 1), 1, stride=1, stride_axis=0)
        strips_ref[head] = turned[:, :span]


def make_strips(window, span):
    heads = window.shape[0]
    return pl.pallas_call(
        functools.partial(strips_kernel, heads=heads, span=span),
        out_shape=jax.ShapeDtypeStruct((heads, STRIP, span), jnp.float32),
        compiler_params=pltpu.CompilerParams(vmem_limit_bytes=VMEM_BYTES),
        name="bias_strips",
    )(window)


def attend_kernel(
    query_ref, key_ref, value_ref, strips_ref, att_ref, low_ref, den_ref, weight_ref, *, heads, chunk, rows
):
    tile = query_ref.shape[0]
    length = key_ref.shape[0]
    step = pl.program_id(0)
    queries = query_ref[...] * jnp.asarray(0.125, jnp.bfloat16)
    out = jnp.zeros(queries.shape, jnp.float32)
    den_out = jnp.ones(queries.shape, jnp.float32)
    for head in range(heads):
        mask = head_mask(queries.shape, head)
        masked = jnp.where(mask, queries, jnp.zeros_like(queries))

        def body(number, running):
            numerator, lanes = running
            at = pl.multiple_of(number * chunk, chunk)
            scores = dot_nt(masked, key_ref[pl.ds(at, chunk), :])
            parts = []
            for sub in range(tile // STRIP):
                start = pl.multiple_of(rows - STRIP - (step * tile + sub * STRIP) + at, STRIP)
                parts.append(
                    jnp.exp(
                        scores[sub * STRIP : (sub + 1) * STRIP, :]
                        + strips_ref[head, :, pl.ds(start, chunk)]
                    )
                )
            weights = jnp.concatenate(parts, 0)
            for group in range(chunk // 128):
                lanes = lanes + weights[:, group * 128 : (group + 1) * 128]
            low = weights.astype(jnp.bfloat16)
            weight_ref[head, :, pl.ds(at, chunk)] = low
            return numerator + dot_nn(low, value_ref[pl.ds(at, chunk), :]), lanes

        initial = (jnp.zeros(queries.shape, jnp.float32), jnp.zeros((tile, 128), jnp.float32))
        numerator, lanes = over_chunks(length // chunk, body, initial)
        total = jnp.sum(lanes, axis=1, keepdims=True)
        out = jnp.where(mask, numerator / total, out)
        den_out = jnp.where(mask, total, den_out)
    att_ref[...] = out
    low_ref[...] = out.astype(jnp.bfloat16)
    den_ref[...] = den_out


def tile_of(length):
    return 256 if length <= 2048 else 128


def attend(queries, keys, values, strips):
    rows, width = queries.shape
    length = keys.shape[0]
    heads = width // HEAD_DIM
    tile = tile_of(length)
    block = pl.BlockSpec((tile, width), lambda i: (i, 0))
    return pl.pallas_call(
        functools.partial(attend_kernel, heads=heads, chunk=512, rows=rows),
        grid=(rows // tile,),
        in_specs=[
            block,
            whole_block((length, width)),
            whole_block((length, width)),
            whole_block(strips.shape),
        ],
        out_specs=[
            block,
            block,
            block,
            pl.BlockSpec((heads, tile, length), lambda i: (0, i, 0)),
        ],
        out_shape=[
            jax.ShapeDtypeStruct((rows, width), jnp.float32),
            jax.ShapeDtypeStruct((rows, width), jnp.bfloat16),
            jax.ShapeDtypeStruct((rows, width), jnp.float32),
            jax.ShapeDtypeStruct((heads, rows, length), jnp.bfloat16),
        ],
        compiler_params=pltpu.CompilerParams(vmem_limit_bytes=VMEM_BYTES),
        name="attend",
    )(queries, keys, values, strips)


def attend_back_kernel(
    query_ref,
    grad_ref,
    att_ref,
    den_ref,
    weight_ref,
    key_ref,
    value_ref,
    query_back_ref,
    key_back_ref,
    value_back_ref,
    diagonal_ref,
    strips_ref,
    key_acc,
    value_acc,
    *,
    heads,
    chunk,
    rows,
):
    tile = query_ref.shape[0]
    length = key_ref.shape[0]
    span = strips_ref.shape[2]
    step = pl.program_id(0)

    @pl.when(step == 0)
    def _():
        strips_ref[...] = jnp.zeros_like(strips_ref)
        key_acc[...] = jnp.zeros_like(key_acc)
        value_acc[...] = jnp.zeros_like(value_acc)

    queries = query_ref[...] * jnp.asarray(0.125, jnp.bfloat16)
    grads = grad_ref[...].astype(jnp.float32)
    total = den_ref[...]
    numer_back = (grads / total).astype(jnp.bfloat16)
    products = -(grads * att_ref[...]) / total
    query_turned = queries.astype(jnp.float32).T.astype(jnp.bfloat16)
    numer_turned = numer_back.astype(jnp.float32).T.astype(jnp.bfloat16)
    out = jnp.zeros(queries.shape, jnp.float32)
    for head in range(heads):
        mask = head_mask(queries.shape, head)
        masked = jnp.where(mask, numer_back, jnp.zeros_like(numer_back))
        denom_back = jnp.sum(jnp.where(mask, products, 0.0), axis=1, keepdims=True)
        here = slice(head * HEAD_DIM, (head + 1) * HEAD_DIM)
        query_here = query_turned[here]
        numer_here = numer_turned[here]

        def body(number, running):
            at = pl.multiple_of(number * chunk, chunk)
            weight_back = dot_nt(masked, value_ref[pl.ds(at, chunk), :])
            weights = weight_ref[head, :, pl.ds(at, chunk)]
            score_back = weights.astype(jnp.float32) * (weight_back + denom_back)
            low = score_back.astype(jnp.bfloat16)
            for sub in range(tile // STRIP):
                start = pl.multiple_of(rows - STRIP - (step * tile + sub * STRIP) + at, STRIP)
                strips_ref[head, :, pl.ds(start, chunk)] += score_back[
                    sub * STRIP : (sub + 1) * STRIP, :
                ]
            key_acc[here, pl.ds(at, chunk)] += dot_nn(query_here, low)
            value_acc[here, pl.ds(at, chunk)] += dot_nn(numer_here, weights)
            return running + dot_nn(low, key_ref[pl.ds(at, chunk), :])

        query_back = over_chunks(
            length // chunk, body, jnp.zeros(queries.shape, jnp.float32)
        )
        out = jnp.where(mask, query_back * 0.125, out)
    query_back_ref[...] = out.astype(jnp.bfloat16)

    @pl.when(step == pl.num_programs(0) - 1)
    def _():
        def finish(number, unused):
            at = pl.multiple_of(number * chunk, chunk)
            key_back_ref[pl.ds(at, chunk), :] = key_acc[:, pl.ds(at, chunk)].T.astype(jnp.bfloat16)
            value_back_ref[pl.ds(at, chunk), :] = value_acc[:, pl.ds(at, chunk)].T.astype(
                jnp.bfloat16
            )
            return unused

        lax.fori_loop(0, length // chunk, finish, 0)
        for head in range(heads):
            folded = strips_ref[head]
            size = STRIP
            while size > 8:
                size //= 2
                folded = folded[:size] + pltpu.roll(folded[size:], span - size, 1)
            row = folded[0:1]
            for place in range(1, 8):
                row = row + pltpu.roll(folded[place : place + 1], span - place, 1)
            diagonal_ref[head : head + 1, :] = row


def attend_back(queries, grads, attended, total, weights, keys, values):
    rows, width = queries.shape
    length = keys.shape[0]
    heads = width // HEAD_DIM
    tile = tile_of(length)
    span = length + rows
    block = pl.BlockSpec((tile, width), lambda i: (i, 0))
    return pl.pallas_call(
        functools.partial(attend_back_kernel, heads=heads, chunk=512, rows=rows),
        grid=(rows // tile,),
        in_specs=[
            block,
            block,
            block,
            block,
            pl.BlockSpec((heads, tile, length), lambda i: (0, i, 0)),
            whole_block((length, width)),
            whole_block((length, width)),
        ],
        out_specs=[
            block,
            whole_block((length, width)),
            whole_block((length, width)),
            whole_block((heads, span)),
        ],
        out_shape=[
            jax.ShapeDtypeStruct((rows, width), jnp.bfloat16),
            jax.ShapeDtypeStruct((length, width), jnp.bfloat16),
            jax.ShapeDtypeStruct((length, width), jnp.bfloat16),
            jax.ShapeDtypeStruct((heads, span), jnp.float32),
        ],
        scratch_shapes=[
            pltpu.VMEM((heads, STRIP, span), jnp.float32),
            pltpu.VMEM((width, length), jnp.float32),
            pltpu.VMEM((width, length), jnp.float32),
        ],
        compiler_params=pltpu.CompilerParams(vmem_limit_bytes=VMEM_BYTES),
        name="attend_back",
    )(queries, grads, attended, total, weights, keys, values)


def to_experts(slots):
    return lax.all_to_all(slots, ("head", "blk"), split_axis=0, concat_axis=1, tiled=True)[0]


def to_tokens(rows):
    return lax.all_to_all(rows[None], ("head", "blk"), split_axis=1, concat_axis=0, tiled=True)


def body(
    tokens,
    first_gain,
    query_weight,
    key_weight,
    value_weight,
    output_weight,
    bias_table,
    second_gain,
    router_weight,
    inner_weight,
    outer_weight,
    expert_index,
    capacity_slot,
    bucket_of_offset,
    upstream,
):
    token_rows = tokens.shape[1]
    model_width = tokens.shape[2]
    residual_in = tokens[0].astype(jnp.float32)
    gain_one = first_gain.astype(jnp.float32)
    normed_one = round_low(rms_scale(residual_in, gain_one))
    query_tok = round_low(jnp.dot(normed_one, query_weight, preferred_element_type=jnp.float32))
    key_tok = round_low(jnp.dot(normed_one, key_weight, preferred_element_type=jnp.float32))
    value_tok = round_low(jnp.dot(normed_one, value_weight, preferred_element_type=jnp.float32))
    query_heads, key_heads, value_heads = (
        lax.all_to_all(query_tok, "head", split_axis=1, concat_axis=0, tiled=True),
        lax.all_to_all(key_tok, "head", split_axis=1, concat_axis=0, tiled=True),
        lax.all_to_all(value_tok, "head", split_axis=1, concat_axis=0, tiled=True),
    )
    local_rows = query_heads.shape[0]
    local_width = query_heads.shape[1]
    heads_here = local_width // HEAD_DIM
    cycle_size = lax.axis_size("blk")
    length = local_rows * cycle_size
    all_keys, all_values = (
        lax.all_gather(key_heads, "blk", axis=0, tiled=True),
        lax.all_gather(value_heads, "blk", axis=0, tiled=True),
    )
    head_start = lax.axis_index("head") * heads_here
    bucket_count = bias_table.shape[0]
    lookup = (
        bucket_of_offset[:, None] == jnp.arange(bucket_count, dtype=jnp.int32)[None, :]
    ).astype(jnp.float32)
    lookup = jnp.pad(lookup, ((0, 1), (0, 0)))
    span = length + local_rows
    window_start = length - (lax.axis_index("blk") + 1) * local_rows
    lookup_window = lax.dynamic_slice_in_dim(lookup, window_start, span, 0)
    table_here = lax.dynamic_slice_in_dim(bias_table.astype(jnp.float32), head_start, heads_here, 1)
    offset_bias = jnp.dot(lookup_window, table_here, precision=PRECISE).T
    strips = make_strips(offset_bias, span - STRIP)
    attended, attended_low, total_rows, weights_low = attend(
        query_heads, all_keys, all_values, strips
    )
    attended_tok = lax.all_to_all(attended_low, "head", split_axis=0, concat_axis=1, tiled=True)
    residual_mid = residual_in + jnp.dot(
        attended_tok, output_weight, preferred_element_type=jnp.float32
    )
    gain_two = second_gain.astype(jnp.float32)
    normed_two = round_low(rms_scale(residual_mid, gain_two))
    logits = jnp.dot(normed_two, router_weight, preferred_element_type=jnp.float32)
    router_probs = jax.nn.softmax(logits, axis=-1)
    expert_count = router_weight.shape[1]
    capacity = max(2, 2 * token_rows // expert_count)
    chosen = expert_index[0]
    chosen_mask = (chosen[:, None] == jnp.arange(expert_count, dtype=jnp.int32)[None, :]).astype(
        jnp.float32
    )
    gate_value = jnp.sum(router_probs * chosen_mask, axis=-1)
    slot_place = chosen * capacity + capacity_slot[0]
    slot_rows = expert_count * capacity
    outgoing = jnp.zeros((slot_rows, model_width), jnp.bfloat16).at[slot_place].set(normed_two)
    expert_rows = to_experts(outgoing.reshape(expert_count, capacity, model_width))
    inner_full, outer_full = (
        lax.all_gather(inner_weight[0], "dp", axis=1, tiled=True),
        lax.all_gather(outer_weight[0], "dp", axis=0, tiled=True),
    )
    hidden_pre = jnp.dot(expert_rows, inner_full, preferred_element_type=jnp.float32)
    hidden_act = round_low(gelu_tanh(hidden_pre))
    expert_result = round_low(jnp.dot(hidden_act, outer_full, preferred_element_type=jnp.float32))
    returned = to_tokens(expert_result).reshape(slot_rows, model_width)
    expert_out = returned[slot_place].astype(jnp.float32)
    layer_output = residual_mid + gate_value[:, None] * expert_out
    incoming = upstream[0].astype(jnp.float32)
    gate_back = jnp.sum(incoming * expert_out, axis=-1)
    out_back = round_low(gate_value[:, None] * incoming)
    outgoing_back = jnp.zeros((slot_rows, model_width), jnp.bfloat16).at[slot_place].set(out_back)
    result_back = to_experts(outgoing_back.reshape(expert_count, capacity, model_width))
    unused, gelu_pull = jax.vjp(gelu_tanh, hidden_pre)
    outer_grad_full = contract_first(hidden_act, result_back)
    act_back = contract_last(result_back, outer_full)
    pre_back = round_low(gelu_pull(act_back)[0])
    inner_grad_full = contract_first(expert_rows, pre_back)
    rows_back = round_low(contract_last(pre_back, inner_full))
    inner_part, outer_part = (
        lax.psum_scatter(
            inner_grad_full.astype(jnp.bfloat16), "dp", scatter_dimension=1, tiled=True
        ).astype(jnp.float32),
        lax.psum_scatter(
            outer_grad_full.astype(jnp.bfloat16), "dp", scatter_dimension=0, tiled=True
        ).astype(jnp.float32),
    )
    rows_home = to_tokens(rows_back).reshape(slot_rows, model_width)
    expert_back = rows_home[slot_place].astype(jnp.float32)
    logit_back = round_low(router_probs * gate_back[:, None] * (chosen_mask - gate_value[:, None]))
    router_grad = contract_first(normed_two, logit_back)
    normed_two_back = contract_last(logit_back, router_weight) + expert_back
    unused, second_pull = jax.vjp(rms_scale, residual_mid, gain_two)
    mid_from_norm, second_gain_grad = second_pull(normed_two_back)
    residual_back = incoming + mid_from_norm
    branch_back = round_low(residual_back)
    output_grad = contract_first(attended_tok, branch_back)
    attended_back = round_low(contract_last(branch_back, output_weight))
    attended_heads = lax.all_to_all(
        attended_back, "head", split_axis=1, concat_axis=0, tiled=True
    )
    query_back, key_parts, value_parts, diagonals = attend_back(
        query_heads, attended_heads, attended, total_rows, weights_low, all_keys, all_values
    )
    diagonals = jnp.roll(diagonals, STRIP - 1, axis=1)
    bucket_acc = jnp.dot(diagonals, lookup_window, precision=PRECISE)
    key_home, value_home = (
        lax.psum_scatter(
            key_parts,
            "blk",
            scatter_dimension=0,
            tiled=True,
        ).astype(jnp.float32),
        lax.psum_scatter(
            value_parts,
            "blk",
            scatter_dimension=0,
            tiled=True,
        ).astype(jnp.float32),
    )
    query_tok_back, key_tok_back, value_tok_back = (
        lax.all_to_all(query_back, "head", split_axis=0, concat_axis=1, tiled=True),
        lax.all_to_all(round_low(key_home), "head", split_axis=0, concat_axis=1, tiled=True),
        lax.all_to_all(round_low(value_home), "head", split_axis=0, concat_axis=1, tiled=True),
    )
    query_grad = contract_first(normed_one, query_tok_back)
    key_grad = contract_first(normed_one, key_tok_back)
    value_grad = contract_first(normed_one, value_tok_back)
    normed_one_back = (
        contract_last(query_tok_back, query_weight)
        + contract_last(key_tok_back, key_weight)
        + contract_last(value_tok_back, value_weight)
    )
    unused, first_pull = jax.vjp(rms_scale, residual_in, gain_one)
    in_from_norm, first_gain_grad = first_pull(normed_one_back)
    tokens_grad = round_low(residual_back + in_from_norm)
    table_grad = lax.dynamic_update_slice_in_dim(
        jnp.zeros(bias_table.shape, jnp.float32), bucket_acc.T, head_start, 1
    )
    dense_sums = lax.psum(
        (
            first_gain_grad,
            query_grad,
            key_grad,
            value_grad,
            output_grad,
            table_grad,
            second_gain_grad,
            router_grad,
        ),
        ("head", "blk", "dp"),
    )
    return (
        round_low(layer_output)[None],
        tokens_grad[None],
        dense_sums[0],
        dense_sums[1],
        dense_sums[2],
        dense_sums[3],
        dense_sums[4],
        dense_sums[5],
        dense_sums[6],
        dense_sums[7],
        inner_part[None],
        outer_part[None],
    )


def solution(mesh):
    return jax.shard_map(
        body,
        mesh=mesh,
        in_specs=(
            P("dp", ("blk", "head"), None),
            P(),
            P(),
            P(),
            P(),
            P(),
            P(),
            P(),
            P(),
            P(("head", "blk"), None, "dp"),
            P(("head", "blk"), "dp", None),
            P("dp", ("blk", "head")),
            P("dp", ("blk", "head")),
            P(),
            P("dp", ("blk", "head"), None),
        ),
        out_specs=(
            P("dp", ("blk", "head"), None),
            P("dp", ("blk", "head"), None),
            P(),
            P(),
            P(),
            P(),
            P(),
            P(),
            P(),
            P(),
            P(("head", "blk"), None, "dp"),
            P(("head", "blk"), "dp", None),
        ),
        check_vma=False,
    )
```

```python
import functools
import math

import jax
import jax.numpy as jnp
from jax import lax
from jax.experimental import pallas as pl
from jax.experimental.pallas import tpu as pltpu
from jax.sharding import PartitionSpec as P

HEAD_DIM = 64
EPSILON = 1e-06
STRIP = 128
VMEM_BYTES = 28 * 2**20
LOW = jnp.bfloat16
WIDE = jnp.float32


def dot_nt(former, latter):
    return lax.dot_general(former, latter, (((1,), (1,)), ((), ())), preferred_element_type=WIDE)


def dot_nn(former, latter):
    return lax.dot_general(former, latter, (((1,), (0,)), ((), ())), preferred_element_type=WIDE)


def dot_tn(former, latter):
    return lax.dot_general(former, latter, (((0,), (0,)), ((), ())), preferred_element_type=WIDE)


def shaped(shape, kind):
    return pltpu.HBM(tuple(shape), kind)


def kept(shape, kind):
    return pltpu.VMEM(tuple(shape), kind)


class Near:
    def __init__(self, values):
        self.values, self.shape, self.dtype = values, values.shape, values.dtype


def near(values):
    return Near(values)


def fixed(shape):
    return pl.BlockSpec(tuple(shape), lambda *_: (0,) * len(shape), pipeline_mode=pl.Buffered(1))


def placed(values):
    if isinstance(values, Near):
        return pltpu.with_memory_space_constraint(values.values, pltpu.VMEM)
    return pltpu.with_memory_space_constraint(values, pltpu.HBM)


def run(
    kernel, outs, operands, name, flops, grid=None, in_specs=None, out_specs=None, scratch=(), after=()
):
    moved = sum(math.prod(x.shape) * jnp.dtype(x.dtype).itemsize for x in (*operands, *outs))
    count, skipped = len(operands), len(after)
    if grid is None:
        grid = (1,)
        out_specs = [fixed(x.shape) for x in outs]
    if in_specs is None:
        in_specs = [VMEM] * count
    in_specs = [fixed(x.shape) if spec is VMEM else spec for x, spec in zip(operands, in_specs)]

    def body(*refs):
        kernel(*refs[:count], *refs[count + skipped :])

    return pl.pallas_call(
        body,
        out_shape=list(outs),
        grid=grid,
        in_specs=in_specs + [pl.BlockSpec(memory_space=pltpu.HBM)] * skipped,
        out_specs=out_specs,
        scratch_shapes=list(scratch),
        compiler_params=pltpu.CompilerParams(vmem_limit_bytes=VMEM_BYTES),
        cost_estimate=pl.CostEstimate(flops=flops, bytes_accessed=moved, transcendentals=0),
        name=name,
    )(
        *(x if spec is SMEM else placed(x) for x, spec in zip(operands, in_specs)),
        *(placed(x) for x in after),
    )


def run_with_scalar(kernel, scalar, outs, operands, name, grid, in_specs, out_specs, scratch=()):
    return pl.pallas_call(
        kernel,
        out_shape=list(outs),
        grid_spec=pltpu.PrefetchScalarGridSpec(
            num_scalar_prefetch=1,
            grid=grid,
            in_specs=in_specs,
            out_specs=out_specs,
            scratch_shapes=list(scratch),
        ),
        compiler_params=pltpu.CompilerParams(vmem_limit_bytes=VMEM_BYTES),
        name=name,
    )(scalar, *(placed(x) for x in operands))


SMEM = pl.BlockSpec(memory_space=pltpu.SMEM)
VMEM = pl.BlockSpec(memory_space=pltpu.VMEM)


def swap(values, axis, bit):
    return lax.ppermute(values, axis, [(i, i ^ bit) for i in range(lax.axis_size(axis))])


def turn(values, axis, step):
    size = lax.axis_size(axis)
    return lax.ppermute(values, axis, [(i, (i + step) % size) for i in range(size)])


def blocks_over(values, axis):
    return lax.all_to_all(values, axis, split_axis=0, concat_axis=0, tiled=True)


def project_pairs_kernel(tokens_ref, gain_ref, key_ref, value_ref, pairs_ref, normed_ref):
    values = tokens_ref[...].astype(WIDE)
    scale = lax.rsqrt(jnp.mean(values * values, axis=-1, keepdims=True) + EPSILON)
    normed = (values * scale * gain_ref[...].astype(WIDE)).astype(LOW)
    normed_ref[...] = normed
    groups, _, width, _ = pairs_ref.shape
    for kind, weight_ref in enumerate((key_ref, value_ref)):
        rows = dot_nn(normed, weight_ref[...]).T
        for group in range(groups):
            pairs_ref[group, kind] = rows[group * width : (group + 1) * width].astype(LOW)


def project_queries_kernel(normed_ref, weight_ref, out_ref):
    rows = dot_nn(normed_ref[...], weight_ref[...]).T
    groups, width, _ = out_ref.shape
    for group in range(groups):
        out_ref[group] = rows[group * width : (group + 1) * width].astype(LOW)


def turn_kernel(normed_ref, out_ref):
    out_ref[...] = normed_ref[...].astype(WIDE).T.astype(LOW)


def strips_kernel(start_ref, table_ref, *refs):
    tiles = (len(refs) - 1) // 2
    bucket_refs, strips_refs, rows_ref = refs[:tiles], refs[tiles : 2 * tiles], refs[-1]
    buckets = table_ref.shape[1]
    for bucket_ref, strips_ref in zip(bucket_refs, strips_refs):
        heads, _, span = strips_ref.shape
        breadth = bucket_ref.shape[1]
        hot = lax.broadcasted_iota(jnp.int32, (buckets, breadth), 0) == bucket_ref[...]
        rows_ref[...] = dot_nn(table_ref[...], hot.astype(WIDE).astype(LOW))
        for head in range(heads):
            row = rows_ref[pl.ds(start_ref[0] + head, 1), :]
            spread = jnp.broadcast_to(row, (STRIP, breadth))
            turned = pltpu.roll(spread, breadth - (STRIP - 1), 1, stride=1, stride_axis=0)
            strips_ref[head] = turned[:, :span]


def make_strips(head_start, table_rows, buckets, heads, after):
    breadth = buckets[0].shape[1]
    return run(
        strips_kernel,
        [kept((heads, STRIP, breadth - STRIP), WIDE)] * len(buckets),
        (head_start, table_rows, *buckets),
        "bias_strips",
        flops=2 * 12 * 32 * breadth,
        in_specs=[SMEM] + [VMEM] * (1 + len(buckets)),
        scratch=[pltpu.VMEM((table_rows.shape[0], breadth), WIDE)],
        after=after,
    )


def head_mask(shape, head):
    lane = lax.broadcasted_iota(jnp.int32, shape, 1)
    return (lane >= head * HEAD_DIM) & (lane < (head + 1) * HEAD_DIM)


def side_by_side(pairs_ref, kind):
    return jnp.concatenate([pairs_ref[group, kind] for group in range(pairs_ref.shape[0])], 1)


def attend_kernel(*refs, heads, rows, tiles, first, last):
    query_ref = refs[0]
    pairs_refs, strips_refs, refs = refs[1 : 1 + tiles], refs[1 + tiles : 1 + 2 * tiles], refs[1 + 2 * tiles :]
    if not first:
        numer_in, total_in = refs[:2]
        refs = refs[2:]
    weight_refs, (total_ref, out_ref) = refs[:tiles], refs[tiles : tiles + 2]
    tile = query_ref.shape[2]
    groups = pairs_refs[0].shape[0]
    step = pl.program_id(0)
    queries = (query_ref[0] * jnp.asarray(0.125, LOW)).astype(WIDE).T.astype(LOW)
    out = jnp.zeros(queries.shape, WIDE)
    sums = jnp.zeros(queries.shape, WIDE)
    for head in range(heads):
        mask = head_mask(queries.shape, head)
        masked = jnp.where(mask, queries, jnp.zeros_like(queries))
        lanes = jnp.zeros((tile, 128), WIDE)
        numerator = jnp.zeros(queries.shape, WIDE)
        for pairs_ref, strips_ref, weight_ref in zip(pairs_refs, strips_refs, weight_refs):
            keys = jnp.concatenate([pairs_ref[group, 0] for group in range(groups)], 1)
            values = jnp.concatenate([pairs_ref[group, 1] for group in range(groups)], 1)
            scores = dot_nn(masked, keys)
            parts = []
            for sub in range(tile // STRIP):
                start = pl.multiple_of(rows - STRIP - (step * tile + sub * STRIP), STRIP)
                parts.append(
                    jnp.exp(
                        scores[sub * STRIP : (sub + 1) * STRIP, :]
                        + strips_ref[head, :, pl.ds(start, rows)]
                    )
                )
            weights = jnp.concatenate(parts, 0)
            for lane in range(rows // 128):
                lanes = lanes + weights[:, lane * 128 : (lane + 1) * 128]
            low = weights.astype(LOW)
            weight_ref[head] = low
            numerator = numerator + dot_nt(low, values)
        total = jnp.sum(lanes, axis=1, keepdims=True)
        out = jnp.where(mask, numerator, out)
        sums = jnp.where(mask, total, sums)
    out, sums = out.T, sums.T
    if not first:
        out = out + numer_in[0]
        sums = sums + total_in[0]
    total_ref[0] = sums
    if last:
        out = out / sums
        refs[-1][0] = out.astype(LOW)
    out_ref[0] = out


def gate(values, after):
    return pl.pallas_call(
        lambda *refs: None,
        out_shape=pltpu.HBM(values.shape, values.dtype),
        in_specs=[pl.BlockSpec(memory_space=pltpu.HBM)] * (1 + len(after)),
        out_specs=pl.BlockSpec(memory_space=pltpu.HBM),
        input_output_aliases={0: 0},
        name="gate",
    )(*(placed(x) for x in (values, *after)))


def attend(queries, pairs, strips, before, last):
    groups, width, tile = queries.shape
    rows = groups * tile
    heads = width // HEAD_DIM
    tiles = len(pairs)
    block = pl.BlockSpec((1, width, tile), lambda i: (i, 0, 0))
    weight_block = pl.BlockSpec((heads, tile, rows), lambda i: (0, i, 0))
    operands = (queries, *pairs, *(near(x) for x in strips), *before)
    return run(
        functools.partial(attend_kernel, heads=heads, rows=rows, tiles=tiles, first=not before, last=last),
        [shaped((heads, rows, rows), LOW)] * tiles
        + [shaped(queries.shape, WIDE)] * 2
        + [shaped(queries.shape, LOW)] * last,
        operands,
        "attend",
        flops=16 * width * rows * rows * tiles,
        grid=(groups,),
        in_specs=[block]
        + [fixed(x.shape) for x in pairs]
        + [fixed(x.shape) for x in strips]
        + [block] * len(before),
        out_specs=[weight_block] * tiles + [block] * (2 + last),
    )


def attend_back_kernel(*refs, heads, rows, first, last):
    query_ref, grad_ref, att_ref, total_ref, weight_ref, pairs_ref = refs[:6]
    refs = refs[6:]
    if not first:
        query_in = refs[0]
        refs = refs[1:]
    query_back_ref, pairs_back_ref, diagonal_ref, strips_ref, key_acc, value_acc = refs
    tile = query_ref.shape[2]
    groups, _, width, chunk = pairs_back_ref.shape
    span = strips_ref.shape[2]
    step = pl.program_id(0)

    @pl.when(step == 0)
    def _():
        strips_ref[...] = jnp.zeros_like(strips_ref)
        key_acc[...] = jnp.zeros_like(key_acc)
        value_acc[...] = jnp.zeros_like(value_acc)

    query_turned = query_ref[0] * jnp.asarray(0.125, LOW)
    grads = grad_ref[0].astype(WIDE)
    inverse = 1.0 / total_ref[0]
    numer_wide = grads * inverse
    numer_turned = numer_wide.astype(LOW)
    products = -(numer_wide * att_ref[0]).T
    numer_back = numer_turned.astype(WIDE).T.astype(LOW)
    out = jnp.zeros(numer_back.shape, WIDE)
    keys = side_by_side(pairs_ref, 0)
    values = side_by_side(pairs_ref, 1)
    for head in range(heads):
        mask = head_mask(numer_back.shape, head)
        masked = jnp.where(mask, numer_back, jnp.zeros_like(numer_back))
        denom_back = jnp.sum(jnp.where(mask, products, 0.0), axis=1, keepdims=True)
        here = slice(head * HEAD_DIM, (head + 1) * HEAD_DIM)
        query_here = query_turned[here]
        numer_here = numer_turned[here]
        weight_back = dot_nn(masked, values)
        weights = weight_ref[head]
        score_back = weights.astype(WIDE) * (weight_back + denom_back)
        low = score_back.astype(LOW)
        for sub in range(tile // STRIP):
            start = pl.multiple_of(rows - STRIP - (step * tile + sub * STRIP), STRIP)
            strips_ref[head, :, pl.ds(start, rows)] += score_back[sub * STRIP : (sub + 1) * STRIP, :]
        key_acc[here, :] += dot_nn(query_here, low)
        value_acc[here, :] += dot_nn(numer_here, weights)
        query_back = dot_nt(low, keys)
        out = jnp.where(mask, query_back * 0.125, out)
    out = out.T
    if not first:
        out = out + query_in[0]
    query_back_ref[0] = out.astype(query_back_ref.dtype)

    @pl.when(step == pl.num_programs(0) - 1)
    def _():
        for group in range(groups):
            at = group * chunk
            pairs_back_ref[group, 0] = key_acc[:, at : at + chunk].astype(pairs_back_ref.dtype)
            pairs_back_ref[group, 1] = value_acc[:, at : at + chunk].astype(pairs_back_ref.dtype)
        diagonal_ref[...] = jnp.zeros_like(diagonal_ref)
        for head in range(heads):
            folded = strips_ref[head]
            size = STRIP
            while size > 8:
                size //= 2
                folded = folded[:size] + pltpu.roll(folded[size:], span - size, 1)
            row = folded[0:1]
            for place in range(1, 8):
                row = row + pltpu.roll(folded[place : place + 1], span - place, 1)
            diagonal_ref[head : head + 1, :] = pltpu.roll(row, STRIP - 1, 1)

def attend_back(queries, grads, attended, total, weights, pairs, before, last, after):
    groups, width, tile = queries.shape
    rows = groups * tile
    heads = width // HEAD_DIM
    span = 2 * rows
    block = pl.BlockSpec((1, width, tile), lambda i: (i, 0, 0))
    operands = (queries, near(grads), attended, total, weights, pairs, *before)
    return run(
        functools.partial(attend_back_kernel, heads=heads, rows=rows, first=not before, last=last),
        [
            shaped(queries.shape, LOW if last else WIDE),
            shaped(pairs.shape, WIDE if last else LOW),
            shaped((8, span), WIDE),
        ],
        operands,
        "attend_back",
        flops=32 * width * rows * rows,
        grid=(groups,),
        in_specs=[block, block, block, block]
        + [pl.BlockSpec((heads, tile, rows), lambda i: (0, i, 0)), fixed(pairs.shape)]
        + [block] * len(before),
        out_specs=[block, fixed(pairs.shape), fixed((8, span))],
        scratch=[pltpu.VMEM((heads, STRIP, span), WIDE), pltpu.VMEM((width, rows), WIDE), pltpu.VMEM((width, rows), WIDE)], after=after)


def hot_rows(place_row, slots):
    tokens = place_row.shape[1]
    hot = lax.broadcasted_iota(jnp.int32, (slots, tokens), 0) == place_row
    return hot.astype(WIDE).astype(LOW)


def hot_columns(place_column, slots):
    tokens = place_column.shape[0]
    hot = lax.broadcasted_iota(jnp.int32, (tokens, slots), 1) == place_column
    return hot.astype(WIDE).astype(LOW)


def scatter_kernel(place_ref, rows_ref, slots_ref):
    hot = hot_rows(place_ref[...], slots_ref.shape[0])
    slots_ref[...] = dot_nn(hot, rows_ref[...]).astype(LOW)


def middle_kernel(
    att_ref, tokens_ref, weight_ref, gain_ref, place_ref, residual_ref, normed_ref, slots_ref
):
    residual = tokens_ref[...].astype(WIDE) + dot_tn(att_ref[...], weight_ref[...])
    residual_ref[...] = residual
    scale = lax.rsqrt(jnp.mean(residual * residual, axis=-1, keepdims=True) + EPSILON)
    normed = (residual * scale * gain_ref[...].astype(WIDE)).astype(LOW)
    normed_ref[...] = normed
    hot = hot_rows(place_ref[...], slots_ref.shape[0])
    slots_ref[...] = dot_nn(hot, normed).astype(LOW)


def route(normed, router, experts):
    logits = dot_nn(normed, router)
    lane = lax.broadcasted_iota(jnp.int32, logits.shape, 1)
    logits = jnp.where(lane < experts, logits, -jnp.inf)
    powers = jnp.exp(logits - jnp.max(logits, axis=-1, keepdims=True))
    return powers / jnp.sum(powers, axis=-1, keepdims=True), lane


def raw_back_kernel(up_ref, outer_ref, raw_ref):
    raw_ref[...] = dot_nt(up_ref[...], outer_ref[0])


def expert_kernel(
    own_ref,
    rows_ref,
    up_ref,
    router_ref,
    raw_ref,
    inner_ref,
    act_ref,
    pre_ref,
    home_ref,
    out_back_ref,
    logit_ref,
    back_acc,
    gate_acc,
    gate_ref,
    *,
    experts,
):
    step = pl.program_id(0)
    rows = rows_ref[...]

    @pl.when(step == 0)
    def _():
        probs, lane = route(rows, router_ref[...], experts)
        hot = (lane == own_ref[0]).astype(WIDE)
        gate = jnp.sum(probs * hot, axis=-1, keepdims=True)
        gate_ref[...] = jnp.broadcast_to(gate, gate_ref.shape)
        out_back_ref[...] = (gate * up_ref[...].astype(WIDE)).astype(LOW)
        back_acc[...] = jnp.zeros_like(back_acc)
        gate_acc[...] = jnp.zeros_like(gate_acc)

    gate = gate_ref[:, 0:1]
    lanes = gate_acc[...]
    back = back_acc[...]
    root = 0.7978845608028654
    size = 256 if inner_ref.shape[2] % 256 == 0 else 128
    count = inner_ref.shape[2] // size
    following = dot_nn(rows, inner_ref[0, :, 0:size])
    for piece in range(count):
        here = slice(piece * size, (piece + 1) * size)
        value = following
        if piece + 1 < count:
            following = dot_nn(rows, inner_ref[0, :, (piece + 1) * size : (piece + 2) * size])
        squared = value * value
        tilted = jnp.tanh(value * (root + (root * 0.044715) * squared))
        half = 0.5 * value
        act = (half + half * tilted).astype(LOW)
        slope = 0.5 + 0.5 * tilted + half * (1.0 - tilted * tilted) * (
            root + (3.0 * root * 0.044715) * squared
        )
        raw = raw_ref[:, here]
        pre = (gate * raw * slope).astype(LOW)
        act_ref[:, here] = act
        pre_ref[:, here] = pre
        back = back + dot_nt(pre, inner_ref[0, :, here])
        shares = act.astype(WIDE) * raw
        for lane in range(size // 128):
            lanes = lanes + shares[:, lane * 128 : (lane + 1) * 128]
    gate_acc[...] = lanes
    back_acc[...] = back

    @pl.when(step == pl.num_programs(0) - 1)
    def _():
        probs, lane = route(rows, router_ref[...], experts)
        hot = (lane == own_ref[0]).astype(WIDE)
        gate = jnp.sum(probs * hot, axis=-1, keepdims=True)
        gate_back = jnp.sum(gate_acc[...], axis=-1, keepdims=True)
        logit_back = (probs * gate_back * (hot - gate)).astype(LOW)
        logit_ref[...] = logit_back
        home_ref[...] = (dot_nt(logit_back, router_ref[...]) + back_acc[...]).astype(LOW)


def inner_grads_kernel(rows_ref, pre_ref, logit_ref, inner_ref, router_ref):
    inner_ref[0] = dot_tn(rows_ref[...], pre_ref[...]).astype(LOW)

    @pl.when(pl.program_id(0) == 0)
    def _():
        router_ref[...] = dot_tn(logit_ref[...], rows_ref[...])[: router_ref.shape[0]]


def outer_grads_kernel(act_ref, out_back_ref, weight_ref, outer_ref, out_ref, total_ref):
    step = pl.program_id(0)

    @pl.when(step == 0)
    def _():
        total_ref[...] = jnp.zeros_like(total_ref)

    outer_ref[0] = dot_tn(act_ref[...], out_back_ref[...]).astype(LOW)
    total_ref[...] += dot_nn(act_ref[...], weight_ref[0])

    @pl.when(step == pl.num_programs(0) - 1)
    def _():
        out_ref[...] = total_ref[...].astype(LOW)


def widen_kernel(values_ref, out_ref):
    out_ref[...] = values_ref[...].astype(WIDE)


def widen(values):
    rows, columns = values.shape
    tile = 256 if rows % 256 == 0 else rows
    block = pl.BlockSpec((tile, columns), lambda i: (i, 0))
    return run(
        widen_kernel,
        [shaped((rows, columns), WIDE)],
        (values,),
        "widen",
        flops=0,
        grid=(rows // tile,),
        in_specs=[block],
        out_specs=[block],
    )[0]


def after_kernel(
    home_ref,
    place_ref,
    residual_ref,
    gain_ref,
    upstream_ref,
    weight_ref,
    att_back_ref,
    residual_back_ref,
    branch_ref,
    gain_back_ref,
):
    hot = hot_columns(place_ref[...], home_ref.shape[0])
    normed_back = dot_nn(hot, home_ref[...])
    residual = residual_ref[...]
    scale = lax.rsqrt(jnp.mean(residual * residual, axis=-1, keepdims=True) + EPSILON)
    spread = residual * scale
    gained = gain_ref[...].astype(WIDE) * normed_back
    inner = jnp.mean(gained * spread, axis=-1, keepdims=True)
    back = upstream_ref[...].astype(WIDE) + scale * (gained - spread * inner)
    residual_back_ref[...] = back
    branch = back.astype(LOW)
    branch_ref[...] = branch
    gain_back_ref[...] = jnp.broadcast_to(
        jnp.sum(normed_back * spread, axis=0, keepdims=True), gain_back_ref.shape
    )
    att_back_ref[...] = dot_nt(weight_ref[...], branch).astype(LOW)


def output_pieces_kernel(core_ref, att_ref, branch_ref, router_ref, gain_ref, *refs):
    *out_refs, full_ref = refs
    at = att_ref.shape[0]
    experts = router_ref.shape[0]
    full_ref[:at, :] = dot_nn(att_ref[...], branch_ref[...])
    rest = [router_ref[...], gain_ref[...]]
    spare = full_ref.shape[0] - at - experts - 8
    if spare > 0:
        rest.append(jnp.zeros((spare, full_ref.shape[1]), WIDE))
    full_ref[at:, :] = jnp.concatenate(rest, 0)
    for place, out_ref in enumerate(out_refs):
        height = out_ref.shape[0]
        start = pl.multiple_of(jnp.bitwise_xor(core_ref[0], place) * height, height)
        out_ref[...] = full_ref[pl.ds(start, height), :].astype(out_ref.dtype)


def is_cube():
    return [lax.axis_size(name) for name in ("head", "blk", "dp")] == [4, 2, 4]


def sums_kernel(me_ref, *refs, count):
    operands, outs = refs[: len(refs) - count], refs[len(refs) - count :]
    for place, out_ref in enumerate(outs):
        height = out_ref.shape[0]
        start = pl.multiple_of(jnp.bitwise_xor(me_ref[0], place) * height, height)
        total = operands[0][pl.ds(start, height), :].astype(WIDE)
        for operand in operands[1:]:
            total += operand[pl.ds(start, height), :].astype(WIDE)
        out_ref[...] = total.astype(out_ref.dtype)


def sums(me, operands, count, name, after=()):
    height, breadth = operands[0].shape
    return run(
        functools.partial(sums_kernel, count=count),
        [shaped((height // count, breadth), LOW)] * count,
        (me[None].astype(jnp.int32), *operands),
        name,
        flops=0,
        in_specs=[SMEM] + [VMEM] * len(operands),
        after=after,
    )


def output_pieces(att_tok, branch_back, router_back, gain_back):
    model_width, experts = branch_back.shape[1], router_back.shape[0]
    cube = is_cube()
    height = -(-(model_width + experts + 8) // 1024) * 1024
    dp, blk = lax.axis_index("dp"), lax.axis_index("blk")
    count = 2 if cube else 1
    outs = run(
        output_pieces_kernel,
        [shaped((height // count, model_width), LOW if cube else WIDE)] * count,
        (
            ((dp & 1) * (count - 1)).astype(jnp.int32)[None],
            att_tok,
            branch_back,
            router_back,
            gain_back,
        ),
        "output_pieces",
        flops=2 * att_tok.size * model_width,
        in_specs=[SMEM] + [VMEM] * 4,
        scratch=[pltpu.VMEM((height, model_width), WIDE)],
    )
    if not cube:
        return (), (), lax.psum(outs[0], ("head", "blk", "dp"))
    mine, other = outs
    came = swap(other, "dp", 1)
    spot = blk * 2 + dp // 2
    own, along, across, corner = sums(spot, (mine, came), 4, "output_core")
    diagonal = [(b * 4 + d, (1 - b) * 4 + (d ^ 2)) for b in range(2) for d in range(4)]
    came = [swap(across, "blk", 1), swap(along, "dp", 2), lax.ppermute(corner, ("blk", "dp"), diagonal)]
    shares = sums(lax.axis_index("head"), (own, *came), 4, "output_sum")
    arrived = [shares[0]] + [swap(shares[step], "head", step) for step in range(1, 4)]
    return (own,), tuple(came), arrived


def output_kernel(
    residual_ref, normed_ref, router_ref, chosen_ref, place_ref, slots_ref, out_ref, *, experts
):
    probs, lane = route(normed_ref[...], router_ref[...], experts)
    hot = (lane == chosen_ref[...]).astype(WIDE)
    gate = jnp.sum(probs * hot, axis=-1, keepdims=True)
    expert_out = dot_nn(hot_columns(place_ref[...], slots_ref.shape[0]), slots_ref[...])
    out_ref[...] = (residual_ref[...] + gate * expert_out).astype(LOW)


def tokens_grad_kernel(
    triples_ref,
    query_weight_ref,
    key_weight_ref,
    value_weight_ref,
    tokens_ref,
    gain_ref,
    residual_back_ref,
    out_ref,
):
    groups = triples_ref.shape[0]
    weight_refs = (query_weight_ref, key_weight_ref, value_weight_ref)
    normed_back = jnp.zeros(out_ref.shape[::-1], WIDE)
    for kind, weight_ref in enumerate(weight_refs):
        rows = jnp.concatenate([triples_ref[group, kind] for group in range(groups)], 0)
        normed_back += dot_nn(weight_ref[...], rows)
    normed_back = normed_back.T
    values = tokens_ref[...].astype(WIDE)
    scale = lax.rsqrt(jnp.mean(values * values, axis=-1, keepdims=True) + EPSILON)
    spread = values * scale
    gained = gain_ref[...].astype(WIDE) * normed_back
    inner = jnp.mean(gained * spread, axis=-1, keepdims=True)
    out_ref[...] = (residual_back_ref[...] + scale * (gained - spread * inner)).astype(LOW)


def bucket_sums(diagonal, bucket_row, buckets):
    breadth = bucket_row.shape[1]
    hot = lax.broadcasted_iota(jnp.int32, (buckets, breadth), 0) == bucket_row
    hot = hot.astype(WIDE).astype(LOW)
    high = diagonal.astype(LOW)
    rest = diagonal - high.astype(WIDE)
    middle = rest.astype(LOW)
    small = (rest - middle.astype(WIDE)).astype(LOW)
    return dot_nt(high, hot) + dot_nt(middle, hot) + dot_nt(small, hot)


def side(grads):
    return -(-3 * grads // 128) * 128


def projection_grads(turned_ref, query_ref, pairs_ref):
    groups, width, tokens = query_ref.shape
    spare = jnp.zeros((side(width) - 3 * width, tokens), LOW)
    total = None
    for group in range(groups):
        rows = [query_ref[group], pairs_ref[group, 0], pairs_ref[group, 1], spare]
        part = dot_nt(turned_ref[group], jnp.concatenate(rows, 0))
        total = part if total is None else total + part
    return total


def table_sums(diagonal_refs, bucket_refs, buckets):
    table = bucket_sums(diagonal_refs[0][...], bucket_refs[0][...], buckets)
    for diagonal_ref, bucket_ref in zip(diagonal_refs[1:], bucket_refs[1:]):
        table += bucket_sums(diagonal_ref[...], bucket_ref[...], buckets)
    return table


def add_pairs(home_refs):
    total = home_refs[0][...].astype(WIDE)
    for home_ref in home_refs[1:]:
        total += home_ref[...].astype(WIDE)
    return total.astype(LOW)


def triples_kernel(query_ref, *refs):
    pairs = add_pairs(refs[:-1])
    for group in range(query_ref.shape[0]):
        refs[-1][group, 0] = query_ref[group]
        refs[-1][group, 1] = pairs[group, 0]
        refs[-1][group, 2] = pairs[group, 1]


def pieces_kernel(turned_ref, query_ref, *refs, tiles, buckets):
    home_refs, refs = refs[:tiles], refs[tiles:]
    diagonal_refs, bucket_refs = refs[:tiles], refs[tiles : 2 * tiles]
    out_ref, pairs_ref = refs[2 * tiles :]
    width = query_ref.shape[1]
    pairs_ref[...] = add_pairs(home_refs)
    full = projection_grads(turned_ref, query_ref, pairs_ref)
    owners, part, _ = out_ref.shape
    for owner in range(owners):
        place = owner if owners < 8 else (owner % 4) * 2 + owner // 4
        out_ref[place] = full[owner * part : (owner + 1) * part].astype(out_ref.dtype)
    table = table_sums(diagonal_refs, bucket_refs, buckets)
    table = jnp.concatenate([table, jnp.zeros_like(table)], 0)
    out_ref[0, 0:16, 3 * width : 3 * width + buckets] = table.astype(out_ref.dtype)


def join_kernel(pieces_ref, *refs):
    packed_refs, out_ref = refs[:-1], refs[-1]
    copies, halves, part, _ = out_ref.shape
    columns = pieces_ref.shape[2]
    total = pieces_ref[0].astype(WIDE)
    for piece in range(1, pieces_ref.shape[0]):
        total += pieces_ref[piece].astype(WIDE)
    packed = packed_refs[0][...].astype(WIDE)
    for packed_ref in packed_refs[1:]:
        packed += packed_ref[...].astype(WIDE)
    height = packed.shape[0] // halves
    for half in range(halves):
        former = total[half * part : (half + 1) * part].astype(LOW)
        rows = packed[half * height : (half + 1) * height]
        blocks = [rows[:, at : at + 256] for at in range(0, rows.shape[1], 256)]
        latter = jnp.concatenate(blocks, 0).astype(LOW)
        for copy in range(copies):
            out_ref[copy, half, :, :columns] = former
            out_ref[copy, half, :, columns:] = latter


def assemble_kernel(spot_ref, *refs, groups, heads, buckets, experts):
    piece_refs, refs = refs[:10], refs[10:]
    weight_refs, out_refs = refs[:3], refs[-11:-8]
    output_ref, gain_out, second_out, table_out, router_out = refs[-8:-3]
    extra_ref, shares_ref, table_ref = refs[-3:]
    part = piece_refs[0].shape[2]
    width = heads * HEAD_DIM
    columns = side(width)
    step = pl.program_id(0)
    owner = jnp.bitwise_xor(spot_ref[0], step)
    owned = output_ref.shape[0] // 128
    for core in range(2):
        own, across, along, corner_one, corner_two = piece_refs[5 * core : 5 * core + 5]
        cases = ((own, own), (along, along), (across, across), (corner_one, corner_two))
        for case, pair in enumerate(cases):

            @pl.when(step == 4 * core + case)
            def _(pair=pair):
                for half in range(2):
                    for group in range(groups):
                        at = half if pair[half].shape[1] == 2 else 0
                        whole = pair[half][group, at]
                        piece = whole[:, :columns].astype(WIDE)
                        for kind in range(3):
                            out_refs[kind][
                                half * part : (half + 1) * part,
                                group * width : (group + 1) * width,
                            ] = piece[:, kind * width : (kind + 1) * width]
                        if half == 0:

                            @pl.when(owner == 0)
                            def _(piece=piece, group=group):
                                table_ref[group] = piece[:8, 3 * width : 3 * width + buckets]

                        packed = whole[:, columns:].astype(WIDE)
                        rows = jnp.concatenate(
                            [packed[at : at + 16] for at in range(0, part, 16)], 1
                        )
                        start = group * 32 + half * 16

                        @pl.when(owner < owned)
                        def _(rows=rows, start=start):
                            output_ref[pl.ds(owner * 128 + start, 16), :] = rows

                        @pl.when(owner >= owned)
                        def _(rows=rows, start=start):
                            extra_ref[pl.ds((owner - owned) * 128 + start, 16), :] = rows

    shares = jnp.zeros((2 * part, 1), WIDE)
    for kind in range(3):
        shares += jnp.sum(
            out_refs[kind][...] * weight_refs[kind][...].astype(WIDE), axis=1, keepdims=True
        )
    shares_ref[pl.ds(owner * 2 * part, 2 * part), :] = jnp.broadcast_to(shares, (2 * part, 128))

    @pl.when(step == pl.num_programs(0) - 1)
    def _():
        first = shares_ref[...].T[0:8] / refs[3][...].astype(WIDE)
        second = extra_ref[experts : experts + 8, :]
        for lane in range(gain_out.shape[0]):
            gain_out[lane : lane + 1, :] = first[0:1, lane * 128 : (lane + 1) * 128]
            second_out[lane : lane + 1, :] = second[0:1, lane * 128 : (lane + 1) * 128]
        router_out[...] = extra_ref[:experts, :]
        for group in range(groups):
            table_out[group * heads : (group + 1) * heads, :] = table_ref[group][:heads]


def weight_sums(
    turned, query_back, home, diagonals, bucket_rows, buckets, weights, gain, experts, packed, early, first
):
    groups, model_width, _ = turned.shape
    width = query_back.shape[1]
    heads = width // HEAD_DIM
    tiles = len(diagonals)
    cube = is_cube()
    columns = side(width)
    pieces = run(
        functools.partial(pieces_kernel, tiles=tiles, buckets=buckets),
        [shaped((8, model_width // 8, columns), LOW) if cube else shaped((1, model_width, columns), WIDE)],
        (turned, query_back, *home, *diagonals, *bucket_rows),
        "projection_pieces",
        flops=6 * turned.size * width,
        after=early,
        scratch=[pltpu.VMEM(home[0].shape, LOW)],
    )[0]
    if not cube:
        sums = lax.psum(pieces[0], ("blk", "dp"))
        table = lax.all_gather(
            sums[:heads, 3 * width : 3 * width + buckets], "head", axis=0, tiled=True
        )
        grads = sums[:, : 3 * width].reshape(model_width, 3, width)
        grads = lax.all_gather(grads, "head", axis=2, tiled=True)
        grads = [grads[:, i] for i in range(3)]
        shares = sum(jnp.sum(x * y.astype(WIDE), axis=1) for x, y in zip(grads, weights))
        rest = packed[model_width:]
        shares = shares / gain[0].astype(WIDE)
        return *grads, shares, table.T, packed[:model_width], rest[:experts].T, rest[experts]
    part = model_width // 16
    came = blocks_over(pieces, ("blk", "dp"))
    copies = run(
        join_kernel,
        [shaped((groups, 2, part, columns + 256), LOW)],
        (came, *packed),
        "join",
        flops=0,
        after=first,
    )[0]
    own = blocks_over(copies, "head")
    across, along = swap(own, "blk", 1), swap(own, "dp", 2)
    corners = swap(across[:, :1], "dp", 2), swap(along[:, 1:], "blk", 1)
    held = (own, across, along, *corners)
    held += tuple(swap(array, "dp", 1) for array in held)
    dp, blk = lax.axis_index("dp"), lax.axis_index("blk")
    me = ((dp & 1) * 4 + blk * 2 + dp // 2).astype(jnp.int32)[None]
    rows_block = pl.BlockSpec((2 * part, model_width), lambda i, me: (i ^ me[0], 0))
    extra = packed[0].shape[0] * 32 - model_width
    *grads, output, shares, second, table, router = run_with_scalar(
        functools.partial(
            assemble_kernel, groups=groups, heads=heads, buckets=buckets, experts=experts
        ),
        me,
        [shaped((model_width, model_width), WIDE)] * 4
        + [
            shaped((model_width // 128, 128), WIDE),
            shaped((model_width // 128, 128), WIDE),
            shaped((groups * heads, buckets), WIDE),
            shaped((experts, model_width), WIDE),
        ],
        (*held, *weights, gain),
        "assemble",
        grid=(8,),
        in_specs=[fixed(array.shape) for array in held] + [rows_block] * 3 + [fixed(gain.shape)],
        out_specs=[rows_block] * 3
        + [
            fixed((model_width, model_width)),
            fixed((model_width // 128, 128)),
            fixed((model_width // 128, 128)),
            fixed((groups * heads, buckets)),
            fixed((experts, model_width)),
        ],
        scratch=[
            pltpu.VMEM((extra, model_width), WIDE),
            pltpu.VMEM((model_width, 128), WIDE),
            pltpu.VMEM((groups, 8, buckets), WIDE),
        ],
    )
    return *grads, shares.reshape(-1), table.T, output, router.T, second.reshape(-1)


def body(
    tokens,
    first_gain,
    query_weight,
    key_weight,
    value_weight,
    output_weight,
    bias_table,
    second_gain,
    router_weight,
    inner_weight,
    outer_weight,
    expert_index,
    capacity_slot,
    bucket_of_offset,
    upstream,
):
    _, token_rows, model_width = tokens.shape
    groups = lax.axis_size("head")
    cycle = lax.axis_size("blk")
    shares = lax.axis_size("dp")
    width = model_width // groups
    heads = width // HEAD_DIM
    local_rows = groups * token_rows
    length = local_rows * cycle
    buckets = bias_table.shape[0]
    experts = router_weight.shape[1]
    capacity = max(2, 2 * token_rows // experts)
    slots = experts * capacity
    token_values, upstream_values = tokens[0], upstream[0]
    gain_one, gain_two = first_gain[None], second_gain[None]
    chosen = expert_index[0]
    place = chosen * capacity + capacity_slot[0]
    place_row, place_column, chosen_column = place[None], place[:, None], chosen[:, None]
    router = jnp.pad(router_weight, ((0, 0), (0, 128 - experts)))

    inner_full = lax.all_gather(inner_weight[0], "dp", axis=0)
    outer_full = lax.all_gather(outer_weight[0], "dp", axis=0)

    square = model_width * model_width
    pairs, normed_one = run(
        project_pairs_kernel,
        [
            shaped((groups, 2, width, token_rows), LOW),
            shaped((token_rows, model_width), LOW),
        ],
        (token_values, gain_one, key_weight, value_weight),
        "project_pairs",
        flops=4 * token_rows * square,
    )
    pairs = blocks_over(pairs, "head")
    head_start = (lax.axis_index("head") * heads).astype(jnp.int32)[None]
    table_rows = jnp.pad(bias_table.T, ((0, -(groups * heads) % 8), (0, 0)))
    bucket_line = jnp.pad(bucket_of_offset, (0, 1))[None]
    blk = lax.axis_index("blk")
    tile_buckets, tile_strips = [], []
    for step in range(cycle):
        number = lax.rem(blk + cycle - step, cycle)
        start = length + (number - blk - 1) * local_rows
        tile_buckets.append(lax.dynamic_slice_in_dim(bucket_line, start, 2 * local_rows, 1))
    tile_pairs = [pairs] + [turn(pairs, "blk", step) for step in range(1, cycle)]
    up_slots = run(
        scatter_kernel,
        [shaped((slots, model_width), LOW)],
        (place_row, upstream_values),
        "scatter_up",
        flops=2 * slots * token_rows * model_width,
        after=(normed_one,),
    )[0]
    turned = run(
        turn_kernel,
        [shaped((model_width, token_rows), LOW)],
        (normed_one,),
        "turn",
        flops=0,
    )[0]
    queries = run(
        project_queries_kernel,
        [shaped((groups, width, token_rows), LOW)],
        (normed_one, query_weight),
        "project_queries",
        flops=2 * token_rows * square,
        after=(pairs, up_slots, turned),
    )[0]
    queries = blocks_over(queries, "head")
    up_rows = blocks_over(up_slots, ("head", "blk"))
    for step in range(0, cycle, 2):
        tile_strips += make_strips(
            head_start, table_rows, tile_buckets[step : step + 2], heads, (queries,)
        )
    tile_weights, before = [], ()
    for step in range(0, cycle, 2):
        tiles = slice(step, step + 2)
        last = step + 2 >= cycle
        results = attend(queries, tile_pairs[tiles], tile_strips[tiles], before, last)
        tile_weights += results[: len(tile_pairs[tiles])]
        total, attended, *rest = results[len(tile_pairs[tiles]) :]
        before = (attended, total)
    attended_low = gate(rest[0], (up_rows,))
    att_tok = blocks_over(attended_low, "head").reshape(model_width, token_rows)
    hidden = inner_full.shape[2]
    full_hidden = shares * hidden
    product = 2 * slots * model_width * full_hidden
    hidden_block = pl.BlockSpec((slots, hidden), lambda i: (0, i))
    inner_block = pl.BlockSpec((1, model_width, hidden), lambda i: (i, 0, 0))
    outer_block = pl.BlockSpec((1, hidden, model_width), lambda i: (i, 0, 0))
    raw = run(
        raw_back_kernel,
        [shaped((slots, full_hidden), WIDE)],
        (near(up_rows), outer_full),
        "raw_back",
        flops=product,
        grid=(shares,),
        in_specs=[fixed(up_rows.shape), outer_block],
        out_specs=[hidden_block],
    )[0]
    residual_mid, normed_two, normed_slots = run(
        middle_kernel,
        [
            shaped((token_rows, model_width), WIDE),
            shaped((token_rows, model_width), LOW),
            shaped((slots, model_width), LOW),
        ],
        (near(att_tok), token_values, output_weight, gain_two, place_row),
        "middle",
        flops=2 * token_rows * square + 2 * slots * token_rows * model_width,
        after=(raw,),
    )
    expert_rows = blocks_over(normed_slots, ("head", "blk"))
    turned_all = lax.all_gather(gate(turned, (expert_rows[:16, :128],)), "head", axis=0)
    own_expert = (lax.axis_index("head") * cycle + blk).astype(jnp.int32)[None]
    hidden_act, pre_back, home_slots, out_back, logit_back = run(
        functools.partial(expert_kernel, experts=experts),
        [
            shaped((slots, full_hidden), LOW),
            shaped((slots, full_hidden), LOW),
            shaped((slots, model_width), LOW),
            shaped((slots, model_width), LOW),
            shaped((slots, 128), LOW),
        ],
        (own_expert, near(expert_rows), near(up_rows), router, raw, inner_full),
        "expert",
        flops=2 * product,
        grid=(shares,),
        in_specs=[
            SMEM,
            fixed(expert_rows.shape),
            fixed(up_rows.shape),
            fixed(router.shape),
            hidden_block,
            inner_block,
        ],
        out_specs=[
            hidden_block,
            hidden_block,
            fixed((slots, model_width)),
            fixed((slots, model_width)),
            fixed((slots, 128)),
        ],
        scratch=[
            pltpu.VMEM((slots, model_width), WIDE),
            pltpu.VMEM((slots, 128), WIDE),
            pltpu.VMEM((slots, 128), WIDE),
        ],
    )
    home_rows = blocks_over(home_slots, ("head", "blk"))
    inner_grads, router_back = run(
        inner_grads_kernel,
        [shaped((shares, model_width, hidden), LOW), shaped((experts, model_width), WIDE)],
        (near(expert_rows), pre_back, logit_back),
        "inner_grads",
        flops=product,
        grid=(shares,),
        in_specs=[fixed(expert_rows.shape), hidden_block, fixed(logit_back.shape)],
        out_specs=[inner_block, fixed((experts, model_width))],
    )
    outer_grads, expert_out = run(
        outer_grads_kernel,
        [
            shaped((shares, hidden, model_width), LOW),
            shaped((slots, model_width), LOW),
        ],
        (hidden_act, out_back, outer_full),
        "outer_grads",
        flops=2 * product,
        grid=(shares,),
        in_specs=[hidden_block, fixed(out_back.shape), outer_block],
        out_specs=[outer_block, fixed((slots, model_width))],
        scratch=[pltpu.VMEM((slots, model_width), WIDE)],
    )

    att_back, residual_back, branch_back, gain_back = run(
        after_kernel,
        [
            shaped((model_width, token_rows), LOW),
            shaped((token_rows, model_width), WIDE),
            shaped((token_rows, model_width), LOW),
            shaped((8, model_width), WIDE),
        ],
        (near(home_rows), place_column, residual_mid, gain_two, upstream_values, output_weight),
        "after",
        flops=2 * token_rows * square + 2 * slots * token_rows * model_width,
        after=(router_back, expert_out),
    )
    head_back = blocks_over(att_back.reshape(groups, width, token_rows), "head")
    packed_core, packed_sum, packed_shares = output_pieces(
        att_tok, branch_back, router_back, gain_back
    )
    inner_part, outer_part = (
        widen(lax.psum_scatter(gate(grads, (branch_back,)), "dp", scatter_dimension=0))
        for grads in (inner_grads, outer_grads)
    )
    out_rows = blocks_over(expert_out, ("head", "blk"))

    before, diagonals, home = (), [None] * cycle, []
    for step in list(range(1, cycle)) + [0]:
        query_back, pairs_part, diagonals[step] = attend_back(
            queries,
            head_back,
            attended,
            total,
            tile_weights[step],
            tile_pairs[step],
            before,
            step == 0,
            () if len(home) == 0 else packed_core,
        )
        before = (query_back,)
        home.append(pairs_part if step == 0 else turn(pairs_part, "blk", cycle - step))
    home = home[-1:] + home[:-1]
    layer_output = run(
        functools.partial(output_kernel, experts=experts),
        [shaped((token_rows, model_width), LOW)],
        (residual_mid, normed_two, router, chosen_column, place_column, near(out_rows)),
        "layer_output",
        flops=2 * slots * token_rows * model_width,
    )[0]
    triples = run(
        triples_kernel,
        [shaped((groups, 3, width, token_rows), LOW)],
        (query_back, *home),
        "triples",
        flops=0,
    )[0]
    (
        query_grad,
        key_grad,
        value_grad,
        first_gain_grad,
        table_grad,
        output_grad,
        router_grad,
        second_gain_grad,
    ) = weight_sums(
        turned_all,
        query_back,
        home,
        diagonals,
        tile_buckets,
        buckets,
        (query_weight, key_weight, value_weight),
        gain_one,
        experts,
        packed_shares,
        (out_rows, *packed_sum),
        (triples, layer_output),
    )
    triples_tok = blocks_over(triples, "head")
    tokens_grad = run(
        tokens_grad_kernel,
        [shaped((token_rows, model_width), LOW)],
        (
            near(triples_tok),
            query_weight,
            key_weight,
            value_weight,
            token_values,
            gain_one,
            residual_back,
        ),
        "tokens_grad",
        flops=6 * token_rows * square,
    )[0]
    return (
        layer_output[None],
        tokens_grad[None],
        first_gain_grad,
        query_grad,
        key_grad,
        value_grad,
        output_grad,
        table_grad,
        second_gain_grad,
        router_grad,
        inner_part[None],
        outer_part[None],
    )


def solution(mesh):
    return jax.shard_map(
        body,
        mesh=mesh,
        in_specs=(
            P("dp", ("blk", "head"), None),
            P(),
            P(),
            P(),
            P(),
            P(),
            P(),
            P(),
            P(),
            P(("head", "blk"), None, "dp"),
            P(("head", "blk"), "dp", None),
            P("dp", ("blk", "head")),
            P("dp", ("blk", "head")),
            P(),
            P("dp", ("blk", "head"), None),
        ),
        out_specs=(
            P("dp", ("blk", "head"), None),
            P("dp", ("blk", "head"), None),
            P(),
            P(),
            P(),
            P(),
            P(),
            P(),
            P(),
            P(),
            P(("head", "blk"), None, "dp"),
            P(("head", "blk"), "dp", None),
        ),
        check_vma=False,
    )
```

```python
import functools
import math

import jax
import jax.numpy as jnp
from jax import lax
from jax.experimental import pallas as pl
from jax.experimental.pallas import tpu as pltpu
from jax.sharding import PartitionSpec as P

HEAD_DIM = 64
EPSILON = 1e-06
STRIP = 128
VMEM_BYTES = 28 * 2**20
LOW = jnp.bfloat16
WIDE = jnp.float32


def dot_nt(former, latter):
    return lax.dot_general(former, latter, (((1,), (1,)), ((), ())), preferred_element_type=WIDE)


def dot_nn(former, latter):
    return lax.dot_general(former, latter, (((1,), (0,)), ((), ())), preferred_element_type=WIDE)


def dot_tn(former, latter):
    return lax.dot_general(former, latter, (((0,), (0,)), ((), ())), preferred_element_type=WIDE)


def shaped(shape, kind):
    return pltpu.HBM(tuple(shape), kind)


def kept(shape, kind):
    return pltpu.VMEM(tuple(shape), kind)


class Near:
    def __init__(self, values):
        self.values, self.shape, self.dtype = values, values.shape, values.dtype


def near(values):
    return Near(values)


def fixed(shape):
    return pl.BlockSpec(tuple(shape), lambda *_: (0,) * len(shape), pipeline_mode=pl.Buffered(1))


def placed(values):
    if isinstance(values, Near):
        return pltpu.with_memory_space_constraint(values.values, pltpu.VMEM)
    return pltpu.with_memory_space_constraint(values, pltpu.HBM)


def run(
    kernel, outs, operands, name, flops, grid=None, in_specs=None, out_specs=None, scratch=(), after=()
):
    moved = sum(math.prod(x.shape) * jnp.dtype(x.dtype).itemsize for x in (*operands, *outs))
    count, skipped = len(operands), len(after)
    if grid is None:
        grid = (1,)
        out_specs = [fixed(x.shape) for x in outs]
    if in_specs is None:
        in_specs = [VMEM] * count
    in_specs = [fixed(x.shape) if spec is VMEM else spec for x, spec in zip(operands, in_specs)]

    def body(*refs):
        kernel(*refs[:count], *refs[count + skipped :])

    return pl.pallas_call(
        body,
        out_shape=list(outs),
        grid=grid,
        in_specs=in_specs + [pl.BlockSpec(memory_space=pltpu.HBM)] * skipped,
        out_specs=out_specs,
        scratch_shapes=list(scratch),
        compiler_params=pltpu.CompilerParams(vmem_limit_bytes=VMEM_BYTES),
        cost_estimate=pl.CostEstimate(flops=flops, bytes_accessed=moved, transcendentals=0),
        name=name,
    )(
        *(x if spec is SMEM else placed(x) for x, spec in zip(operands, in_specs)),
        *(placed(x) for x in after),
    )


def run_with_scalar(
    kernel, scalar, outs, operands, name, grid, in_specs, out_specs, scratch=(), aliases=None
):
    return pl.pallas_call(
        kernel,
        out_shape=list(outs),
        grid_spec=pltpu.PrefetchScalarGridSpec(
            num_scalar_prefetch=1,
            grid=grid,
            in_specs=in_specs,
            out_specs=out_specs,
            scratch_shapes=list(scratch),
        ),
        compiler_params=pltpu.CompilerParams(vmem_limit_bytes=VMEM_BYTES),
        input_output_aliases=aliases or {},
        name=name,
    )(scalar, *(placed(x) for x in operands))


SMEM = pl.BlockSpec(memory_space=pltpu.SMEM)
VMEM = pl.BlockSpec(memory_space=pltpu.VMEM)


def swap(values, axis, bit):
    return lax.ppermute(values, axis, [(i, i ^ bit) for i in range(lax.axis_size(axis))])


def turn(values, axis, step):
    size = lax.axis_size(axis)
    return lax.ppermute(values, axis, [(i, (i + step) % size) for i in range(size)])


def blocks_over(values, axis):
    return lax.all_to_all(values, axis, split_axis=0, concat_axis=0, tiled=True)


def project_pairs_kernel(tokens_ref, gain_ref, key_ref, value_ref, pairs_ref, normed_ref):
    values = tokens_ref[...].astype(WIDE)
    scale = lax.rsqrt(jnp.mean(values * values, axis=-1, keepdims=True) + EPSILON)
    normed = (values * scale * gain_ref[...].astype(WIDE)).astype(LOW)
    normed_ref[...] = normed
    groups, _, width, _ = pairs_ref.shape
    for kind, weight_ref in enumerate((key_ref, value_ref)):
        rows = dot_nn(normed, weight_ref[...]).T
        for group in range(groups):
            pairs_ref[group, kind] = rows[group * width : (group + 1) * width].astype(LOW)


def project_queries_kernel(normed_ref, weight_ref, out_ref):
    rows = dot_nn(normed_ref[...], weight_ref[...]).T
    groups, width, _ = out_ref.shape
    for group in range(groups):
        out_ref[group] = rows[group * width : (group + 1) * width].astype(LOW)


def turn_kernel(normed_ref, out_ref):
    turned = normed_ref[...].astype(WIDE).T.astype(LOW)
    for copy in range(out_ref.shape[0]):
        out_ref[copy] = turned


def strips_kernel(start_ref, table_ref, *refs):
    tiles = (len(refs) - 1) // 2
    bucket_refs, strips_refs, rows_ref = refs[:tiles], refs[tiles : 2 * tiles], refs[-1]
    buckets = table_ref.shape[1]
    for bucket_ref, strips_ref in zip(bucket_refs, strips_refs):
        heads, _, span = strips_ref.shape
        breadth = bucket_ref.shape[1]
        hot = lax.broadcasted_iota(jnp.int32, (buckets, breadth), 0) == bucket_ref[...]
        rows_ref[...] = dot_nn(table_ref[...], hot.astype(WIDE).astype(LOW))
        for head in range(heads):
            row = rows_ref[pl.ds(start_ref[0] + head, 1), :]
            spread = jnp.broadcast_to(row, (STRIP, breadth))
            turned = pltpu.roll(spread, breadth - (STRIP - 1), 1, stride=1, stride_axis=0)
            strips_ref[head] = turned[:, :span]


def make_strips(head_start, table_rows, buckets, heads, after):
    breadth = buckets[0].shape[1]
    return run(
        strips_kernel,
        [kept((heads, STRIP, breadth - STRIP), WIDE)] * len(buckets),
        (head_start, table_rows, *buckets),
        "bias_strips",
        flops=2 * 12 * 32 * breadth,
        in_specs=[SMEM] + [VMEM] * (1 + len(buckets)),
        scratch=[pltpu.VMEM((table_rows.shape[0], breadth), WIDE)],
        after=after,
    )


def head_mask(shape, head):
    lane = lax.broadcasted_iota(jnp.int32, shape, 1)
    return (lane >= head * HEAD_DIM) & (lane < (head + 1) * HEAD_DIM)


def side_by_side(pairs_ref, kind):
    return jnp.concatenate([pairs_ref[group, kind] for group in range(pairs_ref.shape[0])], 1)


def attend_kernel(*refs, heads, rows, tiles, first, last):
    query_ref = refs[0]
    pairs_refs, strips_refs, refs = refs[1 : 1 + tiles], refs[1 + tiles : 1 + 2 * tiles], refs[1 + 2 * tiles :]
    if not first:
        numer_in, total_in = refs[:2]
        refs = refs[2:]
    weight_refs, (total_ref, out_ref) = refs[:tiles], refs[tiles : tiles + 2]
    tile = query_ref.shape[2]
    groups = pairs_refs[0].shape[0]
    step = pl.program_id(0)
    queries = (query_ref[0] * jnp.asarray(0.125, LOW)).astype(WIDE).T.astype(LOW)
    out = jnp.zeros(queries.shape, WIDE)
    sums = jnp.zeros(queries.shape, WIDE)
    for head in range(heads):
        mask = head_mask(queries.shape, head)
        masked = jnp.where(mask, queries, jnp.zeros_like(queries))
        lanes = jnp.zeros((tile, 128), WIDE)
        numerator = jnp.zeros(queries.shape, WIDE)
        for pairs_ref, strips_ref, weight_ref in zip(pairs_refs, strips_refs, weight_refs):
            keys = jnp.concatenate([pairs_ref[group, 0] for group in range(groups)], 1)
            values = jnp.concatenate([pairs_ref[group, 1] for group in range(groups)], 1)
            scores = dot_nn(masked, keys)
            parts = []
            for sub in range(tile // STRIP):
                start = pl.multiple_of(rows - STRIP - (step * tile + sub * STRIP), STRIP)
                parts.append(
                    jnp.exp(
                        scores[sub * STRIP : (sub + 1) * STRIP, :]
                        + strips_ref[head, :, pl.ds(start, rows)]
                    )
                )
            weights = jnp.concatenate(parts, 0)
            for lane in range(rows // 128):
                lanes = lanes + weights[:, lane * 128 : (lane + 1) * 128]
            low = weights.astype(LOW)
            weight_ref[head] = low
            numerator = numerator + dot_nt(low, values)
        total = jnp.sum(lanes, axis=1, keepdims=True)
        out = jnp.where(mask, numerator, out)
        sums = jnp.where(mask, total, sums)
    out, sums = out.T, sums.T
    if not first:
        out = out + numer_in[0]
        sums = sums + total_in[0]
    total_ref[0] = sums
    if last:
        out = out / sums
        refs[-1][0] = out.astype(LOW)
    out_ref[0] = out


def gate(values, after):
    return pl.pallas_call(
        lambda *refs: None,
        out_shape=pltpu.HBM(values.shape, values.dtype),
        in_specs=[pl.BlockSpec(memory_space=pltpu.HBM)] * (1 + len(after)),
        out_specs=pl.BlockSpec(memory_space=pltpu.HBM),
        input_output_aliases={0: 0},
        name="gate",
    )(*(placed(x) for x in (values, *after)))


def attend(queries, pairs, strips, before, last):
    groups, width, tile = queries.shape
    rows = groups * tile
    heads = width // HEAD_DIM
    tiles = len(pairs)
    block = pl.BlockSpec((1, width, tile), lambda i: (i, 0, 0))
    weight_block = pl.BlockSpec((heads, tile, rows), lambda i: (0, i, 0))
    operands = (queries, *pairs, *(near(x) for x in strips), *before)
    return run(
        functools.partial(attend_kernel, heads=heads, rows=rows, tiles=tiles, first=not before, last=last),
        [shaped((heads, rows, rows), LOW)] * tiles
        + [shaped(queries.shape, WIDE)] * 2
        + [shaped(queries.shape, LOW)] * last,
        operands,
        "attend",
        flops=16 * width * rows * rows * tiles,
        grid=(groups,),
        in_specs=[block]
        + [fixed(x.shape) for x in pairs]
        + [fixed(x.shape) for x in strips]
        + [block] * len(before),
        out_specs=[weight_block] * tiles + [block] * (2 + last),
    )


def attend_back_kernel(*refs, heads, rows, first, last, begin):
    query_ref, grad_ref, att_ref, total_ref, weight_ref, pairs_ref = refs[:6]
    refs = refs[6:]
    if not first:
        query_in = refs[0]
        refs = refs[1:]
    query_back_ref, pairs_back_ref, diagonal_ref, strips_ref, key_acc, value_acc = refs
    tile = query_ref.shape[2]
    groups, _, width, chunk = pairs_back_ref.shape
    span = strips_ref.shape[2]
    step = pl.program_id(0)
    block = step + begin

    @pl.when(step == 0)
    def _():
        strips_ref[...] = jnp.zeros_like(strips_ref)
        key_acc[...] = jnp.zeros_like(key_acc)
        value_acc[...] = jnp.zeros_like(value_acc)

    query_turned = query_ref[0] * jnp.asarray(0.125, LOW)
    grads = grad_ref[0].astype(WIDE)
    inverse = 1.0 / total_ref[0]
    numer_wide = grads * inverse
    numer_turned = numer_wide.astype(LOW)
    products = -(numer_wide * att_ref[0]).T
    numer_back = numer_turned.astype(WIDE).T.astype(LOW)
    out = jnp.zeros(numer_back.shape, WIDE)
    keys = side_by_side(pairs_ref, 0)
    values = side_by_side(pairs_ref, 1)
    for head in range(heads):
        mask = head_mask(numer_back.shape, head)
        masked = jnp.where(mask, numer_back, jnp.zeros_like(numer_back))
        denom_back = jnp.sum(jnp.where(mask, products, 0.0), axis=1, keepdims=True)
        here = slice(head * HEAD_DIM, (head + 1) * HEAD_DIM)
        query_here = query_turned[here]
        numer_here = numer_turned[here]
        weight_back = dot_nn(masked, values)
        weights = weight_ref[head]
        score_back = weights.astype(WIDE) * (weight_back + denom_back)
        low = score_back.astype(LOW)
        for sub in range(tile // STRIP):
            start = pl.multiple_of(rows - STRIP - (block * tile + sub * STRIP), STRIP)
            strips_ref[head, :, pl.ds(start, rows)] += score_back[sub * STRIP : (sub + 1) * STRIP, :]
        key_acc[here, :] += dot_nn(query_here, low)
        value_acc[here, :] += dot_nn(numer_here, weights)
        query_back = dot_nt(low, keys)
        out = jnp.where(mask, query_back * 0.125, out)
    out = out.T
    if not first:
        out = out + query_in[0]
    query_back_ref[0] = out.astype(query_back_ref.dtype)

    @pl.when(step == pl.num_programs(0) - 1)
    def _():
        for group in range(groups):
            at = group * chunk
            pairs_back_ref[group, 0] = key_acc[:, at : at + chunk].astype(pairs_back_ref.dtype)
            pairs_back_ref[group, 1] = value_acc[:, at : at + chunk].astype(pairs_back_ref.dtype)
        diagonal_ref[...] = jnp.zeros_like(diagonal_ref)
        for head in range(heads):
            folded = strips_ref[head]
            size = STRIP
            while size > 8:
                size //= 2
                folded = folded[:size] + pltpu.roll(folded[size:], span - size, 1)
            row = folded[0:1]
            for place in range(1, 8):
                row = row + pltpu.roll(folded[place : place + 1], span - place, 1)
            diagonal_ref[head : head + 1, :] = pltpu.roll(row, STRIP - 1, 1)

def attend_back(
    queries, grads, attended, total, weights, pairs, before, last, begin, count, after
):
    groups, width, tile = queries.shape
    rows = groups * tile
    heads = width // HEAD_DIM
    span = 2 * rows
    block = pl.BlockSpec((1, width, tile), lambda i: (i + begin, 0, 0))
    out_block = pl.BlockSpec((1, width, tile), lambda i: (i, 0, 0))
    operands = (queries, grads, attended, total, weights, pairs, *before)
    return run(
        functools.partial(attend_back_kernel, heads=heads, rows=rows, first=not before, last=last, begin=begin),
        [
            shaped((count, width, tile), LOW if last else WIDE),
            shaped(pairs.shape, WIDE if last else LOW),
            shaped((8, span), WIDE),
        ],
        operands,
        "attend_back",
        flops=8 * width * rows * rows * count,
        grid=(count,),
        in_specs=[block, block, block, block]
        + [pl.BlockSpec((heads, tile, rows), lambda i: (0, i + begin, 0)), fixed(pairs.shape)]
        + [block] * len(before),
        out_specs=[out_block, fixed(pairs.shape), fixed((8, span))],
        scratch=[pltpu.VMEM((heads, STRIP, span), WIDE), pltpu.VMEM((width, rows), WIDE), pltpu.VMEM((width, rows), WIDE)], after=after)


def hot_rows(place_row, slots):
    tokens = place_row.shape[1]
    hot = lax.broadcasted_iota(jnp.int32, (slots, tokens), 0) == place_row
    return hot.astype(WIDE).astype(LOW)


def hot_columns(place_column, slots):
    tokens = place_column.shape[0]
    hot = lax.broadcasted_iota(jnp.int32, (tokens, slots), 1) == place_column
    return hot.astype(WIDE).astype(LOW)


def scatter_kernel(place_ref, rows_ref, slots_ref):
    hot = hot_rows(place_ref[...], slots_ref.shape[0])
    slots_ref[...] = dot_nn(hot, rows_ref[...]).astype(LOW)


def middle_kernel(
    att_ref, tokens_ref, weight_ref, gain_ref, place_ref, residual_ref, normed_ref, slots_ref
):
    residual = tokens_ref[...].astype(WIDE) + dot_tn(att_ref[...], weight_ref[...])
    residual_ref[...] = residual
    scale = lax.rsqrt(jnp.mean(residual * residual, axis=-1, keepdims=True) + EPSILON)
    normed = (residual * scale * gain_ref[...].astype(WIDE)).astype(LOW)
    normed_ref[...] = normed
    hot = hot_rows(place_ref[...], slots_ref.shape[0])
    slots_ref[...] = dot_nn(hot, normed).astype(LOW)


def route(normed, router, experts):
    logits = dot_nn(normed, router)
    lane = lax.broadcasted_iota(jnp.int32, logits.shape, 1)
    logits = jnp.where(lane < experts, logits, -jnp.inf)
    powers = jnp.exp(logits - jnp.max(logits, axis=-1, keepdims=True))
    return powers / jnp.sum(powers, axis=-1, keepdims=True), lane


def shard_copy(weight_refs, buffer_ref, semaphores, at):
    return pltpu.make_async_copy(weight_refs[at], buffer_ref.at[at % 2], semaphores.at[at % 2])


def take_shard(weight_refs, buffer_ref, semaphores):
    step = pl.program_id(0)

    @pl.when(step == 0)
    def _():
        for at in range(min(2, len(weight_refs))):
            shard_copy(weight_refs, buffer_ref, semaphores, at).start()

    for at in range(len(weight_refs)):

        @pl.when(step == at)
        def _(at=at):
            shard_copy(weight_refs, buffer_ref, semaphores, at).wait()

    return lax.rem(step, 2)


def next_shard(weight_refs, buffer_ref, semaphores):
    for at in range(len(weight_refs) - 2):

        @pl.when(pl.program_id(0) == at)
        def _(at=at):
            shard_copy(weight_refs, buffer_ref, semaphores, at + 2).start()


def shard_scratch(weights):
    return [pltpu.VMEM((2, *weights[0].shape), LOW), pltpu.SemaphoreType.DMA((2,))]


def shard_places(weights):
    return [pl.BlockSpec(memory_space=pltpu.HBM)] * len(weights)


def raw_back_kernel(up_ref, *refs):
    *weight_refs, raw_ref, buffer_ref, semaphores = refs
    slot = take_shard(weight_refs, buffer_ref, semaphores)
    raw_ref[...] = dot_nt(up_ref[...], buffer_ref[slot]).astype(LOW)
    next_shard(weight_refs, buffer_ref, semaphores)


def expert_kernel(own_ref, rows_ref, up_ref, router_ref, raw_ref, *refs, experts):
    *weight_refs, act_ref, pre_ref, home_ref, out_back_ref, logit_ref = refs[:-5]
    back_acc, gate_acc, gate_ref, buffer_ref, semaphores = refs[-5:]
    slot = take_shard(weight_refs, buffer_ref, semaphores)
    step = pl.program_id(0)
    rows = rows_ref[...]

    @pl.when(step == 0)
    def _():
        probs, lane = route(rows, router_ref[...], experts)
        hot = (lane == own_ref[0]).astype(WIDE)
        gate = jnp.sum(probs * hot, axis=-1, keepdims=True)
        gate_ref[...] = jnp.broadcast_to(gate, gate_ref.shape)
        out_back_ref[...] = (gate * up_ref[...].astype(WIDE)).astype(LOW)
        back_acc[...] = jnp.zeros_like(back_acc)
        gate_acc[...] = jnp.zeros_like(gate_acc)

    gate = gate_ref[:, 0:1]
    lanes = gate_acc[...]
    back = back_acc[...]
    root = 0.7978845608028654
    hidden = buffer_ref.shape[2]
    size = 256 if hidden % 256 == 0 else 128
    count = hidden // size
    following = dot_nn(rows, buffer_ref[slot, :, 0:size])
    for piece in range(count):
        here = slice(piece * size, (piece + 1) * size)
        value = following
        if piece + 1 < count:
            following = dot_nn(rows, buffer_ref[slot, :, (piece + 1) * size : (piece + 2) * size])
        squared = value * value
        tilted = jnp.tanh(value * (root + (root * 0.044715) * squared))
        half = 0.5 * value
        act = (half + half * tilted).astype(LOW)
        slope = 0.5 + 0.5 * tilted + half * (1.0 - tilted * tilted) * (
            root + (3.0 * root * 0.044715) * squared
        )
        raw = raw_ref[:, here].astype(WIDE)
        pre = (gate * raw * slope).astype(LOW)
        act_ref[:, here] = act
        pre_ref[:, here] = pre
        back = back + dot_nt(pre, buffer_ref[slot, :, here])
        shares = act.astype(WIDE) * raw
        for lane in range(size // 128):
            lanes = lanes + shares[:, lane * 128 : (lane + 1) * 128]
    gate_acc[...] = lanes
    back_acc[...] = back
    next_shard(weight_refs, buffer_ref, semaphores)

    @pl.when(step == pl.num_programs(0) - 1)
    def _():
        probs, lane = route(rows, router_ref[...], experts)
        hot = (lane == own_ref[0]).astype(WIDE)
        gate = jnp.sum(probs * hot, axis=-1, keepdims=True)
        gate_back = jnp.sum(gate_acc[...], axis=-1, keepdims=True)
        logit_back = (probs * gate_back * (hot - gate)).astype(LOW)
        logit_ref[...] = logit_back
        home_ref[...] = (dot_nt(logit_back, router_ref[...]) + back_acc[...]).astype(LOW)


def store_half(former_ref, latter_ref, keep_ref, send_ref):
    count = pl.num_programs(0) // 2

    @pl.when(pl.program_id(0) < count)
    def _():
        send_ref[0] = dot_tn(former_ref[...], latter_ref[...]).astype(LOW)

    @pl.when(pl.program_id(0) >= count)
    def _():
        keep_ref[0] = dot_tn(former_ref[...], latter_ref[...]).astype(LOW)


def shard_at(i, shares):
    count = shares // 2
    return jnp.where(i < count, 2 * i + 1, 2 * (i - count))


def keep_spec(shape, shares):
    return pl.BlockSpec((1, *shape), lambda i: (jnp.maximum(i - shares // 2, 0), 0, 0))


def send_spec(shape, shares):
    return pl.BlockSpec((1, *shape), lambda i: (jnp.minimum(i, shares // 2 - 1), 0, 0))


def inner_grads_kernel(rows_ref, pre_ref, logit_ref, keep_ref, send_ref, router_ref):
    store_half(rows_ref, pre_ref, keep_ref, send_ref)

    @pl.when(pl.program_id(0) == 0)
    def _():
        router_ref[...] = dot_tn(logit_ref[...], rows_ref[...])[: router_ref.shape[0]]


def outer_grads_kernel(act_ref, out_back_ref, *refs):
    *weight_refs, keep_ref, send_ref, out_ref, total_ref, buffer_ref, semaphores = refs
    step = pl.program_id(0)
    slot = take_shard(weight_refs, buffer_ref, semaphores)

    @pl.when(step == 0)
    def _():
        total_ref[...] = jnp.zeros_like(total_ref)

    store_half(act_ref, out_back_ref, keep_ref, send_ref)
    total_ref[...] += dot_nn(act_ref[...], buffer_ref[slot])
    next_shard(weight_refs, buffer_ref, semaphores)

    @pl.when(step == pl.num_programs(0) - 1)
    def _():
        out_ref[...] = total_ref[...].astype(LOW)


def add_shards_kernel(*refs, count):
    operands, outs = refs[:count], refs[count:]
    total = operands[0][0].astype(WIDE)
    for operand in operands[1:]:
        total += operand[0].astype(WIDE)
    if len(outs) == 1:
        outs[0][0] = total.astype(outs[0].dtype)
        return
    half = pl.num_programs(1) // 2
    for place, out_ref in enumerate(outs):

        @pl.when(pl.program_id(1) // half == place)
        def _(out_ref=out_ref):
            out_ref[0] = total.astype(out_ref.dtype)


def add_shards(operands, start, count, kind, parts, name, after=()):
    _, rows, columns = operands[0].shape
    tile = rows // 2 if rows % 32 == 0 else rows
    steps = rows // tile
    parts = parts if steps % 2 == 0 else 1
    half = steps // parts
    block = pl.BlockSpec((1, tile, columns), lambda i, j: (start + i, j, 0))

    def out_block(place):
        last = half - 1
        return pl.BlockSpec(
            (1, tile, columns), lambda i, j: (i, jnp.clip(j - place * half, 0, last), 0)
        )

    return run(
        functools.partial(add_shards_kernel, count=len(operands)),
        [shaped((count, rows // parts, columns), kind)] * parts,
        operands,
        name,
        flops=0,
        grid=(count, steps),
        in_specs=[block] * len(operands),
        out_specs=[out_block(place) for place in range(parts)],
        after=after,
    )


def gather_shards(keep, send):
    operands = [keep, swap(send, "dp", 1)]
    size = keep.shape[0]
    while size > 2:
        half = size // 2
        gone = add_shards(operands, half, half, LOW, 1, "add_shards")
        operands.append(swap(gone[0], "dp", 2 * half))
        size = half
    gone = add_shards(operands, 1, 1, LOW, 1, "add_shards")
    return operands, [swap(part, "dp", 2) for part in gone], gone[0]


def finish_kernel(*refs, count, steps):
    former_refs, came_refs, (out_ref, mark_ref) = refs[:count], refs[count:-2], refs[-2:]
    total = former_refs[0][0].astype(WIDE)
    for former_ref in former_refs[1:]:
        total += former_ref[0].astype(WIDE)
    half = steps // len(came_refs)
    for place, came_ref in enumerate(came_refs):

        @pl.when(pl.program_id(0) // half == place)
        def _(came_ref=came_ref):
            out_ref[...] = total + came_ref[0].astype(WIDE)

    mark_ref[...] = jnp.zeros_like(mark_ref)


def finish_shards(formers, came):
    _, rows, columns = formers[0].shape
    tile = rows // 2 if rows % 32 == 0 else rows
    steps = rows // tile
    half = steps // len(came)
    block = pl.BlockSpec((1, tile, columns), lambda i: (0, i, 0))
    parts = [
        pl.BlockSpec(
            (1, tile, columns), lambda i, place=place: (0, jnp.clip(i - place * half, 0, half - 1), 0)
        )
        for place in range(len(came))
    ]
    return run(
        functools.partial(finish_kernel, count=len(formers), steps=steps),
        [shaped((rows, columns), WIDE), shaped((8, 128), WIDE)],
        (*formers, *came),
        "finish_shards",
        flops=0,
        grid=(steps,),
        in_specs=[block] * len(formers) + parts,
        out_specs=[pl.BlockSpec((tile, columns), lambda i: (i, 0)), fixed((8, 128))],
    )


def after_kernel(
    home_ref,
    place_ref,
    residual_ref,
    gain_ref,
    upstream_ref,
    weight_ref,
    att_back_ref,
    residual_back_ref,
    branch_ref,
    gain_back_ref,
):
    hot = hot_columns(place_ref[...], home_ref.shape[0])
    normed_back = dot_nn(hot, home_ref[...])
    residual = residual_ref[...]
    scale = lax.rsqrt(jnp.mean(residual * residual, axis=-1, keepdims=True) + EPSILON)
    spread = residual * scale
    gained = gain_ref[...].astype(WIDE) * normed_back
    inner = jnp.mean(gained * spread, axis=-1, keepdims=True)
    back = upstream_ref[...].astype(WIDE) + scale * (gained - spread * inner)
    residual_back_ref[...] = back
    branch = back.astype(LOW)
    branch_ref[...] = branch
    gain_back_ref[...] = jnp.broadcast_to(
        jnp.sum(normed_back * spread, axis=0, keepdims=True), gain_back_ref.shape
    )
    att_back_ref[...] = dot_nt(weight_ref[...], branch).astype(LOW)


def output_pieces_kernel(core_ref, att_ref, branch_ref, router_ref, gain_ref, *refs, owners):
    *out_refs, full_ref = refs
    grad = dot_nn(att_ref[...], branch_ref[...])
    own = grad.shape[0] // owners
    height = full_ref.shape[0] // owners
    full_ref[...] = jnp.zeros_like(full_ref)
    for owner in range(owners):
        full_ref[owner * height : owner * height + own, :] = grad[owner * own : (owner + 1) * own]
    at = own + router_ref.shape[0]
    full_ref[own:at, :] = router_ref[...]
    full_ref[at : at + 8, :] = gain_ref[...]
    for place, out_ref in enumerate(out_refs):
        height = out_ref.shape[0]
        start = pl.multiple_of(jnp.bitwise_xor(core_ref[0], place) * height, height)
        out_ref[...] = full_ref[pl.ds(start, height), :].astype(out_ref.dtype)


def is_cube():
    return [lax.axis_size(name) for name in ("head", "blk", "dp")] == [4, 2, 4]


def sums_kernel(me_ref, *refs, count):
    operands, outs = refs[: len(refs) - count], refs[len(refs) - count :]
    for place, out_ref in enumerate(outs):
        height = out_ref.shape[0]
        start = pl.multiple_of(jnp.bitwise_xor(me_ref[0], place) * height, height)
        total = operands[0][pl.ds(start, height), :].astype(WIDE)
        for operand in operands[1:]:
            total += operand[pl.ds(start, height), :].astype(WIDE)
        out_ref[...] = total.astype(out_ref.dtype)


def sums(me, operands, count, name, after=()):
    height, breadth = operands[0].shape
    return run(
        functools.partial(sums_kernel, count=count),
        [shaped((height // count, breadth), LOW)] * count,
        (me[None].astype(jnp.int32), *operands),
        name,
        flops=0,
        in_specs=[SMEM] + [VMEM] * len(operands),
        after=after,
    )


def cross(mine, other, name, after=()):
    spot = lax.axis_index("blk") * 2 + lax.axis_index("dp") // 2
    own, along, across, corner = sums(spot, (mine, swap(other, "dp", 1)), 4, name, after)
    diagonal = [(b * 4 + d, (1 - b) * 4 + (d ^ 2)) for b in range(2) for d in range(4)]
    return [
        own,
        swap(across, "blk", 1),
        swap(along, "dp", 2),
        lax.ppermute(corner, ("blk", "dp"), diagonal),
    ]


def output_pieces(att_tok, branch_back, router_back, gain_back):
    model_width, experts = branch_back.shape[1], router_back.shape[0]
    cube = is_cube()
    owners = 8 if cube else 1
    height = owners * -(-(model_width // owners + experts + 8) // 128) * 128
    dp = lax.axis_index("dp")
    count = 2 if cube else 1
    outs = run(
        functools.partial(output_pieces_kernel, owners=owners),
        [shaped((height // count, model_width), LOW if cube else WIDE)] * count,
        (
            ((dp & 1) * (count - 1)).astype(jnp.int32)[None],
            att_tok,
            branch_back,
            router_back,
            gain_back,
        ),
        "output_pieces",
        flops=2 * att_tok.size * model_width,
        in_specs=[SMEM] + [VMEM] * 4,
        scratch=[pltpu.VMEM((height, model_width), WIDE)],
    )
    if not cube:
        return (), (), lax.psum(outs[0], ("head", "blk", "dp"))
    own, *came = cross(*outs, "output_core")
    shares = sums(lax.axis_index("head"), (own, *came), 4, "output_sum")
    arrived = [shares[0]] + [swap(shares[step], "head", step) for step in range(1, 4)]
    return (own,), (shares[0],), arrived


def output_kernel(
    residual_ref, normed_ref, router_ref, chosen_ref, place_ref, slots_ref, out_ref, *, experts
):
    probs, lane = route(normed_ref[...], router_ref[...], experts)
    hot = (lane == chosen_ref[...]).astype(WIDE)
    gate = jnp.sum(probs * hot, axis=-1, keepdims=True)
    expert_out = dot_nn(hot_columns(place_ref[...], slots_ref.shape[0]), slots_ref[...])
    out_ref[...] = (residual_ref[...] + gate * expert_out).astype(LOW)


def tokens_grad_kernel(
    triples_ref,
    query_weight_ref,
    key_weight_ref,
    value_weight_ref,
    tokens_ref,
    gain_ref,
    residual_back_ref,
    out_ref,
):
    groups = triples_ref.shape[0]
    weight_refs = (query_weight_ref, key_weight_ref, value_weight_ref)
    normed_back = jnp.zeros(out_ref.shape[::-1], WIDE)
    for kind, weight_ref in enumerate(weight_refs):
        rows = jnp.concatenate([triples_ref[group, kind] for group in range(groups)], 0)
        normed_back += dot_nn(weight_ref[...], rows)
    normed_back = normed_back.T
    values = tokens_ref[...].astype(WIDE)
    scale = lax.rsqrt(jnp.mean(values * values, axis=-1, keepdims=True) + EPSILON)
    spread = values * scale
    gained = gain_ref[...].astype(WIDE) * normed_back
    inner = jnp.mean(gained * spread, axis=-1, keepdims=True)
    out_ref[...] = (residual_back_ref[...] + scale * (gained - spread * inner)).astype(LOW)


def bucket_sums(diagonal, bucket_row, buckets):
    breadth = bucket_row.shape[1]
    hot = lax.broadcasted_iota(jnp.int32, (buckets, breadth), 0) == bucket_row
    hot = hot.astype(WIDE).astype(LOW)
    high = diagonal.astype(LOW)
    rest = diagonal - high.astype(WIDE)
    middle = rest.astype(LOW)
    small = (rest - middle.astype(WIDE)).astype(LOW)
    return dot_nt(high, hot) + dot_nt(middle, hot) + dot_nt(small, hot)


def side(grads):
    return -(-3 * grads // 128) * 128


def blocks_of(refs):
    return [ref[place] for ref in refs for place in range(ref.shape[0])]


def projection_grads(turned_ref, query_refs, pairs_ref):
    _, width, tokens = query_refs[0].shape
    queries = blocks_of(query_refs)
    groups = len(queries)
    spare = jnp.zeros((side(width) - 3 * width, tokens), LOW)
    total = None
    for group in range(groups):
        rows = [queries[group], pairs_ref[group, 0], pairs_ref[group, 1], spare]
        part = dot_nt(turned_ref[group], jnp.concatenate(rows, 0))
        total = part if total is None else total + part
    return total


def table_sums(diagonal_refs, bucket_refs, buckets):
    table = bucket_sums(diagonal_refs[0][...], bucket_refs[0][...], buckets)
    for diagonal_ref, bucket_ref in zip(diagonal_refs[1:], bucket_refs[1:]):
        table += bucket_sums(diagonal_ref[...], bucket_ref[...], buckets)
    return table


def add_pairs(home_refs):
    total = home_refs[0][...].astype(WIDE)
    for home_ref in home_refs[1:]:
        total += home_ref[...].astype(WIDE)
    return total.astype(LOW)


def triples_kernel(*refs, parts):
    pairs = add_pairs(refs[parts:-1])
    for group, queries in enumerate(blocks_of(refs[:parts])):
        refs[-1][group, 0] = queries
        refs[-1][group, 1] = pairs[group, 0]
        refs[-1][group, 2] = pairs[group, 1]


def pieces_kernel(core_ref, turned_ref, *refs, parts, tiles, buckets):
    query_refs, refs = refs[:parts], refs[parts:]
    home_refs, refs = refs[:tiles], refs[tiles:]
    diagonal_refs, bucket_refs = refs[:tiles], refs[tiles : 2 * tiles]
    *out_refs, pairs_ref, full_ref = refs[2 * tiles :]
    width = query_refs[0].shape[1]
    pairs_ref[...] = add_pairs(home_refs)
    full_ref[...] = projection_grads(turned_ref, query_refs, pairs_ref)
    table = table_sums(diagonal_refs, bucket_refs, buckets)
    full_ref[0:8, 3 * width : 3 * width + buckets] = table
    for place, out_ref in enumerate(out_refs):
        height = out_ref.shape[0]
        start = pl.multiple_of(jnp.bitwise_xor(core_ref[0], place) * height, height)
        out_ref[...] = full_ref[pl.ds(start, height), :].astype(out_ref.dtype)


def join_kernel(*refs):
    *refs, out_ref = refs
    copies, halves, part, _ = out_ref.shape
    count = len(refs) // 2
    columns = refs[0].shape[1]
    total, packed = (
        functools.reduce(jnp.add, [ref[...].astype(WIDE) for ref in group])
        for group in (refs[:count], refs[count:])
    )
    height = packed.shape[0] // halves
    for half in range(halves):
        former = total[half * part : (half + 1) * part].astype(LOW)
        rows = packed[half * height : (half + 1) * height]
        blocks = [rows[:, at : at + 256] for at in range(0, rows.shape[1], 256)]
        latter = jnp.concatenate(blocks, 0).astype(LOW)
        for copy in range(copies):
            out_ref[copy, half, :, :columns] = former
            out_ref[copy, half, :, columns:] = latter


def share_kernel(spot_ref, cases, places, weight_refs, out_refs, sums_ref, table_ref, extra_ref, heads):
    step = pl.program_id(0)
    owner = jnp.bitwise_xor(spot_ref[0], places[0] if len(places) == 1 else place_at(step, places))
    part = out_refs[0].shape[0] // 2
    width = heads * HEAD_DIM
    columns = side(width)
    buckets = table_ref.shape[2]
    for case, pair in enumerate(cases):

        @pl.when(step == case)
        def _(pair=pair):
            for half in range(2):
                groups = pair[half].shape[0]
                for group in range(groups):
                    whole = pair[half][group, half if pair[half].shape[1] == 2 else 0]
                    piece = whole[:, :columns].astype(WIDE)
                    for kind in range(3):
                        out_refs[kind][
                            half * part : (half + 1) * part, group * width : (group + 1) * width
                        ] = piece[:, kind * width : (kind + 1) * width]
                    packed = whole[:, columns:].astype(WIDE)
                    rows = jnp.concatenate([packed[at : at + 16] for at in range(0, part, 16)], 1)
                    if group + 1 < groups:
                        start = group * 32 + half * 16
                        out_refs[3][start : start + 16, :] = rows
                    else:

                        @pl.when(owner == 0)
                        def _(rows=rows, half=half):
                            extra_ref[half * 16 : half * 16 + 16, :] = rows

                    if half == 0:

                        @pl.when(owner == 0)
                        def _(piece=piece, group=group):
                            table_ref[group] = piece[:8, 3 * width : 3 * width + buckets]

    shares = jnp.zeros((2 * part, 1), WIDE)
    for kind in range(3):
        shares += jnp.sum(
            out_refs[kind][...] * weight_refs[kind][...].astype(WIDE), axis=1, keepdims=True
        )
    shares = jnp.broadcast_to(shares, (2 * part, 128))
    if sums_ref.shape[0] == 2 * part:
        sums_ref[...] = shares
    else:
        sums_ref[pl.ds(owner * 2 * part, 2 * part), :] = shares


def place_at(step, places):
    return sum(jnp.where(step == at, place, 0) for at, place in enumerate(places))


FIRST_PLACES, LAST_PLACES = (0, 1, 2, 4, 5, 6), (3, 7)


def first_shares_kernel(spot_ref, *refs, heads):
    piece_refs, weight_refs, refs = refs[:6], refs[6:9], refs[9:]
    out_refs, (sums_ref, table_ref, extra_ref) = refs[:4], refs[4:]

    @pl.when(pl.program_id(0) == 0)
    def _():
        table_ref[...] = jnp.zeros_like(table_ref)
        extra_ref[...] = jnp.zeros_like(extra_ref)

    cases = [(ref, ref) for ref in piece_refs]
    share_kernel(
        spot_ref, cases, FIRST_PLACES, weight_refs, out_refs, sums_ref, table_ref, extra_ref, heads
    )


def last_shares_kernel(spot_ref, *refs, heads, experts):
    piece_refs, weight_refs, refs = refs[:4], refs[4:7], refs[7:]
    gain_ref, sums_in, table_in, extra_in, *refs = refs
    out_refs, refs = refs[4:8], refs[8:]
    gain_out, second_out, table_out, router_out, sums_ref, table_ref, extra_ref = refs
    step = pl.program_id(0)

    @pl.when(step == 0)
    def _():
        sums_ref[...] = sums_in[...]
        table_ref[...] = table_in[...]
        extra_ref[...] = extra_in[...]

    cases = [(piece_refs[0], piece_refs[1]), (piece_refs[2], piece_refs[3])]
    share_kernel(
        spot_ref, cases, LAST_PLACES, weight_refs, out_refs, sums_ref, table_ref, extra_ref, heads
    )

    @pl.when(step == pl.num_programs(0) - 1)
    def _():
        first = sums_ref[...].T[0:8] / gain_ref[...].astype(WIDE)
        second = extra_ref[experts : experts + 8, :]
        for lane in range(gain_out.shape[0]):
            gain_out[lane : lane + 1, :] = first[0:1, lane * 128 : (lane + 1) * 128]
            second_out[lane : lane + 1, :] = second[0:1, lane * 128 : (lane + 1) * 128]
        router_out[...] = extra_ref[:experts, :]
        for group in range(table_ref.shape[0]):
            table_out[group * heads : (group + 1) * heads, :] = table_ref[group][:heads]


def put_together(me, first, corners, weights, gain, heads, buckets, experts):
    model_width = weights[0].shape[0]
    groups, _, part, _ = first[0].shape

    def rows(places, breadth):
        return pl.BlockSpec(
            (2 * part, breadth), lambda i, me: (place_at(i, places) ^ me[0], 0)
        )

    square = shaped((model_width, model_width), WIDE)
    kept_shapes = [(groups, 8, buckets), (32, model_width)]
    *grads, sums, table, extra = run_with_scalar(
        functools.partial(first_shares_kernel, heads=heads),
        me,
        [square] * 4 + [shaped((model_width, 128), WIDE)] + [shaped(x, WIDE) for x in kept_shapes],
        (*first, *weights),
        "first_shares",
        grid=(len(FIRST_PLACES),),
        in_specs=[fixed(x.shape) for x in first] + [rows(FIRST_PLACES, model_width)] * 3,
        out_specs=[rows(FIRST_PLACES, model_width)] * 4
        + [rows(FIRST_PLACES, 128)]
        + [fixed(x) for x in kept_shapes],
    )
    corners = [gate(array, (table,)) for array in corners]
    last = (*corners, *(swap(array, "dp", 1) for array in corners))
    operands = (*last, *weights, gain, sums, table, extra, *grads)
    vectors = [(model_width // 128, 128)] * 2 + [(groups * heads, buckets), (experts, model_width)]
    count = len(last)
    *grads, shares, second, table, router = run_with_scalar(
        functools.partial(last_shares_kernel, heads=heads, experts=experts),
        me,
        [square] * 4 + [shaped(x, WIDE) for x in vectors],
        operands,
        "last_shares",
        grid=(len(LAST_PLACES),),
        in_specs=[fixed(x.shape) for x in last]
        + [rows(LAST_PLACES, model_width)] * 3
        + [fixed(x.shape) for x in operands[count + 3 : count + 7]]
        + [pl.BlockSpec(memory_space=pltpu.HBM)] * 4,
        out_specs=[rows(LAST_PLACES, model_width)] * 4 + [fixed(x) for x in vectors],
        scratch=[pltpu.VMEM((model_width, 128), WIDE)] + [pltpu.VMEM(x, WIDE) for x in kept_shapes],
        aliases={count + 8 + i: i for i in range(4)},
    )
    query_grad, key_grad, value_grad, output_grad = grads
    return (
        query_grad,
        key_grad,
        value_grad,
        shares.reshape(-1),
        table.T,
        output_grad,
        router.T,
        second.reshape(-1),
    )


def take_half_kernel(values_ref, out_ref):
    out_ref[...] = values_ref[...]


def take_half(values, half):
    groups, _, *rest = values.shape
    return pl.pallas_call(
        take_half_kernel,
        out_shape=pltpu.HBM((groups, 1, *rest), values.dtype),
        grid=(groups,),
        in_specs=[pl.BlockSpec((1, 1, *rest), lambda i: (i, half, 0, 0))],
        out_specs=pl.BlockSpec((1, 1, *rest), lambda i: (i, 0, 0, 0)),
        compiler_params=pltpu.CompilerParams(vmem_limit_bytes=VMEM_BYTES),
        name="take_half",
    )(values)


def weight_sums(
    turned, query_backs, home, diagonals, bucket_rows, buckets, weights, gain, experts, packed, middle, late
):
    groups, model_width, _ = turned.shape
    width = query_backs[0].shape[1]
    heads = width // HEAD_DIM
    tiles = len(diagonals)
    cube = is_cube()
    columns = side(width)
    dp, blk = lax.axis_index("dp"), lax.axis_index("blk")
    count = 2 if cube else 1
    pieces = run(
        functools.partial(pieces_kernel, parts=len(query_backs), tiles=tiles, buckets=buckets),
        [shaped((model_width // count, columns), LOW if cube else WIDE)] * count,
        (
            ((dp & 1) * (count - 1)).astype(jnp.int32)[None],
            turned,
            *query_backs,
            *home,
            *diagonals,
            *bucket_rows,
        ),
        "projection_pieces",
        flops=6 * turned.size * width,
        in_specs=[SMEM] + [VMEM] * (1 + len(query_backs) + 3 * tiles),
        scratch=[pltpu.VMEM(home[0].shape, LOW), pltpu.VMEM((model_width, columns), WIDE)],
    )
    if not cube:
        sums = lax.psum(pieces[0], ("blk", "dp"))
        table = lax.all_gather(
            sums[:heads, 3 * width : 3 * width + buckets], "head", axis=0, tiled=True
        )
        grads = sums[:, : 3 * width].reshape(model_width, 3, width)
        grads = lax.all_gather(grads, "head", axis=2, tiled=True)
        grads = [grads[:, i] for i in range(3)]
        shares = sum(jnp.sum(x * y.astype(WIDE), axis=1) for x, y in zip(grads, weights))
        rest = packed[model_width:]
        shares = shares / gain[0].astype(WIDE)
        packed = packed[:model_width], rest[:experts].T, rest[experts]
        return pieces, *grads, shares, table.T, *packed
    part = model_width // 16
    copies = run(
        join_kernel,
        [shaped((groups, 2, part, columns + 256), LOW)],
        (*cross(*pieces, "projection_core", middle), *packed),
        "join",
        flops=0,
        after=late,
    )[0]
    own = blocks_over(copies, "head")
    across, along = swap(own, "blk", 1), swap(own, "dp", 2)
    corners = (
        swap(take_half(across, 0), "dp", 2),
        swap(take_half(along, 1), "blk", 1),
    )
    near_ones = (own, along, across)
    first = (*near_ones, *(swap(array, "dp", 1) for array in near_ones))
    me = ((dp & 1) * 4 + blk * 2 + dp // 2).astype(jnp.int32)[None]
    return pieces, *put_together(me, first, corners, weights, gain, heads, buckets, experts)


def body(
    tokens,
    first_gain,
    query_weight,
    key_weight,
    value_weight,
    output_weight,
    bias_table,
    second_gain,
    router_weight,
    inner_weight,
    outer_weight,
    expert_index,
    capacity_slot,
    bucket_of_offset,
    upstream,
):
    _, token_rows, model_width = tokens.shape
    groups = lax.axis_size("head")
    cycle = lax.axis_size("blk")
    shares = lax.axis_size("dp")
    width = model_width // groups
    heads = width // HEAD_DIM
    local_rows = groups * token_rows
    length = local_rows * cycle
    buckets = bias_table.shape[0]
    experts = router_weight.shape[1]
    capacity = max(2, 2 * token_rows // experts)
    slots = experts * capacity
    token_values, upstream_values = tokens[0], upstream[0]
    gain_one, gain_two = first_gain[None], second_gain[None]
    chosen = expert_index[0]
    place = chosen * capacity + capacity_slot[0]
    place_row, place_column, chosen_column = place[None], place[:, None], chosen[:, None]
    router = jnp.pad(router_weight, ((0, 0), (0, 128 - experts)))

    inner_shards, outer_shards = [inner_weight[0]], [outer_weight[0]]
    for held in (outer_shards, inner_shards):
        for bit in range(1, shares.bit_length() - 1):
            held += [swap(values, "dp", 1 << bit) for values in held]
    far_inner, far_outer = inner_shards[1:], outer_shards[1:]
    for held in (outer_shards, inner_shards):
        held[:] = [x for values in held for x in (values, swap(values, "dp", 1))]

    square = model_width * model_width
    pairs, normed_one = run(
        project_pairs_kernel,
        [
            shaped((groups, 2, width, token_rows), LOW),
            shaped((token_rows, model_width), LOW),
        ],
        (token_values, gain_one, key_weight, value_weight),
        "project_pairs",
        flops=4 * token_rows * square,
    )
    pairs = blocks_over(pairs, "head")
    head_start = (lax.axis_index("head") * heads).astype(jnp.int32)[None]
    table_rows = jnp.pad(bias_table.T, ((0, -(groups * heads) % 8), (0, 0)))
    bucket_line = jnp.pad(bucket_of_offset, (0, 1))[None]
    blk = lax.axis_index("blk")
    tile_buckets, tile_strips = [], []
    for step in range(cycle):
        number = lax.rem(blk + cycle - step, cycle)
        start = length + (number - blk - 1) * local_rows
        tile_buckets.append(lax.dynamic_slice_in_dim(bucket_line, start, 2 * local_rows, 1))
    tile_pairs = [pairs] + [turn(pairs, "blk", step) for step in range(1, cycle)]
    up_slots = run(
        scatter_kernel,
        [shaped((slots, model_width), LOW)],
        (place_row, upstream_values),
        "scatter_up",
        flops=2 * slots * token_rows * model_width,
        after=(normed_one,),
    )[0]
    turned = run(
        turn_kernel,
        [shaped((groups, model_width, token_rows), LOW)],
        (normed_one,),
        "turn",
        flops=0,
    )[0]
    queries = run(
        project_queries_kernel,
        [shaped((groups, width, token_rows), LOW)],
        (normed_one, query_weight),
        "project_queries",
        flops=2 * token_rows * square,
        after=(pairs, up_slots, turned),
    )[0]
    queries = blocks_over(queries, "head")
    up_rows = blocks_over(up_slots, ("head", "blk"))
    for step in range(0, cycle, 2):
        tile_strips += make_strips(
            head_start, table_rows, tile_buckets[step : step + 2], heads, (queries,)
        )
    tile_weights, before = [], ()
    for step in range(0, cycle, 2):
        tiles = slice(step, step + 2)
        last = step + 2 >= cycle
        results = attend(queries, tile_pairs[tiles], tile_strips[tiles], before, last)
        tile_weights += results[: len(tile_pairs[tiles])]
        total, attended, *rest = results[len(tile_pairs[tiles]) :]
        before = (attended, total)
    attended_low = gate(rest[0], (up_rows,))
    att_tok = blocks_over(attended_low, "head").reshape(model_width, token_rows)
    hidden = inner_shards[0].shape[1]
    full_hidden = shares * hidden
    product = 2 * slots * model_width * full_hidden
    hidden_block = pl.BlockSpec((slots, hidden), lambda i: (0, i))
    turned_block = pl.BlockSpec((slots, hidden), lambda i: (0, shard_at(i, shares)))
    raw = run(
        raw_back_kernel,
        [shaped((slots, full_hidden), LOW)],
        (near(up_rows), *outer_shards),
        "raw_back",
        flops=product,
        grid=(shares,),
        in_specs=[fixed(up_rows.shape)] + shard_places(outer_shards),
        out_specs=[hidden_block],
        scratch=shard_scratch(outer_shards),
    )[0]
    residual_mid, normed_two, normed_slots = run(
        middle_kernel,
        [
            shaped((token_rows, model_width), WIDE),
            shaped((token_rows, model_width), LOW),
            shaped((slots, model_width), LOW),
        ],
        (near(att_tok), token_values, output_weight, gain_two, place_row),
        "middle",
        flops=2 * token_rows * square + 2 * slots * token_rows * model_width,
        after=(raw, router, *far_inner),
    )
    expert_rows = blocks_over(normed_slots, ("head", "blk"))
    own_expert = (lax.axis_index("head") * cycle + blk).astype(jnp.int32)[None]
    hidden_act, pre_back, home_slots, out_back, logit_back = run(
        functools.partial(expert_kernel, experts=experts),
        [
            shaped((slots, full_hidden), LOW),
            shaped((slots, full_hidden), LOW),
            shaped((slots, model_width), LOW),
            shaped((slots, model_width), LOW),
            shaped((slots, 128), LOW),
        ],
        (own_expert, near(expert_rows), near(up_rows), router, raw, *inner_shards),
        "expert",
        flops=2 * product,
        grid=(shares,),
        in_specs=[
            SMEM,
            fixed(expert_rows.shape),
            fixed(up_rows.shape),
            fixed(router.shape),
            hidden_block,
            *shard_places(inner_shards),
        ],
        out_specs=[
            hidden_block,
            hidden_block,
            fixed((slots, model_width)),
            fixed((slots, model_width)),
            fixed((slots, 128)),
        ],
        scratch=[
            pltpu.VMEM((slots, model_width), WIDE),
            pltpu.VMEM((slots, 128), WIDE),
            pltpu.VMEM((slots, 128), WIDE),
            *shard_scratch(inner_shards),
        ],
    )
    home_rows = blocks_over(home_slots, ("head", "blk"))
    inner_shape, outer_shape = (model_width, hidden), (hidden, model_width)
    inner_keep, inner_send, router_back = run(
        inner_grads_kernel,
        [shaped((shares // 2, *inner_shape), LOW)] * 2 + [shaped((experts, model_width), WIDE)],
        (near(expert_rows), pre_back, logit_back),
        "inner_grads",
        flops=product,
        grid=(shares,),
        in_specs=[fixed(expert_rows.shape), turned_block, fixed(logit_back.shape)],
        out_specs=[
            keep_spec(inner_shape, shares),
            send_spec(inner_shape, shares),
            fixed((experts, model_width)),
        ],
    )
    turned_shards = outer_shards[1::2] + outer_shards[0::2]
    outer_keep, outer_send, expert_out = run(
        outer_grads_kernel,
        [shaped((shares // 2, *outer_shape), LOW)] * 2 + [shaped((slots, model_width), LOW)],
        (hidden_act, out_back, *turned_shards),
        "outer_grads",
        flops=2 * product,
        grid=(shares,),
        in_specs=[turned_block, fixed(out_back.shape)] + shard_places(outer_shards),
        out_specs=[
            keep_spec(outer_shape, shares),
            send_spec(outer_shape, shares),
            fixed((slots, model_width)),
        ],
        scratch=[pltpu.VMEM((slots, model_width), WIDE)] + shard_scratch(outer_shards),
    )
    att_back, residual_back, branch_back, gain_back = run(
        after_kernel,
        [
            shaped((model_width, token_rows), LOW),
            shaped((token_rows, model_width), WIDE),
            shaped((token_rows, model_width), LOW),
            shaped((8, model_width), WIDE),
        ],
        (near(home_rows), place_column, residual_mid, gain_two, upstream_values, output_weight),
        "after",
        flops=2 * token_rows * square + 2 * slots * token_rows * model_width,
        after=(router_back, expert_out),
    )
    head_back = blocks_over(att_back.reshape(groups, width, token_rows), "head")
    packed_core, packed_sum, packed_shares = output_pieces(
        att_tok, branch_back, router_back, gain_back
    )
    *inner_parts, inner_gone = gather_shards(inner_keep, gate(inner_send, (att_back,)))
    *outer_parts, outer_gone = gather_shards(outer_keep, gate(outer_send, (att_back,)))
    turned = gate(turned, (head_back, *packed_core, inner_gone, outer_gone))
    turned_all = blocks_over(turned, "head")

    before, diagonals, home, query_backs = (), [], [], []
    for step in range(1, cycle):
        query_back, pairs_part, diagonal = attend_back(
            queries,
            head_back,
            attended,
            total,
            tile_weights[step],
            tile_pairs[step],
            before,
            False,
            0,
            groups,
            (),
        )
        before = (query_back,)
        diagonals.append(diagonal)
        home.append(turn(pairs_part, "blk", cycle - step))
    cut = groups - 1
    for begin, count, after in (
        (0, cut, packed_sum),
        (cut, groups - cut, (turned_all, *home[:1], *inner_parts[1])),
    ):
        query_back, pairs_part, diagonal = attend_back(
            queries,
            head_back,
            attended,
            total,
            tile_weights[0],
            tile_pairs[0],
            before,
            True,
            begin,
            count,
            after,
        )
        query_backs.append(query_back)
        if begin == 0:
            out_rows = blocks_over(gate(expert_out, (turned_all, query_back)), ("head", "blk"))
        diagonals.append(diagonal)
        home.append(pairs_part)
    diagonal_buckets = [*tile_buckets[1:], tile_buckets[0], tile_buckets[0]]
    (
        pieces,
        query_grad,
        key_grad,
        value_grad,
        first_gain_grad,
        table_grad,
        output_grad,
        router_grad,
        second_gain_grad,
    ) = weight_sums(
        turned_all,
        query_backs,
        home,
        diagonals,
        diagonal_buckets,
        buckets,
        (query_weight, key_weight, value_weight),
        gain_one,
        experts,
        packed_shares,
        (out_rows,),
        tuple(outer_parts[1]),
    )
    layer_output = run(
        functools.partial(output_kernel, experts=experts),
        [shaped((token_rows, model_width), LOW)],
        (residual_mid, normed_two, router, chosen_column, place_column, out_rows),
        "layer_output",
        flops=2 * slots * token_rows * model_width,
    )[0]
    inner_part, inner_mark = finish_shards(*inner_parts)
    outer_part, outer_mark = finish_shards(*outer_parts)
    triples = run(
        functools.partial(triples_kernel, parts=len(query_backs)),
        [shaped((groups, 3, width, token_rows), LOW)],
        (*query_backs, *home),
        "triples",
        flops=0,
        after=(pieces[0], layer_output, inner_mark),
    )[0]
    triples_tok = blocks_over(triples, "head")
    tokens_grad = run(
        tokens_grad_kernel,
        [shaped((token_rows, model_width), LOW)],
        (
            triples_tok,
            query_weight,
            key_weight,
            value_weight,
            token_values,
            gain_one,
            residual_back,
        ),
        "tokens_grad",
        flops=6 * token_rows * square,
        after=(outer_mark,),
    )[0]
    return (
        layer_output[None],
        tokens_grad[None],
        first_gain_grad,
        query_grad,
        key_grad,
        value_grad,
        output_grad,
        table_grad,
        second_gain_grad,
        router_grad,
        inner_part[None],
        outer_part[None],
    )


def solution(mesh):
    return jax.shard_map(
        body,
        mesh=mesh,
        in_specs=(
            P("dp", ("blk", "head"), None),
            P(),
            P(),
            P(),
            P(),
            P(),
            P(),
            P(),
            P(),
            P(("head", "blk"), None, "dp"),
            P(("head", "blk"), "dp", None),
            P("dp", ("blk", "head")),
            P("dp", ("blk", "head")),
            P(),
            P("dp", ("blk", "head"), None),
        ),
        out_specs=(
            P("dp", ("blk", "head"), None),
            P("dp", ("blk", "head"), None),
            P(),
            P(),
            P(),
            P(),
            P(),
            P(),
            P(),
            P(),
            P(("head", "blk"), None, "dp"),
            P(("head", "blk"), "dp", None),
        ),
        check_vma=False,
    )
```

```python
import functools
import math

import jax
import jax.numpy as jnp
from jax import lax
from jax.experimental import pallas as pl
from jax.experimental.pallas import tpu as pltpu
from jax.sharding import PartitionSpec as P

HEAD_DIM = 64
EPSILON = 1e-06
STRIP = 128
VMEM_BYTES = 28 * 2**20
LOW = jnp.bfloat16
WIDE = jnp.float32


def dot_nt(former, latter):
    return lax.dot_general(former, latter, (((1,), (1,)), ((), ())), preferred_element_type=WIDE)


def dot_nn(former, latter):
    return lax.dot_general(former, latter, (((1,), (0,)), ((), ())), preferred_element_type=WIDE)


def dot_tn(former, latter):
    return lax.dot_general(former, latter, (((0,), (0,)), ((), ())), preferred_element_type=WIDE)


def shaped(shape, kind):
    return pltpu.HBM(tuple(shape), kind)


def kept(shape, kind):
    return pltpu.VMEM(tuple(shape), kind)


class Near:
    def __init__(self, values):
        self.values, self.shape, self.dtype = values, values.shape, values.dtype


def near(values):
    return Near(values)


class Loose(Near):
    pass


def loose(values):
    return Loose(values)


def fixed(shape):
    return pl.BlockSpec(tuple(shape), lambda *_: (0,) * len(shape), pipeline_mode=pl.Buffered(1))


def received_loose(home):
    return [loose(x) if x.dtype == LOW else x for x in home]


def placed(values):
    if isinstance(values, Loose):
        return values.values
    if isinstance(values, Near):
        return pltpu.with_memory_space_constraint(values.values, pltpu.VMEM)
    return pltpu.with_memory_space_constraint(values, pltpu.HBM)


def unread(values):
    return pl.BlockSpec(memory_space=pl.ANY if isinstance(values, Loose) else pltpu.HBM)


def run(
    kernel, outs, operands, name, flops, grid=None, in_specs=None, out_specs=None, scratch=(), after=()
):
    moved = sum(math.prod(x.shape) * jnp.dtype(x.dtype).itemsize for x in (*operands, *outs))
    count, skipped = len(operands), len(after)
    if grid is None:
        grid = (1,)
        out_specs = [fixed(x.shape) for x in outs]
    if in_specs is None:
        in_specs = [VMEM] * count
    in_specs = [fixed(x.shape) if spec is VMEM else spec for x, spec in zip(operands, in_specs)]

    def body(*refs):
        kernel(*refs[:count], *refs[count + skipped :])

    return pl.pallas_call(
        body,
        out_shape=list(outs),
        grid=grid,
        in_specs=in_specs + [unread(x) for x in after],
        out_specs=out_specs,
        scratch_shapes=list(scratch),
        compiler_params=pltpu.CompilerParams(vmem_limit_bytes=VMEM_BYTES),
        cost_estimate=pl.CostEstimate(flops=flops, bytes_accessed=moved, transcendentals=0),
        name=name,
    )(
        *(x if spec is SMEM else placed(x) for x, spec in zip(operands, in_specs)),
        *(placed(x) for x in after),
    )


def run_with_scalar(
    kernel, scalar, outs, operands, name, grid, in_specs, out_specs, scratch=(), aliases=None
):
    return pl.pallas_call(
        kernel,
        out_shape=list(outs),
        grid_spec=pltpu.PrefetchScalarGridSpec(
            num_scalar_prefetch=1,
            grid=grid,
            in_specs=in_specs,
            out_specs=out_specs,
            scratch_shapes=list(scratch),
        ),
        compiler_params=pltpu.CompilerParams(vmem_limit_bytes=VMEM_BYTES),
        input_output_aliases=aliases or {},
        name=name,
    )(scalar, *(placed(x) for x in operands))


SMEM = pl.BlockSpec(memory_space=pltpu.SMEM)
VMEM = pl.BlockSpec(memory_space=pltpu.VMEM)


def swap(values, axis, bit):
    return lax.ppermute(values, axis, [(i, i ^ bit) for i in range(lax.axis_size(axis))])


def turn(values, axis, step):
    size = lax.axis_size(axis)
    return lax.ppermute(values, axis, [(i, (i + step) % size) for i in range(size)])


def blocks_over(values, axis):
    return lax.all_to_all(values, axis, split_axis=0, concat_axis=0, tiled=True)


def project_pairs_kernel(tokens_ref, gain_ref, key_ref, value_ref, pairs_ref, normed_ref):
    values = tokens_ref[...].astype(WIDE)
    scale = lax.rsqrt(jnp.mean(values * values, axis=-1, keepdims=True) + EPSILON)
    normed = (values * scale * gain_ref[...].astype(WIDE)).astype(LOW)
    normed_ref[...] = normed
    groups, _, width, _ = pairs_ref.shape
    for kind, weight_ref in enumerate((key_ref, value_ref)):
        rows = dot_nn(normed, weight_ref[...]).T
        for group in range(groups):
            pairs_ref[group, kind] = rows[group * width : (group + 1) * width].astype(LOW)


def project_queries_kernel(normed_ref, weight_ref, out_ref):
    rows = dot_nn(normed_ref[...], weight_ref[...]).T
    groups, width, _ = out_ref.shape
    for group in range(groups):
        out_ref[group] = rows[group * width : (group + 1) * width].astype(LOW)


def turn_kernel(normed_ref, out_ref):
    turned = normed_ref[...].astype(WIDE).T.astype(LOW)
    for copy in range(out_ref.shape[0]):
        out_ref[copy] = turned


def strips_kernel(start_ref, table_ref, *refs):
    tiles = (len(refs) - 1) // 2
    bucket_refs, strips_refs, rows_ref = refs[:tiles], refs[tiles : 2 * tiles], refs[-1]
    buckets = table_ref.shape[1]
    for bucket_ref, strips_ref in zip(bucket_refs, strips_refs):
        heads, _, span = strips_ref.shape
        breadth = bucket_ref.shape[1]
        hot = lax.broadcasted_iota(jnp.int32, (buckets, breadth), 0) == bucket_ref[...]
        rows_ref[...] = dot_nn(table_ref[...], hot.astype(WIDE).astype(LOW))
        for head in range(heads):
            row = rows_ref[pl.ds(start_ref[0] + head, 1), :]
            spread = jnp.broadcast_to(row, (STRIP, breadth))
            turned = pltpu.roll(spread, breadth - (STRIP - 1), 1, stride=1, stride_axis=0)
            strips_ref[head] = turned[:, :span]


def make_strips(head_start, table_rows, buckets, heads, after):
    breadth = buckets[0].shape[1]
    return run(
        strips_kernel,
        [kept((heads, STRIP, breadth - STRIP), WIDE)] * len(buckets),
        (head_start, table_rows, *buckets),
        "bias_strips",
        flops=2 * 12 * 32 * breadth,
        in_specs=[SMEM] + [VMEM] * (1 + len(buckets)),
        scratch=[pltpu.VMEM((table_rows.shape[0], breadth), WIDE)],
        after=after,
    )


def head_mask(shape, head):
    lane = lax.broadcasted_iota(jnp.int32, shape, 1)
    return (lane >= head * HEAD_DIM) & (lane < (head + 1) * HEAD_DIM)


def side_by_side(pairs_ref, kind):
    return jnp.concatenate([pairs_ref[group, kind] for group in range(pairs_ref.shape[0])], 1)


def attend_kernel(*refs, heads, rows, tiles, first, last):
    query_ref = refs[0]
    pairs_refs, strips_refs, refs = refs[1 : 1 + tiles], refs[1 + tiles : 1 + 2 * tiles], refs[1 + 2 * tiles :]
    if not first:
        numer_in, total_in = refs[:2]
        refs = refs[2:]
    weight_refs, (total_ref, out_ref) = refs[:tiles], refs[tiles : tiles + 2]
    tile = query_ref.shape[2]
    groups = pairs_refs[0].shape[0]
    step = pl.program_id(0)
    queries = (query_ref[0] * jnp.asarray(0.125, LOW)).astype(WIDE).T.astype(LOW)
    out = jnp.zeros(queries.shape, WIDE)
    sums = jnp.zeros(queries.shape, WIDE)
    for head in range(heads):
        mask = head_mask(queries.shape, head)
        masked = jnp.where(mask, queries, jnp.zeros_like(queries))
        lanes = jnp.zeros((tile, 128), WIDE)
        numerator = jnp.zeros(queries.shape, WIDE)
        for pairs_ref, strips_ref, weight_ref in zip(pairs_refs, strips_refs, weight_refs):
            keys = jnp.concatenate([pairs_ref[group, 0] for group in range(groups)], 1)
            values = jnp.concatenate([pairs_ref[group, 1] for group in range(groups)], 1)
            scores = dot_nn(masked, keys)
            parts = []
            for sub in range(tile // STRIP):
                start = pl.multiple_of(rows - STRIP - (step * tile + sub * STRIP), STRIP)
                parts.append(
                    jnp.exp(
                        scores[sub * STRIP : (sub + 1) * STRIP, :]
                        + strips_ref[head, :, pl.ds(start, rows)]
                    )
                )
            weights = jnp.concatenate(parts, 0)
            for lane in range(rows // 128):
                lanes = lanes + weights[:, lane * 128 : (lane + 1) * 128]
            low = weights.astype(LOW)
            weight_ref[head] = low
            numerator = numerator + dot_nt(low, values)
        total = jnp.sum(lanes, axis=1, keepdims=True)
        out = jnp.where(mask, numerator, out)
        sums = jnp.where(mask, total, sums)
    out, sums = out.T, sums.T
    if not first:
        out = out + numer_in[0]
        sums = sums + total_in[0]
    total_ref[0] = sums
    if last:
        out = out / sums
        refs[-1][0] = out.astype(LOW)
    out_ref[0] = out


def gate(values, after):
    return pl.pallas_call(
        lambda *refs: None,
        out_shape=jax.ShapeDtypeStruct(values.shape, values.dtype),
        in_specs=[pl.BlockSpec(memory_space=pl.ANY)] + [unread(x) for x in after],
        out_specs=pl.BlockSpec(memory_space=pl.ANY),
        input_output_aliases={0: 0},
        name="gate",
    )(values, *(placed(x) for x in after))


def attend(queries, pairs, strips, before, last):
    groups, width, tile = queries.shape
    rows = groups * tile
    heads = width // HEAD_DIM
    tiles = len(pairs)
    block = pl.BlockSpec((1, width, tile), lambda i: (i, 0, 0))
    weight_block = pl.BlockSpec((heads, tile, rows), lambda i: (0, i, 0))
    operands = (queries, *(loose(x) for x in pairs), *(near(x) for x in strips), *before)
    return run(
        functools.partial(attend_kernel, heads=heads, rows=rows, tiles=tiles, first=not before, last=last),
        [shaped((heads, rows, rows), LOW)] * tiles
        + [shaped(queries.shape, WIDE)] * 2
        + [shaped(queries.shape, LOW)] * last,
        operands,
        "attend",
        flops=16 * width * rows * rows * tiles,
        grid=(groups,),
        in_specs=[block]
        + [fixed(x.shape) for x in pairs]
        + [fixed(x.shape) for x in strips]
        + [block] * len(before),
        out_specs=[weight_block] * tiles + [block] * (2 + last),
    )


def attend_back_kernel(*refs, heads, rows, first, last, begin):
    query_ref, grad_ref, att_ref, total_ref, weight_ref, pairs_ref = refs[:6]
    refs = refs[6:]
    if not first:
        query_in = refs[0]
        refs = refs[1:]
    query_back_ref, pairs_back_ref, diagonal_ref, strips_ref, key_acc, value_acc = refs
    tile = query_ref.shape[2]
    groups, _, width, chunk = pairs_back_ref.shape
    span = strips_ref.shape[2]
    step = pl.program_id(0)
    block = step + begin

    @pl.when(step == 0)
    def _():
        strips_ref[...] = jnp.zeros_like(strips_ref)
        key_acc[...] = jnp.zeros_like(key_acc)
        value_acc[...] = jnp.zeros_like(value_acc)

    query_turned = query_ref[0] * jnp.asarray(0.125, LOW)
    grads = grad_ref[0].astype(WIDE)
    inverse = 1.0 / total_ref[0]
    numer_wide = grads * inverse
    numer_turned = numer_wide.astype(LOW)
    products = -(numer_wide * att_ref[0]).T
    numer_back = numer_turned.astype(WIDE).T.astype(LOW)
    out = jnp.zeros(numer_back.shape, WIDE)
    keys = side_by_side(pairs_ref, 0)
    values = side_by_side(pairs_ref, 1)
    for head in range(heads):
        mask = head_mask(numer_back.shape, head)
        masked = jnp.where(mask, numer_back, jnp.zeros_like(numer_back))
        denom_back = jnp.sum(jnp.where(mask, products, 0.0), axis=1, keepdims=True)
        here = slice(head * HEAD_DIM, (head + 1) * HEAD_DIM)
        query_here = query_turned[here]
        numer_here = numer_turned[here]
        weight_back = dot_nn(masked, values)
        weights = weight_ref[head]
        score_back = weights.astype(WIDE) * (weight_back + denom_back)
        low = score_back.astype(LOW)
        for sub in range(tile // STRIP):
            start = pl.multiple_of(rows - STRIP - (block * tile + sub * STRIP), STRIP)
            strips_ref[head, :, pl.ds(start, rows)] += score_back[sub * STRIP : (sub + 1) * STRIP, :]
        key_acc[here, :] += dot_nn(query_here, low)
        value_acc[here, :] += dot_nn(numer_here, weights)
        query_back = dot_nt(low, keys)
        out = jnp.where(mask, query_back * 0.125, out)
    out = out.T
    if not first:
        out = out + query_in[0]
    query_back_ref[0] = out.astype(query_back_ref.dtype)

    @pl.when(step == pl.num_programs(0) - 1)
    def _():
        for group in range(groups):
            at = group * chunk
            pairs_back_ref[group, 0] = key_acc[:, at : at + chunk].astype(pairs_back_ref.dtype)
            pairs_back_ref[group, 1] = value_acc[:, at : at + chunk].astype(pairs_back_ref.dtype)
        diagonal_ref[...] = jnp.zeros_like(diagonal_ref)
        for head in range(heads):
            folded = strips_ref[head]
            size = STRIP
            while size > 8:
                size //= 2
                folded = folded[:size] + pltpu.roll(folded[size:], span - size, 1)
            row = folded[0:1]
            for place in range(1, 8):
                row = row + pltpu.roll(folded[place : place + 1], span - place, 1)
            diagonal_ref[head : head + 1, :] = pltpu.roll(row, STRIP - 1, 1)

def attend_back(
    queries, grads, attended, total, weights, pairs, before, last, begin, count, after
):
    groups, width, tile = queries.shape
    rows = groups * tile
    heads = width // HEAD_DIM
    span = 2 * rows
    block = pl.BlockSpec((1, width, tile), lambda i: (i + begin, 0, 0))
    out_block = pl.BlockSpec((1, width, tile), lambda i: (i, 0, 0))
    operands = (queries, grads, attended, total, weights, pairs, *before)
    return run(
        functools.partial(attend_back_kernel, heads=heads, rows=rows, first=not before, last=last, begin=begin),
        [
            shaped((count, width, tile), LOW if last else WIDE),
            shaped(pairs.shape, WIDE if last else LOW),
            shaped((8, span), WIDE),
        ],
        operands,
        "attend_back",
        flops=8 * width * rows * rows * count,
        grid=(count,),
        in_specs=[block, block, block, block]
        + [pl.BlockSpec((heads, tile, rows), lambda i: (0, i + begin, 0)), fixed(pairs.shape)]
        + [block] * len(before),
        out_specs=[out_block, fixed(pairs.shape), fixed((8, span))],
        scratch=[pltpu.VMEM((heads, STRIP, span), WIDE), pltpu.VMEM((width, rows), WIDE), pltpu.VMEM((width, rows), WIDE)], after=after)


def hot_rows(place_row, slots):
    tokens = place_row.shape[1]
    hot = lax.broadcasted_iota(jnp.int32, (slots, tokens), 0) == place_row
    return hot.astype(WIDE).astype(LOW)


def hot_columns(place_column, slots):
    tokens = place_column.shape[0]
    hot = lax.broadcasted_iota(jnp.int32, (tokens, slots), 1) == place_column
    return hot.astype(WIDE).astype(LOW)


def scatter_kernel(place_ref, rows_ref, slots_ref):
    hot = hot_rows(place_ref[...], slots_ref.shape[0])
    slots_ref[...] = dot_nn(hot, rows_ref[...]).astype(LOW)


def middle_kernel(
    att_ref, tokens_ref, weight_ref, gain_ref, place_ref, residual_ref, normed_ref, slots_ref
):
    residual = tokens_ref[...].astype(WIDE) + dot_tn(att_ref[...], weight_ref[...])
    residual_ref[...] = residual
    scale = lax.rsqrt(jnp.mean(residual * residual, axis=-1, keepdims=True) + EPSILON)
    normed = (residual * scale * gain_ref[...].astype(WIDE)).astype(LOW)
    normed_ref[...] = normed
    hot = hot_rows(place_ref[...], slots_ref.shape[0])
    slots_ref[...] = dot_nn(hot, normed).astype(LOW)


def route(normed, router, experts):
    logits = dot_nn(normed, router)
    lane = lax.broadcasted_iota(jnp.int32, logits.shape, 1)
    logits = jnp.where(lane < experts, logits, -jnp.inf)
    powers = jnp.exp(logits - jnp.max(logits, axis=-1, keepdims=True))
    return powers / jnp.sum(powers, axis=-1, keepdims=True), lane


def shard_copy(weight_refs, buffer_ref, semaphores, at):
    return pltpu.make_async_copy(weight_refs[at], buffer_ref.at[at % 2], semaphores.at[at % 2])


def take_shard(weight_refs, buffer_ref, semaphores):
    step = pl.program_id(0)

    @pl.when(step == 0)
    def _():
        for at in range(min(2, len(weight_refs))):
            shard_copy(weight_refs, buffer_ref, semaphores, at).start()

    for at in range(len(weight_refs)):

        @pl.when(step == at)
        def _(at=at):
            shard_copy(weight_refs, buffer_ref, semaphores, at).wait()

    return lax.rem(step, 2)


def next_shard(weight_refs, buffer_ref, semaphores):
    for at in range(len(weight_refs) - 2):

        @pl.when(pl.program_id(0) == at)
        def _(at=at):
            shard_copy(weight_refs, buffer_ref, semaphores, at + 2).start()


def shard_scratch(weights):
    return [pltpu.VMEM((2, *weights[0].shape), LOW), pltpu.SemaphoreType.DMA((2,))]


def shard_places(weights):
    return [pl.BlockSpec(memory_space=pltpu.HBM)] * len(weights)


def raw_back_kernel(up_ref, *refs):
    *weight_refs, raw_ref, buffer_ref, semaphores = refs
    slot = take_shard(weight_refs, buffer_ref, semaphores)
    raw_ref[...] = dot_nt(up_ref[...], buffer_ref[slot]).astype(LOW)
    next_shard(weight_refs, buffer_ref, semaphores)


def expert_kernel(own_ref, rows_ref, up_ref, router_ref, raw_ref, *refs, experts):
    *weight_refs, act_ref, pre_ref, home_ref, out_back_ref, logit_ref = refs[:-5]
    back_acc, gate_acc, gate_ref, buffer_ref, semaphores = refs[-5:]
    slot = take_shard(weight_refs, buffer_ref, semaphores)
    step = pl.program_id(0)
    rows = rows_ref[...]

    @pl.when(step == 0)
    def _():
        probs, lane = route(rows, router_ref[...], experts)
        hot = (lane == own_ref[0]).astype(WIDE)
        gate = jnp.sum(probs * hot, axis=-1, keepdims=True)
        gate_ref[...] = jnp.broadcast_to(gate, gate_ref.shape)
        out_back_ref[...] = (gate * up_ref[...].astype(WIDE)).astype(LOW)
        back_acc[...] = jnp.zeros_like(back_acc)
        gate_acc[...] = jnp.zeros_like(gate_acc)

    gate = gate_ref[:, 0:1]
    lanes = gate_acc[...]
    back = back_acc[...]
    root = 0.7978845608028654
    hidden = buffer_ref.shape[2]
    size = 256 if hidden % 256 == 0 else 128
    count = hidden // size
    following = dot_nn(rows, buffer_ref[slot, :, 0:size])
    for piece in range(count):
        here = slice(piece * size, (piece + 1) * size)
        value = following
        if piece + 1 < count:
            following = dot_nn(rows, buffer_ref[slot, :, (piece + 1) * size : (piece + 2) * size])
        squared = value * value
        tilted = jnp.tanh(value * (root + (root * 0.044715) * squared))
        share = 0.5 + 0.5 * tilted
        wide = value * share
        act = wide.astype(LOW)
        slope = share + wide * (1.0 - share) * (2.0 * root + (6.0 * root * 0.044715) * squared)
        raw = raw_ref[:, here].astype(WIDE)
        pre = (gate * raw * slope).astype(LOW)
        act_ref[:, here] = act
        pre_ref[:, here] = pre
        back = back + dot_nt(pre, buffer_ref[slot, :, here])
        shares = act.astype(WIDE) * raw
        for lane in range(size // 128):
            lanes = lanes + shares[:, lane * 128 : (lane + 1) * 128]
    gate_acc[...] = lanes
    back_acc[...] = back
    next_shard(weight_refs, buffer_ref, semaphores)

    @pl.when(step == pl.num_programs(0) - 1)
    def _():
        probs, lane = route(rows, router_ref[...], experts)
        hot = (lane == own_ref[0]).astype(WIDE)
        gate = jnp.sum(probs * hot, axis=-1, keepdims=True)
        gate_back = jnp.sum(gate_acc[...], axis=-1, keepdims=True)
        logit_back = (probs * gate_back * (hot - gate)).astype(LOW)
        logit_ref[...] = logit_back
        home_ref[...] = (dot_nt(logit_back, router_ref[...]) + back_acc[...]).astype(LOW)


def store_half(former_ref, latter_ref, keep_ref, send_ref):
    count = pl.num_programs(0) // 2

    @pl.when(pl.program_id(0) < count)
    def _():
        send_ref[0] = dot_tn(former_ref[...], latter_ref[...]).astype(LOW)

    @pl.when(pl.program_id(0) >= count)
    def _():
        keep_ref[0] = dot_tn(former_ref[...], latter_ref[...]).astype(LOW)


def shard_at(i, shares):
    count = shares // 2
    return jnp.where(i < count, 2 * i + 1, 2 * (i - count))


def keep_spec(shape, shares):
    return pl.BlockSpec((1, *shape), lambda i: (jnp.maximum(i - shares // 2, 0), 0, 0))


def send_spec(shape, shares):
    return pl.BlockSpec((1, *shape), lambda i: (jnp.minimum(i, shares // 2 - 1), 0, 0))


def inner_grads_kernel(rows_ref, pre_ref, logit_ref, keep_ref, send_ref, router_ref):
    store_half(rows_ref, pre_ref, keep_ref, send_ref)

    @pl.when(pl.program_id(0) == 0)
    def _():
        router_ref[...] = dot_tn(logit_ref[...], rows_ref[...])[: router_ref.shape[0]]


def outer_grads_kernel(act_ref, out_back_ref, *refs):
    *weight_refs, keep_ref, send_ref, out_ref, total_ref, buffer_ref, semaphores = refs
    step = pl.program_id(0)
    slot = take_shard(weight_refs, buffer_ref, semaphores)

    @pl.when(step == 0)
    def _():
        total_ref[...] = jnp.zeros_like(total_ref)

    store_half(act_ref, out_back_ref, keep_ref, send_ref)
    total_ref[...] += dot_nn(act_ref[...], buffer_ref[slot])
    next_shard(weight_refs, buffer_ref, semaphores)

    @pl.when(step == pl.num_programs(0) - 1)
    def _():
        out_ref[...] = total_ref[...].astype(LOW)


def add_shards_kernel(*refs, count):
    operands, outs = refs[:count], refs[count:]
    total = operands[0][0].astype(WIDE)
    for operand in operands[1:]:
        total += operand[0].astype(WIDE)
    if len(outs) == 1:
        outs[0][0] = total.astype(outs[0].dtype)
        return
    half = pl.num_programs(1) // 2
    for place, out_ref in enumerate(outs):

        @pl.when(pl.program_id(1) // half == place)
        def _(out_ref=out_ref):
            out_ref[0] = total.astype(out_ref.dtype)


def add_shards(operands, start, count, kind, parts, name, after=()):
    _, rows, columns = operands[0].shape
    tile = rows // 2 if rows % 32 == 0 else rows
    steps = rows // tile
    parts = parts if steps % 2 == 0 else 1
    half = steps // parts
    block = pl.BlockSpec((1, tile, columns), lambda i, j: (start + i, j, 0))

    def out_block(place):
        last = half - 1
        return pl.BlockSpec(
            (1, tile, columns), lambda i, j: (i, jnp.clip(j - place * half, 0, last), 0)
        )

    return run(
        functools.partial(add_shards_kernel, count=len(operands)),
        [shaped((count, rows // parts, columns), kind)] * parts,
        (operands[0], *(loose(x) for x in operands[1:])),
        name,
        flops=0,
        grid=(count, steps),
        in_specs=[block] * len(operands),
        out_specs=[out_block(place) for place in range(parts)],
        after=after,
    )


def gather_shards(keep, send):
    operands = [keep, swap(send, "dp", 1)]
    size = keep.shape[0]
    while size > 2:
        half = size // 2
        gone = add_shards(operands, half, half, LOW, 1, "add_shards")
        operands.append(swap(gone[0], "dp", 2 * half))
        size = half
    gone = add_shards(operands, 1, 1, LOW, 1, "add_shards")
    return operands, [swap(part, "dp", 2) for part in gone], gone[0]


def finish_kernel(*refs, count, steps):
    former_refs, came_refs, (out_ref, mark_ref) = refs[:count], refs[count:-2], refs[-2:]
    total = former_refs[0][0].astype(WIDE)
    for former_ref in former_refs[1:]:
        total += former_ref[0].astype(WIDE)
    half = steps // len(came_refs)
    for place, came_ref in enumerate(came_refs):

        @pl.when(pl.program_id(0) // half == place)
        def _(came_ref=came_ref):
            out_ref[...] = total + came_ref[0].astype(WIDE)

    mark_ref[...] = jnp.zeros_like(mark_ref)


def finish_shards(formers, came):
    _, rows, columns = formers[0].shape
    tile = rows // 2 if rows % 32 == 0 else rows
    steps = rows // tile
    half = steps // len(came)
    block = pl.BlockSpec((1, tile, columns), lambda i: (0, i, 0))
    parts = [
        pl.BlockSpec(
            (1, tile, columns), lambda i, place=place: (0, jnp.clip(i - place * half, 0, half - 1), 0)
        )
        for place in range(len(came))
    ]
    return run(
        functools.partial(finish_kernel, count=len(formers), steps=steps),
        [shaped((rows, columns), WIDE), shaped((8, 128), WIDE)],
        (formers[0], *(loose(x) for x in (*formers[1:], *came))),
        "finish_shards",
        flops=0,
        grid=(steps,),
        in_specs=[block] * len(formers) + parts,
        out_specs=[pl.BlockSpec((tile, columns), lambda i: (i, 0)), fixed((8, 128))],
    )


def after_kernel(
    home_ref,
    place_ref,
    residual_ref,
    gain_ref,
    upstream_ref,
    weight_ref,
    att_back_ref,
    residual_back_ref,
    branch_ref,
    gain_back_ref,
):
    hot = hot_columns(place_ref[...], home_ref.shape[0])
    normed_back = dot_nn(hot, home_ref[...])
    residual = residual_ref[...]
    scale = lax.rsqrt(jnp.mean(residual * residual, axis=-1, keepdims=True) + EPSILON)
    spread = residual * scale
    gained = gain_ref[...].astype(WIDE) * normed_back
    inner = jnp.mean(gained * spread, axis=-1, keepdims=True)
    back = upstream_ref[...].astype(WIDE) + scale * (gained - spread * inner)
    residual_back_ref[...] = back
    branch = back.astype(LOW)
    branch_ref[...] = branch
    gain_back_ref[...] = jnp.broadcast_to(
        jnp.sum(normed_back * spread, axis=0, keepdims=True), gain_back_ref.shape
    )
    att_back_ref[...] = dot_nt(weight_ref[...], branch).astype(LOW)


def output_pieces_kernel(core_ref, att_ref, branch_ref, router_ref, gain_ref, *refs, owners):
    *out_refs, full_ref = refs
    grad = dot_nn(att_ref[...], branch_ref[...])
    own = grad.shape[0] // owners
    height = full_ref.shape[0] // owners
    full_ref[...] = jnp.zeros_like(full_ref)
    for owner in range(owners):
        full_ref[owner * height : owner * height + own, :] = grad[owner * own : (owner + 1) * own]
    at = own + router_ref.shape[0]
    full_ref[own:at, :] = router_ref[...]
    full_ref[at : at + 8, :] = gain_ref[...]
    for place, out_ref in enumerate(out_refs):
        height = out_ref.shape[0]
        start = pl.multiple_of(jnp.bitwise_xor(core_ref[0], place) * height, height)
        out_ref[...] = full_ref[pl.ds(start, height), :].astype(out_ref.dtype)


def is_cube():
    return [lax.axis_size(name) for name in ("head", "blk", "dp")] == [4, 2, 4]


def sums_kernel(me_ref, *refs, count):
    operands, outs = refs[: len(refs) - count], refs[len(refs) - count :]
    for place, out_ref in enumerate(outs):
        height = out_ref.shape[0]
        start = pl.multiple_of(jnp.bitwise_xor(me_ref[0], place) * height, height)
        total = operands[0][pl.ds(start, height), :].astype(WIDE)
        for operand in operands[1:]:
            total += operand[pl.ds(start, height), :].astype(WIDE)
        out_ref[...] = total.astype(out_ref.dtype)


def sums(me, operands, count, name, after=()):
    height, breadth = operands[0].shape
    return run(
        functools.partial(sums_kernel, count=count),
        [shaped((height // count, breadth), LOW)] * count,
        (me[None].astype(jnp.int32), operands[0], *(loose(x) for x in operands[1:])),
        name,
        flops=0,
        in_specs=[SMEM] + [VMEM] * len(operands),
        after=after,
    )


def cross(mine, other, name, after=()):
    spot = lax.axis_index("blk") * 2 + lax.axis_index("dp") // 2
    own, along, across, corner = sums(spot, (mine, swap(other, "dp", 1)), 4, name, after)
    diagonal = [(b * 4 + d, (1 - b) * 4 + (d ^ 2)) for b in range(2) for d in range(4)]
    return [
        own,
        swap(across, "blk", 1),
        swap(along, "dp", 2),
        lax.ppermute(corner, ("blk", "dp"), diagonal),
    ]


def output_pieces(att_tok, branch_back, router_back, gain_back):
    model_width, experts = branch_back.shape[1], router_back.shape[0]
    cube = is_cube()
    owners = 8 if cube else 1
    height = owners * -(-(model_width // owners + experts + 8) // 128) * 128
    dp = lax.axis_index("dp")
    count = 2 if cube else 1
    outs = run(
        functools.partial(output_pieces_kernel, owners=owners),
        [shaped((height // count, model_width), LOW if cube else WIDE)] * count,
        (
            ((dp & 1) * (count - 1)).astype(jnp.int32)[None],
            att_tok,
            branch_back,
            router_back,
            gain_back,
        ),
        "output_pieces",
        flops=2 * att_tok.size * model_width,
        in_specs=[SMEM] + [VMEM] * 4,
        scratch=[pltpu.VMEM((height, model_width), WIDE)],
    )
    if not cube:
        return (), (), lax.psum(outs[0], ("head", "blk", "dp"))
    own, *came = cross(*outs, "output_core")
    shares = sums(lax.axis_index("head"), (own, *came), 4, "output_sum")
    arrived = [shares[0]] + [swap(shares[step], "head", step) for step in range(1, 4)]
    return (own,), (shares[0],), arrived


def output_kernel(
    residual_ref, normed_ref, router_ref, chosen_ref, place_ref, slots_ref, out_ref, *, experts
):
    probs, lane = route(normed_ref[...], router_ref[...], experts)
    hot = (lane == chosen_ref[...]).astype(WIDE)
    gate = jnp.sum(probs * hot, axis=-1, keepdims=True)
    expert_out = dot_nn(hot_columns(place_ref[...], slots_ref.shape[0]), slots_ref[...])
    out_ref[...] = (residual_ref[...] + gate * expert_out).astype(LOW)


def tokens_grad_kernel(
    triples_ref,
    query_weight_ref,
    key_weight_ref,
    value_weight_ref,
    tokens_ref,
    gain_ref,
    residual_back_ref,
    out_ref,
):
    groups = triples_ref.shape[0]
    weight_refs = (query_weight_ref, key_weight_ref, value_weight_ref)
    normed_back = jnp.zeros(out_ref.shape[::-1], WIDE)
    for kind, weight_ref in enumerate(weight_refs):
        rows = jnp.concatenate([triples_ref[group, kind] for group in range(groups)], 0)
        normed_back += dot_nn(weight_ref[...], rows)
    normed_back = normed_back.T
    values = tokens_ref[...].astype(WIDE)
    scale = lax.rsqrt(jnp.mean(values * values, axis=-1, keepdims=True) + EPSILON)
    spread = values * scale
    gained = gain_ref[...].astype(WIDE) * normed_back
    inner = jnp.mean(gained * spread, axis=-1, keepdims=True)
    out_ref[...] = (residual_back_ref[...] + scale * (gained - spread * inner)).astype(LOW)


def bucket_sums(diagonal, bucket_row, buckets):
    breadth = bucket_row.shape[1]
    hot = lax.broadcasted_iota(jnp.int32, (buckets, breadth), 0) == bucket_row
    hot = hot.astype(WIDE).astype(LOW)
    high = diagonal.astype(LOW)
    rest = diagonal - high.astype(WIDE)
    middle = rest.astype(LOW)
    small = (rest - middle.astype(WIDE)).astype(LOW)
    return dot_nt(high, hot) + dot_nt(middle, hot) + dot_nt(small, hot)


def side(grads):
    return -(-3 * grads // 128) * 128


def blocks_of(refs):
    return [ref[place] for ref in refs for place in range(ref.shape[0])]


def projection_grads(turned_ref, query_refs, pairs_ref):
    _, width, tokens = query_refs[0].shape
    queries = blocks_of(query_refs)
    groups = len(queries)
    spare = jnp.zeros((side(width) - 3 * width, tokens), LOW)
    total = None
    for group in range(groups):
        rows = [queries[group], pairs_ref[group, 0], pairs_ref[group, 1], spare]
        part = dot_nt(turned_ref[group], jnp.concatenate(rows, 0))
        total = part if total is None else total + part
    return total


def table_sums(diagonal_refs, bucket_refs, buckets):
    table = bucket_sums(diagonal_refs[0][...], bucket_refs[0][...], buckets)
    for diagonal_ref, bucket_ref in zip(diagonal_refs[1:], bucket_refs[1:]):
        table += bucket_sums(diagonal_ref[...], bucket_ref[...], buckets)
    return table


def add_pairs(home_refs):
    total = home_refs[0][...].astype(WIDE)
    for home_ref in home_refs[1:]:
        total += home_ref[...].astype(WIDE)
    return total.astype(LOW)


def triples_kernel(*refs, parts):
    pairs = add_pairs(refs[parts:-1])
    for group, queries in enumerate(blocks_of(refs[:parts])):
        refs[-1][group, 0] = queries
        refs[-1][group, 1] = pairs[group, 0]
        refs[-1][group, 2] = pairs[group, 1]


def pieces_kernel(core_ref, turned_ref, *refs, parts, tiles, buckets):
    query_refs, refs = refs[:parts], refs[parts:]
    home_refs, refs = refs[:tiles], refs[tiles:]
    diagonal_refs, bucket_refs = refs[:tiles], refs[tiles : 2 * tiles]
    *out_refs, pairs_ref, full_ref = refs[2 * tiles :]
    width = query_refs[0].shape[1]
    pairs_ref[...] = add_pairs(home_refs)
    full_ref[...] = projection_grads(turned_ref, query_refs, pairs_ref)
    table = table_sums(diagonal_refs, bucket_refs, buckets)
    full_ref[0:8, 3 * width : 3 * width + buckets] = table
    for place, out_ref in enumerate(out_refs):
        height = out_ref.shape[0]
        start = pl.multiple_of(jnp.bitwise_xor(core_ref[0], place) * height, height)
        out_ref[...] = full_ref[pl.ds(start, height), :].astype(out_ref.dtype)


def join_kernel(*refs):
    *refs, out_ref = refs
    copies, halves, part, _ = out_ref.shape
    count = len(refs) // 2
    columns = refs[0].shape[1]
    total, packed = (
        functools.reduce(jnp.add, [ref[...].astype(WIDE) for ref in group])
        for group in (refs[:count], refs[count:])
    )
    height = packed.shape[0] // halves
    for half in range(halves):
        former = total[half * part : (half + 1) * part].astype(LOW)
        rows = packed[half * height : (half + 1) * height]
        blocks = [rows[:, at : at + 256] for at in range(0, rows.shape[1], 256)]
        latter = jnp.concatenate(blocks, 0).astype(LOW)
        for copy in range(copies):
            out_ref[copy, half, :, :columns] = former
            out_ref[copy, half, :, columns:] = latter


def share_kernel(spot_ref, cases, places, weight_refs, out_refs, sums_ref, table_ref, extra_ref, heads):
    step = pl.program_id(0)
    owner = jnp.bitwise_xor(spot_ref[0], places[0] if len(places) == 1 else place_at(step, places))
    part = out_refs[0].shape[0] // 2
    width = heads * HEAD_DIM
    columns = side(width)
    buckets = table_ref.shape[2]
    for case, pair in enumerate(cases):

        @pl.when(step == case)
        def _(pair=pair):
            for half in range(2):
                ref = pair[half]
                groups = ref.shape[0]
                at = half if ref.shape[1] == 2 else 0
                rows = slice(half * part, (half + 1) * part)

                def tile(group, place, ref=ref, at=at):
                    return ref[group, at, :, place * 128 : (place + 1) * 128].astype(WIDE)

                def turned(group, place, tile=tile):
                    return pltpu.roll(tile(group, place), 64, 1)

                lower = lax.broadcasted_iota(jnp.int32, (part, 128), 1) < 64
                for one in range(0, groups, 2):
                    two = one + 1
                    for kind in range(3):
                        if kind == 1:
                            middle = turned(one, 2)
                            parts = (
                                jnp.where(lower, turned(one, 1), middle),
                                jnp.where(lower, middle, tile(two, 1)),
                                tile(two, 2),
                            )
                        else:
                            place = 3 * kind // 2
                            first = turned(two, place)
                            parts = (
                                tile(one, place),
                                jnp.where(lower, tile(one, place + 1), first),
                                jnp.where(lower, first, turned(two, place + 1)),
                            )
                        for number, values in enumerate(parts):
                            lane = one * width + number * 128
                            out_refs[kind][rows, lane : lane + 128] = values
                for group in range(groups):
                    packed = ref[group, at, :, columns:].astype(WIDE)
                    start = group * 32 + half * 16
                    for number in range(part // 16):
                        lane = number * 256
                        values = packed[number * 16 : (number + 1) * 16]
                        if group + 1 < groups:
                            out_refs[3][start : start + 16, lane : lane + 256] = values
                        else:

                            @pl.when(owner == 0)
                            def _(values=values, half=half, lane=lane):
                                extra_ref[half * 16 : half * 16 + 16, lane : lane + 256] = values

                    if half == 0:

                        @pl.when(owner == 0)
                        def _(group=group, tile=tile):
                            table_ref[group] = tile(group, 4)[:8, 64 : 64 + buckets]

    shares = jnp.zeros((2 * part, 1), WIDE)
    for kind in range(3):
        shares += jnp.sum(
            out_refs[kind][...] * weight_refs[kind][...].astype(WIDE), axis=1, keepdims=True
        )
    shares = jnp.broadcast_to(shares, (2 * part, 128))
    if sums_ref.shape[0] == 2 * part:
        sums_ref[...] = shares
    else:
        sums_ref[pl.ds(owner * 2 * part, 2 * part), :] = shares


def place_at(step, places):
    return sum(jnp.where(step == at, place, 0) for at, place in enumerate(places))


FIRST_PLACES, LAST_PLACES = (0, 1, 2, 4, 5, 6), (3, 7)


def first_shares_kernel(spot_ref, *refs, heads):
    piece_refs, weight_refs, refs = refs[:6], refs[6:9], refs[9:]
    out_refs, (sums_ref, table_ref, extra_ref) = refs[:4], refs[4:]

    @pl.when(pl.program_id(0) == 0)
    def _():
        table_ref[...] = jnp.zeros_like(table_ref)
        extra_ref[...] = jnp.zeros_like(extra_ref)

    cases = [(ref, ref) for ref in piece_refs]
    share_kernel(
        spot_ref, cases, FIRST_PLACES, weight_refs, out_refs, sums_ref, table_ref, extra_ref, heads
    )


def last_shares_kernel(spot_ref, *refs, heads, experts):
    piece_refs, weight_refs, refs = refs[:4], refs[4:7], refs[7:]
    gain_ref, sums_in, table_in, extra_in, *refs = refs
    out_refs, refs = refs[4:8], refs[8:]
    gain_out, second_out, table_out, router_out, sums_ref, table_ref, extra_ref = refs
    step = pl.program_id(0)

    @pl.when(step == 0)
    def _():
        sums_ref[...] = sums_in[...]
        table_ref[...] = table_in[...]
        extra_ref[...] = extra_in[...]

    cases = [(piece_refs[0], piece_refs[1]), (piece_refs[2], piece_refs[3])]
    share_kernel(
        spot_ref, cases, LAST_PLACES, weight_refs, out_refs, sums_ref, table_ref, extra_ref, heads
    )

    @pl.when(step == pl.num_programs(0) - 1)
    def _():
        first = sums_ref[...].T[0:8] / gain_ref[...].astype(WIDE)
        second = extra_ref[experts : experts + 8, :]
        for lane in range(gain_out.shape[0]):
            gain_out[lane : lane + 1, :] = first[0:1, lane * 128 : (lane + 1) * 128]
            second_out[lane : lane + 1, :] = second[0:1, lane * 128 : (lane + 1) * 128]
        router_out[...] = extra_ref[:experts, :]
        for group in range(table_ref.shape[0]):
            table_out[group * heads : (group + 1) * heads, :] = table_ref[group][:heads]


def put_together(me, first, corners, weights, gain, heads, buckets, experts):
    model_width = weights[0].shape[0]
    groups, _, part, _ = first[0].shape

    def rows(places, breadth):
        return pl.BlockSpec(
            (2 * part, breadth), lambda i, me: (place_at(i, places) ^ me[0], 0)
        )

    square = shaped((model_width, model_width), WIDE)
    kept_shapes = [(groups, 8, buckets), (32, model_width)]
    *grads, sums, table, extra = run_with_scalar(
        functools.partial(first_shares_kernel, heads=heads),
        me,
        [square] * 4 + [shaped((model_width, 128), WIDE)] + [shaped(x, WIDE) for x in kept_shapes],
        (*(loose(x) for x in first), *weights),
        "first_shares",
        grid=(len(FIRST_PLACES),),
        in_specs=[fixed(x.shape) for x in first] + [rows(FIRST_PLACES, model_width)] * 3,
        out_specs=[rows(FIRST_PLACES, model_width)] * 4
        + [rows(FIRST_PLACES, 128)]
        + [fixed(x) for x in kept_shapes],
    )
    corners = [gate(array, (table,)) for array in corners]
    last = (*corners, *(swap(array, "dp", 1) for array in corners))
    operands = (*(loose(x) for x in last), *weights, gain, sums, table, extra, *grads)
    vectors = [(model_width // 128, 128)] * 2 + [(groups * heads, buckets), (experts, model_width)]
    count = len(last)
    *grads, shares, second, table, router = run_with_scalar(
        functools.partial(last_shares_kernel, heads=heads, experts=experts),
        me,
        [square] * 4 + [shaped(x, WIDE) for x in vectors],
        operands,
        "last_shares",
        grid=(len(LAST_PLACES),),
        in_specs=[fixed(x.shape) for x in last]
        + [rows(LAST_PLACES, model_width)] * 3
        + [fixed(x.shape) for x in operands[count + 3 : count + 7]]
        + [pl.BlockSpec(memory_space=pltpu.HBM)] * 4,
        out_specs=[rows(LAST_PLACES, model_width)] * 4 + [fixed(x) for x in vectors],
        scratch=[pltpu.VMEM((model_width, 128), WIDE)] + [pltpu.VMEM(x, WIDE) for x in kept_shapes],
        aliases={count + 8 + i: i for i in range(4)},
    )
    query_grad, key_grad, value_grad, output_grad = grads
    return (
        query_grad,
        key_grad,
        value_grad,
        shares.reshape(-1),
        table.T,
        output_grad,
        router.T,
        second.reshape(-1),
    )


def take_half_kernel(values_ref, out_ref):
    out_ref[...] = values_ref[...]


def take_half(values, half):
    groups, _, *rest = values.shape
    return pl.pallas_call(
        take_half_kernel,
        out_shape=pltpu.HBM((groups, 1, *rest), values.dtype),
        grid=(groups,),
        in_specs=[pl.BlockSpec((1, 1, *rest), lambda i: (i, half, 0, 0))],
        out_specs=pl.BlockSpec((1, 1, *rest), lambda i: (i, 0, 0, 0)),
        compiler_params=pltpu.CompilerParams(vmem_limit_bytes=VMEM_BYTES),
        name="take_half",
    )(values)


def weight_sums(
    turned, query_backs, home, diagonals, bucket_rows, buckets, weights, gain, experts, packed, middle, late
):
    groups, model_width, _ = turned.shape
    width = query_backs[0].shape[1]
    heads = width // HEAD_DIM
    tiles = len(diagonals)
    cube = is_cube()
    columns = side(width)
    dp, blk = lax.axis_index("dp"), lax.axis_index("blk")
    count = 2 if cube else 1
    pieces = run(
        functools.partial(pieces_kernel, parts=len(query_backs), tiles=tiles, buckets=buckets),
        [shaped((model_width // count, columns), LOW if cube else WIDE)] * count,
        (
            ((dp & 1) * (count - 1)).astype(jnp.int32)[None],
            near(turned),
            *query_backs,
            *received_loose(home),
            *diagonals,
            *bucket_rows,
        ),
        "projection_pieces",
        flops=6 * turned.size * width,
        in_specs=[SMEM] + [VMEM] * (1 + len(query_backs) + 3 * tiles),
        scratch=[pltpu.VMEM(home[0].shape, LOW), pltpu.VMEM((model_width, columns), WIDE)],
    )
    if not cube:
        sums = lax.psum(pieces[0], ("blk", "dp"))
        table = lax.all_gather(
            sums[:heads, 3 * width : 3 * width + buckets], "head", axis=0, tiled=True
        )
        grads = sums[:, : 3 * width].reshape(model_width, 3, width)
        grads = lax.all_gather(grads, "head", axis=2, tiled=True)
        grads = [grads[:, i] for i in range(3)]
        shares = sum(jnp.sum(x * y.astype(WIDE), axis=1) for x, y in zip(grads, weights))
        rest = packed[model_width:]
        shares = shares / gain[0].astype(WIDE)
        packed = packed[:model_width], rest[:experts].T, rest[experts]
        return pieces, *grads, shares, table.T, *packed
    part = model_width // 16
    copies = run(
        join_kernel,
        [shaped((groups, 2, part, columns + 256), LOW)],
        tuple(loose(x) for x in (*cross(*pieces, "projection_core", middle), *packed)),
        "join",
        flops=0,
        after=late,
    )[0]
    own = blocks_over(copies, "head")
    across, along = swap(own, "blk", 1), swap(own, "dp", 2)
    corners = (
        swap(take_half(across, 0), "dp", 2),
        swap(take_half(along, 1), "blk", 1),
    )
    near_ones = (own, along, across)
    first = (*near_ones, *(swap(array, "dp", 1) for array in near_ones))
    me = ((dp & 1) * 4 + blk * 2 + dp // 2).astype(jnp.int32)[None]
    return pieces, *put_together(me, first, corners, weights, gain, heads, buckets, experts)


def body(
    tokens,
    first_gain,
    query_weight,
    key_weight,
    value_weight,
    output_weight,
    bias_table,
    second_gain,
    router_weight,
    inner_weight,
    outer_weight,
    expert_index,
    capacity_slot,
    bucket_of_offset,
    upstream,
):
    _, token_rows, model_width = tokens.shape
    groups = lax.axis_size("head")
    cycle = lax.axis_size("blk")
    shares = lax.axis_size("dp")
    width = model_width // groups
    heads = width // HEAD_DIM
    local_rows = groups * token_rows
    length = local_rows * cycle
    buckets = bias_table.shape[0]
    experts = router_weight.shape[1]
    capacity = max(2, 2 * token_rows // experts)
    slots = experts * capacity
    token_values, upstream_values = tokens[0], upstream[0]
    gain_one, gain_two = first_gain[None], second_gain[None]
    chosen = expert_index[0]
    place = chosen * capacity + capacity_slot[0]
    place_row, place_column, chosen_column = place[None], place[:, None], chosen[:, None]
    router = jnp.pad(router_weight, ((0, 0), (0, 128 - experts)))

    inner_shards, outer_shards = [inner_weight[0]], [outer_weight[0]]
    for held in (outer_shards, inner_shards):
        for bit in range(1, shares.bit_length() - 1):
            held += [swap(values, "dp", 1 << bit) for values in held]
    far_inner, far_outer = inner_shards[1:], outer_shards[1:]
    for held in (outer_shards, inner_shards):
        held[:] = [x for values in held for x in (values, swap(values, "dp", 1))]

    square = model_width * model_width
    pairs, normed_one = run(
        project_pairs_kernel,
        [
            shaped((groups, 2, width, token_rows), LOW),
            shaped((token_rows, model_width), LOW),
        ],
        (token_values, gain_one, key_weight, value_weight),
        "project_pairs",
        flops=4 * token_rows * square,
    )
    pairs = blocks_over(pairs, "head")
    head_start = (lax.axis_index("head") * heads).astype(jnp.int32)[None]
    table_rows = jnp.pad(bias_table.T, ((0, -(groups * heads) % 8), (0, 0)))
    bucket_line = jnp.pad(bucket_of_offset, (0, 1))[None]
    blk = lax.axis_index("blk")
    tile_buckets, tile_strips = [], []
    for step in range(cycle):
        number = lax.rem(blk + cycle - step, cycle)
        start = length + (number - blk - 1) * local_rows
        tile_buckets.append(lax.dynamic_slice_in_dim(bucket_line, start, 2 * local_rows, 1))
    tile_pairs = [pairs] + [turn(pairs, "blk", step) for step in range(1, cycle)]
    up_slots = run(
        scatter_kernel,
        [shaped((slots, model_width), LOW)],
        (place_row, upstream_values),
        "scatter_up",
        flops=2 * slots * token_rows * model_width,
        after=(normed_one,),
    )[0]
    turned = run(
        turn_kernel,
        [shaped((groups, model_width, token_rows), LOW)],
        (normed_one,),
        "turn",
        flops=0,
    )[0]
    queries = run(
        project_queries_kernel,
        [shaped((groups, width, token_rows), LOW)],
        (normed_one, query_weight),
        "project_queries",
        flops=2 * token_rows * square,
        after=(pairs, up_slots, turned),
    )[0]
    queries = blocks_over(queries, "head")
    up_rows = blocks_over(up_slots, ("head", "blk"))
    for step in range(0, cycle, 2):
        tile_strips += make_strips(
            head_start, table_rows, tile_buckets[step : step + 2], heads, (queries,)
        )
    tile_weights, before = [], ()
    for step in range(0, cycle, 2):
        tiles = slice(step, step + 2)
        last = step + 2 >= cycle
        results = attend(queries, tile_pairs[tiles], tile_strips[tiles], before, last)
        tile_weights += results[: len(tile_pairs[tiles])]
        total, attended, *rest = results[len(tile_pairs[tiles]) :]
        before = (attended, total)
    attended_low = gate(rest[0], (loose(up_rows),))
    att_tok = blocks_over(attended_low, "head").reshape(model_width, token_rows)
    hidden = inner_shards[0].shape[1]
    full_hidden = shares * hidden
    product = 2 * slots * model_width * full_hidden
    hidden_block = pl.BlockSpec((slots, hidden), lambda i: (0, i))
    turned_block = pl.BlockSpec((slots, hidden), lambda i: (0, shard_at(i, shares)))
    raw = run(
        raw_back_kernel,
        [shaped((slots, full_hidden), LOW)],
        (near(up_rows), *outer_shards),
        "raw_back",
        flops=product,
        grid=(shares,),
        in_specs=[fixed(up_rows.shape)] + shard_places(outer_shards),
        out_specs=[hidden_block],
        scratch=shard_scratch(outer_shards),
    )[0]
    residual_mid, normed_two, normed_slots = run(
        middle_kernel,
        [
            shaped((token_rows, model_width), WIDE),
            shaped((token_rows, model_width), LOW),
            shaped((slots, model_width), LOW),
        ],
        (near(att_tok), token_values, output_weight, gain_two, place_row),
        "middle",
        flops=2 * token_rows * square + 2 * slots * token_rows * model_width,
        after=(raw, router, *far_inner),
    )
    expert_rows = blocks_over(normed_slots, ("head", "blk"))
    own_expert = (lax.axis_index("head") * cycle + blk).astype(jnp.int32)[None]
    hidden_act, pre_back, home_slots, out_back, logit_back = run(
        functools.partial(expert_kernel, experts=experts),
        [
            shaped((slots, full_hidden), LOW),
            shaped((slots, full_hidden), LOW),
            shaped((slots, model_width), LOW),
            shaped((slots, model_width), LOW),
            shaped((slots, 128), LOW),
        ],
        (own_expert, near(expert_rows), near(up_rows), router, raw, *inner_shards),
        "expert",
        flops=2 * product,
        grid=(shares,),
        in_specs=[
            SMEM,
            fixed(expert_rows.shape),
            fixed(up_rows.shape),
            fixed(router.shape),
            hidden_block,
            *shard_places(inner_shards),
        ],
        out_specs=[
            hidden_block,
            hidden_block,
            fixed((slots, model_width)),
            fixed((slots, model_width)),
            fixed((slots, 128)),
        ],
        scratch=[
            pltpu.VMEM((slots, model_width), WIDE),
            pltpu.VMEM((slots, 128), WIDE),
            pltpu.VMEM((slots, 128), WIDE),
            *shard_scratch(inner_shards),
        ],
    )
    home_rows = blocks_over(home_slots, ("head", "blk"))
    inner_shape, outer_shape = (model_width, hidden), (hidden, model_width)
    inner_keep, inner_send, router_back = run(
        inner_grads_kernel,
        [shaped((shares // 2, *inner_shape), LOW)] * 2 + [shaped((experts, model_width), WIDE)],
        (near(expert_rows), pre_back, logit_back),
        "inner_grads",
        flops=product,
        grid=(shares,),
        in_specs=[fixed(expert_rows.shape), turned_block, fixed(logit_back.shape)],
        out_specs=[
            keep_spec(inner_shape, shares),
            send_spec(inner_shape, shares),
            fixed((experts, model_width)),
        ],
    )
    turned_shards = outer_shards[1::2] + outer_shards[0::2]
    outer_keep, outer_send, expert_out = run(
        outer_grads_kernel,
        [shaped((shares // 2, *outer_shape), LOW)] * 2 + [shaped((slots, model_width), LOW)],
        (hidden_act, out_back, *turned_shards),
        "outer_grads",
        flops=2 * product,
        grid=(shares,),
        in_specs=[turned_block, fixed(out_back.shape)] + shard_places(outer_shards),
        out_specs=[
            keep_spec(outer_shape, shares),
            send_spec(outer_shape, shares),
            fixed((slots, model_width)),
        ],
        scratch=[pltpu.VMEM((slots, model_width), WIDE)] + shard_scratch(outer_shards),
    )
    att_back, residual_back, branch_back, gain_back = run(
        after_kernel,
        [
            shaped((model_width, token_rows), LOW),
            shaped((token_rows, model_width), WIDE),
            shaped((token_rows, model_width), LOW),
            shaped((8, model_width), WIDE),
        ],
        (near(home_rows), place_column, residual_mid, gain_two, upstream_values, output_weight),
        "after",
        flops=2 * token_rows * square + 2 * slots * token_rows * model_width,
        after=(router_back, expert_out),
    )
    head_back = blocks_over(att_back.reshape(groups, width, token_rows), "head")
    packed_core, packed_sum, packed_shares = output_pieces(
        att_tok, branch_back, router_back, gain_back
    )
    *inner_parts, inner_gone = gather_shards(inner_keep, gate(inner_send, (att_back,)))
    *outer_parts, outer_gone = gather_shards(outer_keep, gate(outer_send, (att_back,)))
    turned = gate(turned, (head_back, *packed_core, inner_gone, outer_gone))
    turned_all = blocks_over(turned, "head")

    before, diagonals, home, query_backs = (), [], [], []
    for step in range(1, cycle):
        query_back, pairs_part, diagonal = attend_back(
            queries,
            head_back,
            attended,
            total,
            tile_weights[step],
            tile_pairs[step],
            before,
            False,
            0,
            groups,
            (),
        )
        before = (query_back,)
        diagonals.append(diagonal)
        home.append(turn(pairs_part, "blk", cycle - step))
    cut = groups - 1
    for begin, count, after in (
        (0, cut, packed_sum),
        (cut, groups - cut, tuple(loose(x) for x in (turned_all, *home[:1], *inner_parts[1]))),
    ):
        query_back, pairs_part, diagonal = attend_back(
            queries,
            head_back,
            attended,
            total,
            tile_weights[0],
            tile_pairs[0],
            before,
            True,
            begin,
            count,
            after,
        )
        query_backs.append(query_back)
        if begin == 0:
            out_rows = blocks_over(gate(expert_out, (loose(turned_all), query_back)), ("head", "blk"))
        diagonals.append(diagonal)
        home.append(pairs_part)
    diagonal_buckets = [*tile_buckets[1:], tile_buckets[0], tile_buckets[0]]
    layer_output = run(
        functools.partial(output_kernel, experts=experts),
        [shaped((token_rows, model_width), LOW)],
        (residual_mid, normed_two, router, chosen_column, place_column, loose(out_rows)),
        "layer_output",
        flops=2 * slots * token_rows * model_width,
    )[0]
    (
        pieces,
        query_grad,
        key_grad,
        value_grad,
        first_gain_grad,
        table_grad,
        output_grad,
        router_grad,
        second_gain_grad,
    ) = weight_sums(
        turned_all,
        query_backs,
        home,
        diagonals,
        diagonal_buckets,
        buckets,
        (query_weight, key_weight, value_weight),
        gain_one,
        experts,
        packed_shares,
        (loose(out_rows),),
        (*(loose(x) for x in outer_parts[1]), layer_output),
    )
    inner_part, inner_mark = finish_shards(*inner_parts)
    outer_part, outer_mark = finish_shards(*outer_parts)
    triples = run(
        functools.partial(triples_kernel, parts=len(query_backs)),
        [shaped((groups, 3, width, token_rows), LOW)],
        (*query_backs, *received_loose(home)),
        "triples",
        flops=0,
        after=(pieces[0], inner_mark, outer_mark),
    )[0]
    triples_tok = blocks_over(triples, "head")
    tokens_grad = run(
        tokens_grad_kernel,
        [shaped((token_rows, model_width), LOW)],
        (
            loose(triples_tok),
            query_weight,
            key_weight,
            value_weight,
            token_values,
            gain_one,
            residual_back,
        ),
        "tokens_grad",
        flops=6 * token_rows * square,
    )[0]
    return (
        layer_output[None],
        tokens_grad[None],
        first_gain_grad,
        query_grad,
        key_grad,
        value_grad,
        output_grad,
        table_grad,
        second_gain_grad,
        router_grad,
        inner_part[None],
        outer_part[None],
    )


def solution(mesh):
    return jax.shard_map(
        body,
        mesh=mesh,
        in_specs=(
            P("dp", ("blk", "head"), None),
            P(),
            P(),
            P(),
            P(),
            P(),
            P(),
            P(),
            P(),
            P(("head", "blk"), None, "dp"),
            P(("head", "blk"), "dp", None),
            P("dp", ("blk", "head")),
            P("dp", ("blk", "head")),
            P(),
            P("dp", ("blk", "head"), None),
        ),
        out_specs=(
            P("dp", ("blk", "head"), None),
            P("dp", ("blk", "head"), None),
            P(),
            P(),
            P(),
            P(),
            P(),
            P(),
            P(),
            P(),
            P(("head", "blk"), None, "dp"),
            P(("head", "blk"), "dp", None),
        ),
        check_vma=False,
    )
```

```python
import functools
import math

import jax
import jax.numpy as jnp
from jax import lax
from jax.experimental import pallas as pl
from jax.experimental.pallas import tpu as pltpu
from jax.sharding import PartitionSpec as P

HEAD_DIM = 64
EPSILON = 1e-06
STRIP = 128
VMEM_BYTES = 28 * 2**20
LOW = jnp.bfloat16
WIDE = jnp.float32


def dot_nt(former, latter):
    return lax.dot_general(former, latter, (((1,), (1,)), ((), ())), preferred_element_type=WIDE)


def dot_nn(former, latter):
    return lax.dot_general(former, latter, (((1,), (0,)), ((), ())), preferred_element_type=WIDE)


def dot_tn(former, latter):
    return lax.dot_general(former, latter, (((0,), (0,)), ((), ())), preferred_element_type=WIDE)


def shaped(shape, kind):
    return pltpu.HBM(tuple(shape), kind)


def kept(shape, kind):
    return pltpu.VMEM(tuple(shape), kind)


class Near:
    def __init__(self, values):
        self.values, self.shape, self.dtype = values, values.shape, values.dtype


def near(values):
    return Near(values)


class Loose(Near):
    pass


def loose(values):
    return Loose(values)


def fixed(shape):
    return pl.BlockSpec(tuple(shape), lambda *_: (0,) * len(shape), pipeline_mode=pl.Buffered(1))


def received_loose(home):
    return [loose(x) if x.dtype == LOW else x for x in home]


def placed(values):
    if isinstance(values, Loose):
        return values.values
    if isinstance(values, Near):
        return pltpu.with_memory_space_constraint(values.values, pltpu.VMEM)
    return pltpu.with_memory_space_constraint(values, pltpu.HBM)


def unread(values):
    return pl.BlockSpec(memory_space=pl.ANY if isinstance(values, Loose) else pltpu.HBM)


def run(
    kernel, outs, operands, name, flops, grid=None, in_specs=None, out_specs=None, scratch=(), after=()
):
    moved = sum(math.prod(x.shape) * jnp.dtype(x.dtype).itemsize for x in (*operands, *outs))
    count, skipped = len(operands), len(after)
    if grid is None:
        grid = (1,)
        out_specs = [fixed(x.shape) for x in outs]
    if in_specs is None:
        in_specs = [VMEM] * count
    in_specs = [fixed(x.shape) if spec is VMEM else spec for x, spec in zip(operands, in_specs)]

    def body(*refs):
        kernel(*refs[:count], *refs[count + skipped :])

    return pl.pallas_call(
        body,
        out_shape=list(outs),
        grid=grid,
        in_specs=in_specs + [unread(x) for x in after],
        out_specs=out_specs,
        scratch_shapes=list(scratch),
        compiler_params=pltpu.CompilerParams(vmem_limit_bytes=VMEM_BYTES),
        cost_estimate=pl.CostEstimate(flops=flops, bytes_accessed=moved, transcendentals=0),
        name=name,
    )(
        *(x if spec is SMEM else placed(x) for x, spec in zip(operands, in_specs)),
        *(placed(x) for x in after),
    )


def run_with_scalar(
    kernel, scalar, outs, operands, name, grid, in_specs, out_specs, scratch=(), aliases=None
):
    return pl.pallas_call(
        kernel,
        out_shape=list(outs),
        grid_spec=pltpu.PrefetchScalarGridSpec(
            num_scalar_prefetch=1,
            grid=grid,
            in_specs=in_specs,
            out_specs=out_specs,
            scratch_shapes=list(scratch),
        ),
        compiler_params=pltpu.CompilerParams(vmem_limit_bytes=VMEM_BYTES),
        input_output_aliases=aliases or {},
        name=name,
    )(scalar, *(placed(x) for x in operands))


SMEM = pl.BlockSpec(memory_space=pltpu.SMEM)
VMEM = pl.BlockSpec(memory_space=pltpu.VMEM)


def swap(values, axis, bit):
    return lax.ppermute(values, axis, [(i, i ^ bit) for i in range(lax.axis_size(axis))])


def turn(values, axis, step):
    size = lax.axis_size(axis)
    return lax.ppermute(values, axis, [(i, (i + step) % size) for i in range(size)])


def blocks_over(values, axis):
    return lax.all_to_all(values, axis, split_axis=0, concat_axis=0, tiled=True)


def row_of(ref):
    values = ref[...].astype(WIDE)
    return jnp.concatenate([values[at : at + 1] for at in range(values.shape[0])], 1)


def project_pairs_kernel(tokens_ref, gain_ref, key_ref, value_ref, pairs_ref, normed_ref):
    values = tokens_ref[...].astype(WIDE)
    scale = lax.rsqrt(jnp.mean(values * values, axis=-1, keepdims=True) + EPSILON)
    normed = (values * scale * row_of(gain_ref)).astype(LOW)
    normed_ref[...] = normed
    groups, _, width, _ = pairs_ref.shape
    for kind, weight_ref in enumerate((key_ref, value_ref)):
        rows = dot_nn(normed, weight_ref[...]).T
        for group in range(groups):
            pairs_ref[group, kind] = rows[group * width : (group + 1) * width].astype(LOW)


def project_queries_kernel(normed_ref, weight_ref, out_ref):
    rows = dot_nn(normed_ref[...], weight_ref[...]).T
    groups, width, _ = out_ref.shape
    for group in range(groups):
        out_ref[group] = rows[group * width : (group + 1) * width].astype(LOW)


def turn_kernel(normed_ref, out_ref):
    turned = normed_ref[...].astype(WIDE).T.astype(LOW)
    for copy in range(out_ref.shape[0]):
        out_ref[copy] = turned


def strips_kernel(start_ref, table_ref, *refs):
    tiles = (len(refs) - 1) // 2
    bucket_refs, strips_refs, rows_ref = refs[:tiles], refs[tiles : 2 * tiles], refs[-1]
    buckets = table_ref.shape[1]
    for bucket_ref, strips_ref in zip(bucket_refs, strips_refs):
        heads, _, span = strips_ref.shape
        breadth = bucket_ref.shape[1]
        hot = lax.broadcasted_iota(jnp.int32, (buckets, breadth), 0) == bucket_ref[...]
        rows_ref[...] = dot_nn(table_ref[...], hot.astype(WIDE).astype(LOW))
        for head in range(heads):
            row = rows_ref[pl.ds(start_ref[0] + head, 1), :]
            spread = jnp.broadcast_to(row, (STRIP, breadth))
            turned = pltpu.roll(spread, breadth - (STRIP - 1), 1, stride=1, stride_axis=0)
            strips_ref[head] = turned[:, :span]


def make_strips(head_start, table_rows, buckets, heads, after):
    breadth = buckets[0].shape[1]
    return run(
        strips_kernel,
        [kept((heads, STRIP, breadth - STRIP), WIDE)] * len(buckets),
        (head_start, table_rows, *buckets),
        "bias_strips",
        flops=2 * 12 * 32 * breadth,
        in_specs=[SMEM] + [VMEM] * (1 + len(buckets)),
        scratch=[pltpu.VMEM((table_rows.shape[0], breadth), WIDE)],
        after=after,
    )


def head_mask(shape, head):
    lane = lax.broadcasted_iota(jnp.int32, shape, 1)
    return (lane >= head * HEAD_DIM) & (lane < (head + 1) * HEAD_DIM)


def side_by_side(pairs_ref, kind):
    return jnp.concatenate([pairs_ref[group, kind] for group in range(pairs_ref.shape[0])], 1)


def attend_kernel(*refs, heads, rows, tiles, first, last):
    query_ref = refs[0]
    pairs_refs, strips_refs, refs = refs[1 : 1 + tiles], refs[1 + tiles : 1 + 2 * tiles], refs[1 + 2 * tiles :]
    if not first:
        numer_in, total_in = refs[:2]
        refs = refs[2:]
    weight_refs, (total_ref, out_ref) = refs[:tiles], refs[tiles : tiles + 2]
    tile = query_ref.shape[2]
    groups = pairs_refs[0].shape[0]
    step = pl.program_id(0)
    queries = (query_ref[0] * jnp.asarray(0.125, LOW)).astype(WIDE).T.astype(LOW)
    out = jnp.zeros(queries.shape, WIDE)
    sums = jnp.zeros(queries.shape, WIDE)
    for head in range(heads):
        mask = head_mask(queries.shape, head)
        masked = jnp.where(mask, queries, jnp.zeros_like(queries))
        lanes = jnp.zeros((tile, 128), WIDE)
        numerator = jnp.zeros(queries.shape, WIDE)
        for pairs_ref, strips_ref, weight_ref in zip(pairs_refs, strips_refs, weight_refs):
            keys = jnp.concatenate([pairs_ref[group, 0] for group in range(groups)], 1)
            values = jnp.concatenate([pairs_ref[group, 1] for group in range(groups)], 1)
            scores = dot_nn(masked, keys)
            parts = []
            for sub in range(tile // STRIP):
                start = pl.multiple_of(rows - STRIP - (step * tile + sub * STRIP), STRIP)
                parts.append(
                    jnp.exp(
                        scores[sub * STRIP : (sub + 1) * STRIP, :]
                        + strips_ref[head, :, pl.ds(start, rows)]
                    )
                )
            weights = jnp.concatenate(parts, 0)
            for lane in range(rows // 128):
                lanes = lanes + weights[:, lane * 128 : (lane + 1) * 128]
            low = weights.astype(LOW)
            weight_ref[head] = low
            numerator = numerator + dot_nt(low, values)
        total = jnp.sum(lanes, axis=1, keepdims=True)
        out = jnp.where(mask, numerator, out)
        sums = jnp.where(mask, total, sums)
    out, sums = out.T, sums.T
    if not first:
        out = out + numer_in[0]
        sums = sums + total_in[0]
    total_ref[0] = sums
    if last:
        out = out / sums
        refs[-1][0] = out.astype(LOW)
    out_ref[0] = out


def gate(values, after):
    return pl.pallas_call(
        lambda *refs: None,
        out_shape=jax.ShapeDtypeStruct(values.shape, values.dtype),
        in_specs=[pl.BlockSpec(memory_space=pl.ANY)] + [unread(x) for x in after],
        out_specs=pl.BlockSpec(memory_space=pl.ANY),
        input_output_aliases={0: 0},
        name="gate",
    )(values, *(placed(x) for x in after))


def attend(queries, pairs, strips, before, last):
    groups, width, tile = queries.shape
    rows = groups * tile
    heads = width // HEAD_DIM
    tiles = len(pairs)
    block = pl.BlockSpec((1, width, tile), lambda i: (i, 0, 0))
    weight_block = pl.BlockSpec((heads, tile, rows), lambda i: (0, i, 0))
    operands = (queries, *(loose(x) for x in pairs), *(near(x) for x in strips), *before)
    return run(
        functools.partial(attend_kernel, heads=heads, rows=rows, tiles=tiles, first=not before, last=last),
        [shaped((heads, rows, rows), LOW)] * tiles
        + [shaped(queries.shape, WIDE)] * 2
        + [shaped(queries.shape, LOW)] * last,
        operands,
        "attend",
        flops=16 * width * rows * rows * tiles,
        grid=(groups,),
        in_specs=[block]
        + [fixed(x.shape) for x in pairs]
        + [fixed(x.shape) for x in strips]
        + [block] * len(before),
        out_specs=[weight_block] * tiles + [block] * (2 + last),
    )


def attend_back_kernel(*refs, heads, rows, first, last, begin):
    query_ref, grad_ref, att_ref, total_ref, weight_ref, pairs_ref = refs[:6]
    refs = refs[6:]
    if not first:
        query_in = refs[0]
        refs = refs[1:]
    query_back_ref, pairs_back_ref, diagonal_ref, strips_ref, key_acc, value_acc = refs
    tile = query_ref.shape[2]
    groups, _, width, chunk = pairs_back_ref.shape
    span = strips_ref.shape[2]
    step = pl.program_id(0)
    block = step + begin

    @pl.when(step == 0)
    def _():
        strips_ref[...] = jnp.zeros_like(strips_ref)
        key_acc[...] = jnp.zeros_like(key_acc)
        value_acc[...] = jnp.zeros_like(value_acc)

    query_turned = query_ref[0] * jnp.asarray(0.125, LOW)
    grads = grad_ref[0].astype(WIDE)
    inverse = 1.0 / total_ref[0]
    numer_wide = grads * inverse
    numer_turned = numer_wide.astype(LOW)
    products = -(numer_wide * att_ref[0]).T
    numer_back = numer_turned.astype(WIDE).T.astype(LOW)
    out = jnp.zeros(numer_back.shape, WIDE)
    keys = side_by_side(pairs_ref, 0)
    values = side_by_side(pairs_ref, 1)
    for head in range(heads):
        mask = head_mask(numer_back.shape, head)
        masked = jnp.where(mask, numer_back, jnp.zeros_like(numer_back))
        denom_back = jnp.sum(jnp.where(mask, products, 0.0), axis=1, keepdims=True)
        here = slice(head * HEAD_DIM, (head + 1) * HEAD_DIM)
        query_here = query_turned[here]
        numer_here = numer_turned[here]
        weight_back = dot_nn(masked, values)
        weights = weight_ref[head]
        score_back = weights.astype(WIDE) * (weight_back + denom_back)
        low = score_back.astype(LOW)
        upper, lower = score_back[:STRIP], score_back[STRIP:]
        start = pl.multiple_of(rows - 2 * STRIP - block * tile, STRIP)
        joined = [lower[:, :STRIP], upper[:, :-STRIP] + lower[:, STRIP:], upper[:, -STRIP:]]
        strips_ref[head, :, pl.ds(start, rows + STRIP)] += jnp.concatenate(joined, 1)
        key_acc[here, :] += dot_nn(query_here, low)
        value_acc[here, :] += dot_nn(numer_here, weights)
        query_back = dot_nt(low, keys)
        out = jnp.where(mask, query_back * 0.125, out)
    out = out.T
    if not first:
        out = out + query_in[0]
    query_back_ref[0] = out.astype(query_back_ref.dtype)

    @pl.when(step == pl.num_programs(0) - 1)
    def _():
        for group in range(groups):
            at = group * chunk
            pairs_back_ref[group, 0] = key_acc[:, at : at + chunk].astype(pairs_back_ref.dtype)
            pairs_back_ref[group, 1] = value_acc[:, at : at + chunk].astype(pairs_back_ref.dtype)
        diagonal_ref[...] = jnp.zeros_like(diagonal_ref)
        for head in range(heads):
            folded = strips_ref[head]
            size = STRIP
            while size > 8:
                size //= 2
                folded = folded[:size] + pltpu.roll(folded[size:], span - size, 1)
            row = folded[0:1]
            for place in range(1, 8):
                row = row + pltpu.roll(folded[place : place + 1], span - place, 1)
            diagonal_ref[head : head + 1, :] = pltpu.roll(row, STRIP - 1, 1)

def attend_back(
    queries, grads, attended, total, weights, pairs, before, last, begin, count, after
):
    groups, width, tile = queries.shape
    rows = groups * tile
    heads = width // HEAD_DIM
    span = 2 * rows
    block = pl.BlockSpec((1, width, tile), lambda i: (i + begin, 0, 0))
    out_block = pl.BlockSpec((1, width, tile), lambda i: (i, 0, 0))
    operands = (queries, grads, attended, total, weights, pairs, *before)
    return run(
        functools.partial(attend_back_kernel, heads=heads, rows=rows, first=not before, last=last, begin=begin),
        [
            shaped((count, width, tile), LOW if last else WIDE),
            shaped(pairs.shape, WIDE if last else LOW),
            shaped((8, span), WIDE),
        ],
        operands,
        "attend_back",
        flops=8 * width * rows * rows * count,
        grid=(count,),
        in_specs=[block, block, block, block]
        + [pl.BlockSpec((heads, tile, rows), lambda i: (0, i + begin, 0)), fixed(pairs.shape)]
        + [block] * len(before),
        out_specs=[out_block, fixed(pairs.shape), fixed((8, span))],
        scratch=[pltpu.VMEM((heads, STRIP, span), WIDE), pltpu.VMEM((width, rows), WIDE), pltpu.VMEM((width, rows), WIDE)], after=after)


def hot_rows(place_row, slots):
    tokens = place_row.shape[1]
    hot = lax.broadcasted_iota(jnp.int32, (slots, tokens), 0) == place_row
    return hot.astype(WIDE).astype(LOW)


def hot_columns(place_column, slots):
    tokens = place_column.shape[0]
    hot = lax.broadcasted_iota(jnp.int32, (tokens, slots), 1) == place_column
    return hot.astype(WIDE).astype(LOW)


def scatter_kernel(place_ref, rows_ref, slots_ref):
    hot = hot_rows(place_ref[...], slots_ref.shape[0])
    slots_ref[...] = dot_nn(hot, rows_ref[...]).astype(LOW)


def middle_kernel(
    att_ref, tokens_ref, weight_ref, gain_ref, place_ref, residual_ref, normed_ref, slots_ref
):
    residual = tokens_ref[...].astype(WIDE) + dot_tn(att_ref[...], weight_ref[...])
    residual_ref[...] = residual
    scale = lax.rsqrt(jnp.mean(residual * residual, axis=-1, keepdims=True) + EPSILON)
    normed = (residual * scale * row_of(gain_ref)).astype(LOW)
    normed_ref[...] = normed
    hot = hot_rows(place_ref[...], slots_ref.shape[0])
    slots_ref[...] = dot_nn(hot, normed).astype(LOW)


def route(normed, router, experts):
    logits = dot_nn(normed, router)
    lane = lax.broadcasted_iota(jnp.int32, logits.shape, 1)
    logits = jnp.where(lane < experts, logits, -jnp.inf)
    powers = jnp.exp(logits - jnp.max(logits, axis=-1, keepdims=True))
    return powers / jnp.sum(powers, axis=-1, keepdims=True), lane


def shard_copy(weight_refs, buffer_ref, semaphores, at):
    return pltpu.make_async_copy(weight_refs[at], buffer_ref.at[at % 2], semaphores.at[at % 2])


def take_shard(weight_refs, buffer_ref, semaphores):
    step = pl.program_id(0)

    @pl.when(step == 0)
    def _():
        for at in range(min(2, len(weight_refs))):
            shard_copy(weight_refs, buffer_ref, semaphores, at).start()

    for at in range(len(weight_refs)):

        @pl.when(step == at)
        def _(at=at):
            shard_copy(weight_refs, buffer_ref, semaphores, at).wait()

    return lax.rem(step, 2)


def next_shard(weight_refs, buffer_ref, semaphores):
    for at in range(len(weight_refs) - 2):

        @pl.when(pl.program_id(0) == at)
        def _(at=at):
            shard_copy(weight_refs, buffer_ref, semaphores, at + 2).start()


def shard_scratch(weights):
    return [pltpu.VMEM((2, *weights[0].shape), LOW), pltpu.SemaphoreType.DMA((2,))]


def shard_places(weights):
    return [pl.BlockSpec(memory_space=pltpu.HBM)] * len(weights)


def raw_back_kernel(up_ref, *refs):
    *weight_refs, raw_ref, buffer_ref, semaphores = refs
    slot = take_shard(weight_refs, buffer_ref, semaphores)
    raw_ref[...] = dot_nt(up_ref[...], buffer_ref[slot]).astype(LOW)
    next_shard(weight_refs, buffer_ref, semaphores)


def expert_kernel(own_ref, rows_ref, up_ref, router_ref, raw_ref, *refs, experts):
    *weight_refs, act_ref, pre_ref, home_ref, out_back_ref, logit_ref = refs[:-6]
    probs_ref, back_acc, gate_acc, gate_ref, buffer_ref, semaphores = refs[-6:]
    slot = take_shard(weight_refs, buffer_ref, semaphores)
    step = pl.program_id(0)
    rows = rows_ref[...]

    @pl.when(step == 0)
    def _():
        probs, lane = route(rows, router_ref[...], experts)
        probs_ref[...] = probs
        hot = (lane == own_ref[0]).astype(WIDE)
        gate = jnp.sum(probs * hot, axis=-1, keepdims=True)
        gate_ref[...] = jnp.broadcast_to(gate, gate_ref.shape)
        out_back_ref[...] = (gate * up_ref[...].astype(WIDE)).astype(LOW)
        back_acc[...] = jnp.zeros_like(back_acc)
        gate_acc[...] = jnp.zeros_like(gate_acc)

    gate = gate_ref[:, 0:1]
    lanes = gate_acc[...]
    back = back_acc[...]
    root = 0.7978845608028654
    hidden = buffer_ref.shape[2]
    size = 256 if hidden % 256 == 0 else 128
    count = hidden // size
    following = dot_nn(rows, buffer_ref[slot, :, 0:size])
    for piece in range(count):
        here = slice(piece * size, (piece + 1) * size)
        value = following
        if piece + 1 < count:
            following = dot_nn(rows, buffer_ref[slot, :, (piece + 1) * size : (piece + 2) * size])
        squared = value * value
        tilted = jnp.tanh(value * (root + (root * 0.044715) * squared))
        share = 0.5 + 0.5 * tilted
        wide = value * share
        act = wide.astype(LOW)
        slope = share + wide * (1.0 - share) * (2.0 * root + (6.0 * root * 0.044715) * squared)
        raw = raw_ref[:, here].astype(WIDE)
        pre = (gate * raw * slope).astype(LOW)
        act_ref[:, here] = act
        pre_ref[:, here] = pre
        back = back + dot_nt(pre, buffer_ref[slot, :, here])
        shares = act.astype(WIDE) * raw
        for lane in range(size // 128):
            lanes = lanes + shares[:, lane * 128 : (lane + 1) * 128]
    gate_acc[...] = lanes
    back_acc[...] = back
    next_shard(weight_refs, buffer_ref, semaphores)

    @pl.when(step == pl.num_programs(0) - 1)
    def _():
        probs = probs_ref[...]
        hot = (lax.broadcasted_iota(jnp.int32, probs.shape, 1) == own_ref[0]).astype(WIDE)
        gate_back = jnp.sum(gate_acc[...], axis=-1, keepdims=True)
        logit_back = (probs * gate_back * (hot - gate_ref[...])).astype(LOW)
        logit_ref[...] = logit_back
        home_ref[...] = (dot_nt(logit_back, router_ref[...]) + back_acc[...]).astype(LOW)


def store_half(former_ref, latter_ref, keep_ref, send_ref):
    count = pl.num_programs(0) // 2

    @pl.when(pl.program_id(0) < count)
    def _():
        send_ref[0] = dot_tn(former_ref[...], latter_ref[...]).astype(LOW)

    @pl.when(pl.program_id(0) >= count)
    def _():
        keep_ref[0] = dot_tn(former_ref[...], latter_ref[...]).astype(LOW)


def shard_at(i, shares):
    count = shares // 2
    return jnp.where(i < count, 2 * i + 1, 2 * (i - count))


def keep_spec(shape, shares):
    return pl.BlockSpec((1, *shape), lambda i: (jnp.maximum(i - shares // 2, 0), 0, 0))


def send_spec(shape, shares):
    return pl.BlockSpec((1, *shape), lambda i: (jnp.minimum(i, shares // 2 - 1), 0, 0))


def inner_grads_kernel(rows_ref, pre_ref, logit_ref, keep_ref, send_ref, router_ref):
    store_half(rows_ref, pre_ref, keep_ref, send_ref)

    @pl.when(pl.program_id(0) == 0)
    def _():
        router_ref[...] = dot_tn(logit_ref[...], rows_ref[...])[: router_ref.shape[0]]


def outer_grads_kernel(act_ref, out_back_ref, *refs):
    *weight_refs, keep_ref, send_ref, out_ref, total_ref, buffer_ref, semaphores = refs
    step = pl.program_id(0)
    slot = take_shard(weight_refs, buffer_ref, semaphores)

    @pl.when(step == 0)
    def _():
        total_ref[...] = jnp.zeros_like(total_ref)

    store_half(act_ref, out_back_ref, keep_ref, send_ref)
    total_ref[...] += dot_nn(act_ref[...], buffer_ref[slot])
    next_shard(weight_refs, buffer_ref, semaphores)

    @pl.when(step == pl.num_programs(0) - 1)
    def _():
        out_ref[...] = total_ref[...].astype(LOW)


def add_shards_kernel(*refs, count):
    operands, outs = refs[:count], refs[count:]
    total = operands[0][0].astype(WIDE)
    for operand in operands[1:]:
        total += operand[0].astype(WIDE)
    if len(outs) == 1:
        outs[0][0] = total.astype(outs[0].dtype)
        return
    half = pl.num_programs(1) // 2
    for place, out_ref in enumerate(outs):

        @pl.when(pl.program_id(1) // half == place)
        def _(out_ref=out_ref):
            out_ref[0] = total.astype(out_ref.dtype)


def add_shards(operands, start, count, kind, parts, name, after=()):
    _, rows, columns = operands[0].shape
    tile = rows // 2 if rows % 32 == 0 else rows
    steps = rows // tile
    parts = parts if steps % 2 == 0 else 1
    half = steps // parts
    block = pl.BlockSpec((1, tile, columns), lambda i, j: (start + i, j, 0))

    def out_block(place):
        last = half - 1
        return pl.BlockSpec(
            (1, tile, columns), lambda i, j: (i, jnp.clip(j - place * half, 0, last), 0)
        )

    return run(
        functools.partial(add_shards_kernel, count=len(operands)),
        [shaped((count, rows // parts, columns), kind)] * parts,
        (operands[0], *(loose(x) for x in operands[1:])),
        name,
        flops=0,
        grid=(count, steps),
        in_specs=[block] * len(operands),
        out_specs=[out_block(place) for place in range(parts)],
        after=after,
    )


def gather_shards(keep, send):
    operands = [keep, swap(send, "dp", 1)]
    size = keep.shape[0]
    while size > 2:
        half = size // 2
        gone = add_shards(operands, half, half, LOW, 1, "add_shards")
        operands.append(swap(gone[0], "dp", 2 * half))
        size = half
    gone = add_shards(operands, 1, 1, LOW, 1, "add_shards")
    return operands, [swap(part, "dp", 2) for part in gone], gone[0]


def finish_kernel(*refs, count, steps):
    former_refs, came_refs, (out_ref, mark_ref) = refs[:count], refs[count:-2], refs[-2:]
    total = former_refs[0][0].astype(WIDE)
    for former_ref in former_refs[1:]:
        total += former_ref[0].astype(WIDE)
    half = steps // len(came_refs)
    for place, came_ref in enumerate(came_refs):

        @pl.when(pl.program_id(0) // half == place)
        def _(came_ref=came_ref):
            out_ref[...] = total + came_ref[0].astype(WIDE)

    mark_ref[...] = jnp.zeros_like(mark_ref)


def finish_shards(formers, came):
    _, rows, columns = formers[0].shape
    tile = rows // 2 if rows % 32 == 0 else rows
    steps = rows // tile
    half = steps // len(came)
    block = pl.BlockSpec((1, tile, columns), lambda i: (0, i, 0))
    parts = [
        pl.BlockSpec(
            (1, tile, columns), lambda i, place=place: (0, jnp.clip(i - place * half, 0, half - 1), 0)
        )
        for place in range(len(came))
    ]
    return run(
        functools.partial(finish_kernel, count=len(formers), steps=steps),
        [shaped((rows, columns), WIDE), shaped((8, 128), WIDE)],
        (formers[0], *(loose(x) for x in (*formers[1:], *came))),
        "finish_shards",
        flops=0,
        grid=(steps,),
        in_specs=[block] * len(formers) + parts,
        out_specs=[pl.BlockSpec((tile, columns), lambda i: (i, 0)), fixed((8, 128))],
    )


def after_kernel(
    home_ref,
    place_ref,
    residual_ref,
    gain_ref,
    upstream_ref,
    weight_ref,
    att_back_ref,
    residual_back_ref,
    branch_ref,
    gain_back_ref,
):
    hot = hot_columns(place_ref[...], home_ref.shape[0])
    normed_back = dot_nn(hot, home_ref[...])
    residual = residual_ref[...]
    scale = lax.rsqrt(jnp.mean(residual * residual, axis=-1, keepdims=True) + EPSILON)
    spread = residual * scale
    gained = row_of(gain_ref) * normed_back
    inner = jnp.mean(gained * spread, axis=-1, keepdims=True)
    back = upstream_ref[...].astype(WIDE) + scale * (gained - spread * inner)
    residual_back_ref[...] = back
    branch = back.astype(LOW)
    branch_ref[...] = branch
    gain_back_ref[...] = jnp.broadcast_to(
        jnp.sum(normed_back * spread, axis=0, keepdims=True), gain_back_ref.shape
    )
    att_back_ref[...] = dot_nt(weight_ref[...], branch).astype(LOW)


def output_pieces_kernel(core_ref, att_ref, branch_ref, router_ref, gain_ref, *refs, owners):
    *out_refs, full_ref = refs
    grad = dot_nn(att_ref[...], branch_ref[...])
    own = grad.shape[0] // owners
    height = full_ref.shape[0] // owners
    full_ref[...] = jnp.zeros_like(full_ref)
    for owner in range(owners):
        full_ref[owner * height : owner * height + own, :] = grad[owner * own : (owner + 1) * own]
    at = own + router_ref.shape[0]
    full_ref[own:at, :] = router_ref[...]
    full_ref[at : at + 8, :] = gain_ref[...]
    for place, out_ref in enumerate(out_refs):
        height = out_ref.shape[0]
        start = pl.multiple_of(jnp.bitwise_xor(core_ref[0], place) * height, height)
        out_ref[...] = full_ref[pl.ds(start, height), :].astype(out_ref.dtype)


def is_cube():
    return [lax.axis_size(name) for name in ("head", "blk", "dp")] == [4, 2, 4]


def sums_kernel(me_ref, *refs, count):
    operands, outs = refs[: len(refs) - count], refs[len(refs) - count :]
    for place, out_ref in enumerate(outs):
        height = out_ref.shape[0]
        start = pl.multiple_of(jnp.bitwise_xor(me_ref[0], place) * height, height)
        total = operands[0][pl.ds(start, height), :].astype(WIDE)
        for operand in operands[1:]:
            total += operand[pl.ds(start, height), :].astype(WIDE)
        out_ref[...] = total.astype(out_ref.dtype)


def sums(me, operands, count, name, after=()):
    height, breadth = operands[0].shape
    return run(
        functools.partial(sums_kernel, count=count),
        [shaped((height // count, breadth), LOW)] * count,
        (me[None].astype(jnp.int32), operands[0], *(loose(x) for x in operands[1:])),
        name,
        flops=0,
        in_specs=[SMEM] + [VMEM] * len(operands),
        after=after,
    )


def cross(mine, other, name, after=()):
    spot = lax.axis_index("blk") * 2 + lax.axis_index("dp") // 2
    own, along, across, corner = sums(spot, (mine, swap(other, "dp", 1)), 4, name, after)
    diagonal = [(b * 4 + d, (1 - b) * 4 + (d ^ 2)) for b in range(2) for d in range(4)]
    return [
        own,
        swap(across, "blk", 1),
        swap(along, "dp", 2),
        lax.ppermute(corner, ("blk", "dp"), diagonal),
    ]


def output_pieces(att_tok, branch_back, router_back, gain_back):
    model_width, experts = branch_back.shape[1], router_back.shape[0]
    cube = is_cube()
    owners = 8 if cube else 1
    height = owners * -(-(model_width // owners + experts + 8) // 128) * 128
    dp = lax.axis_index("dp")
    count = 2 if cube else 1
    outs = run(
        functools.partial(output_pieces_kernel, owners=owners),
        [shaped((height // count, model_width), LOW if cube else WIDE)] * count,
        (
            ((dp & 1) * (count - 1)).astype(jnp.int32)[None],
            att_tok,
            branch_back,
            router_back,
            gain_back,
        ),
        "output_pieces",
        flops=2 * att_tok.size * model_width,
        in_specs=[SMEM] + [VMEM] * 4,
        scratch=[pltpu.VMEM((height, model_width), WIDE)],
    )
    if not cube:
        return (), (), lax.psum(outs[0], ("head", "blk", "dp"))
    own, *came = cross(*outs, "output_core")
    shares = sums(lax.axis_index("head"), (own, *came), 4, "output_sum")
    arrived = [shares[0]] + [swap(shares[step], "head", step) for step in range(1, 4)]
    return (own,), (shares[0],), arrived


def output_kernel(
    residual_ref, normed_ref, router_ref, chosen_ref, place_ref, slots_ref, out_ref, *, experts
):
    probs, lane = route(normed_ref[...], router_ref[...], experts)
    hot = (lane == chosen_ref[...]).astype(WIDE)
    gate = jnp.sum(probs * hot, axis=-1, keepdims=True)
    expert_out = dot_nn(hot_columns(place_ref[...], slots_ref.shape[0]), slots_ref[...])
    out_ref[...] = (residual_ref[...] + gate * expert_out).astype(LOW)


def tokens_grad_kernel(
    triples_ref,
    query_weight_ref,
    key_weight_ref,
    value_weight_ref,
    tokens_ref,
    gain_ref,
    residual_back_ref,
    out_ref,
):
    groups = triples_ref.shape[0]
    weight_refs = (query_weight_ref, key_weight_ref, value_weight_ref)
    normed_back = jnp.zeros(out_ref.shape[::-1], WIDE)
    for kind, weight_ref in enumerate(weight_refs):
        rows = jnp.concatenate([triples_ref[group, kind] for group in range(groups)], 0)
        normed_back += dot_nn(weight_ref[...], rows)
    normed_back = normed_back.T
    values = tokens_ref[...].astype(WIDE)
    scale = lax.rsqrt(jnp.mean(values * values, axis=-1, keepdims=True) + EPSILON)
    spread = values * scale
    gained = row_of(gain_ref) * normed_back
    inner = jnp.mean(gained * spread, axis=-1, keepdims=True)
    out_ref[...] = (residual_back_ref[...] + scale * (gained - spread * inner)).astype(LOW)


def bucket_sums(diagonal, bucket_row, buckets):
    breadth = bucket_row.shape[1]
    hot = lax.broadcasted_iota(jnp.int32, (buckets, breadth), 0) == bucket_row
    hot = hot.astype(WIDE).astype(LOW)
    high = diagonal.astype(LOW)
    rest = diagonal - high.astype(WIDE)
    middle = rest.astype(LOW)
    small = (rest - middle.astype(WIDE)).astype(LOW)
    return dot_nt(high, hot) + dot_nt(middle, hot) + dot_nt(small, hot)


def side(grads):
    return -(-3 * grads // 128) * 128


def blocks_of(refs):
    return [ref[place] for ref in refs for place in range(ref.shape[0])]


def projection_grads(turned_ref, query_refs, pairs_ref):
    _, width, tokens = query_refs[0].shape
    queries = blocks_of(query_refs)
    groups = len(queries)
    spare = jnp.zeros((side(width) - 3 * width, tokens), LOW)
    total = None
    for group in range(groups):
        rows = [queries[group], pairs_ref[group, 0], pairs_ref[group, 1], spare]
        part = dot_nt(turned_ref[group], jnp.concatenate(rows, 0))
        total = part if total is None else total + part
    return total


def table_sums(diagonal_refs, bucket_refs, buckets):
    table = bucket_sums(diagonal_refs[0][...], bucket_refs[0][...], buckets)
    for diagonal_ref, bucket_ref in zip(diagonal_refs[1:], bucket_refs[1:]):
        table += bucket_sums(diagonal_ref[...], bucket_ref[...], buckets)
    return table


def add_pairs(home_refs):
    total = home_refs[0][...].astype(WIDE)
    for home_ref in home_refs[1:]:
        total += home_ref[...].astype(WIDE)
    return total.astype(LOW)


def triples_kernel(*refs, parts):
    pairs = add_pairs(refs[parts:-1])
    for group, queries in enumerate(blocks_of(refs[:parts])):
        refs[-1][group, 0] = queries
        refs[-1][group, 1] = pairs[group, 0]
        refs[-1][group, 2] = pairs[group, 1]


def pieces_kernel(core_ref, turned_ref, *refs, parts, tiles, buckets):
    query_refs, refs = refs[:parts], refs[parts:]
    home_refs, refs = refs[:tiles], refs[tiles:]
    diagonal_refs, bucket_refs = refs[:tiles], refs[tiles : 2 * tiles]
    *out_refs, pairs_ref, full_ref = refs[2 * tiles :]
    width = query_refs[0].shape[1]
    pairs_ref[...] = add_pairs(home_refs)
    full_ref[...] = projection_grads(turned_ref, query_refs, pairs_ref)
    table = table_sums(diagonal_refs, bucket_refs, buckets)
    full_ref[0:8, 3 * width : 3 * width + buckets] = table
    for place, out_ref in enumerate(out_refs):
        height = out_ref.shape[0]
        start = pl.multiple_of(jnp.bitwise_xor(core_ref[0], place) * height, height)
        out_ref[...] = full_ref[pl.ds(start, height), :].astype(out_ref.dtype)


def join_kernel(*refs):
    *refs, out_ref = refs
    copies, halves, part, _ = out_ref.shape
    count = len(refs) // 2
    columns = refs[0].shape[1]
    total, packed = (
        functools.reduce(jnp.add, [ref[...].astype(WIDE) for ref in group])
        for group in (refs[:count], refs[count:])
    )
    height = packed.shape[0] // halves
    for half in range(halves):
        former = total[half * part : (half + 1) * part].astype(LOW)
        rows = packed[half * height : (half + 1) * height]
        blocks = [rows[:, at : at + 256] for at in range(0, rows.shape[1], 256)]
        latter = jnp.concatenate(blocks, 0).astype(LOW)
        for copy in range(copies):
            out_ref[copy, half, :, :columns] = former
            out_ref[copy, half, :, columns:] = latter


def share_kernel(spot_ref, cases, places, weight_refs, out_refs, sums_ref, table_ref, extra_ref, heads):
    step = pl.program_id(0)
    owner = jnp.bitwise_xor(spot_ref[0], places[0] if len(places) == 1 else place_at(step, places))
    part = out_refs[0].shape[0] // 2
    width = heads * HEAD_DIM
    columns = side(width)
    buckets = table_ref.shape[2]
    for case, pair in enumerate(cases):

        @pl.when(step == case)
        def _(pair=pair):
            for half in range(2):
                ref = pair[half]
                groups = ref.shape[0]
                at = half if ref.shape[1] == 2 else 0
                rows = slice(half * part, (half + 1) * part)

                def tile(group, place, ref=ref, at=at):
                    return ref[group, at, :, place * 128 : (place + 1) * 128].astype(WIDE)

                def turned(group, place, tile=tile):
                    return pltpu.roll(tile(group, place), 64, 1)

                lower = lax.broadcasted_iota(jnp.int32, (part, 128), 1) < 64
                for one in range(0, groups, 2):
                    two = one + 1
                    for kind in range(3):
                        if kind == 1:
                            middle = turned(one, 2)
                            parts = (
                                jnp.where(lower, turned(one, 1), middle),
                                jnp.where(lower, middle, tile(two, 1)),
                                tile(two, 2),
                            )
                        else:
                            place = 3 * kind // 2
                            first = turned(two, place)
                            parts = (
                                tile(one, place),
                                jnp.where(lower, tile(one, place + 1), first),
                                jnp.where(lower, first, turned(two, place + 1)),
                            )
                        for number, values in enumerate(parts):
                            lane = one * width + number * 128
                            out_refs[kind][rows, lane : lane + 128] = values
                for group in range(groups):
                    packed = ref[group, at, :, columns:].astype(WIDE)
                    start = group * 32 + half * 16
                    for number in range(part // 16):
                        lane = number * 256
                        values = packed[number * 16 : (number + 1) * 16]
                        if group + 1 < groups:
                            out_refs[3][start : start + 16, lane : lane + 256] = values
                        else:

                            @pl.when(owner == 0)
                            def _(values=values, half=half, lane=lane):
                                extra_ref[half * 16 : half * 16 + 16, lane : lane + 256] = values

                    if half == 0:

                        @pl.when(owner == 0)
                        def _(group=group, tile=tile):
                            table_ref[group] = tile(group, 4)[:8, 64 : 64 + buckets]

    shares = jnp.zeros((2 * part, 1), WIDE)
    for kind in range(3):
        shares += jnp.sum(
            out_refs[kind][...] * weight_refs[kind][...].astype(WIDE), axis=1, keepdims=True
        )
    shares = jnp.broadcast_to(shares, (2 * part, 128))
    if sums_ref.shape[0] == 2 * part:
        sums_ref[...] = shares
    else:
        sums_ref[pl.ds(owner * 2 * part, 2 * part), :] = shares


def place_at(step, places):
    return sum(jnp.where(step == at, place, 0) for at, place in enumerate(places))


FIRST_PLACES, LAST_PLACES = (0, 1, 2, 4, 5, 6), (3, 7)


def first_shares_kernel(spot_ref, *refs, heads):
    piece_refs, weight_refs, refs = refs[:6], refs[6:9], refs[9:]
    out_refs, (sums_ref, table_ref, extra_ref) = refs[:4], refs[4:]

    @pl.when(pl.program_id(0) == 0)
    def _():
        table_ref[...] = jnp.zeros_like(table_ref)
        extra_ref[...] = jnp.zeros_like(extra_ref)

    cases = [(ref, ref) for ref in piece_refs]
    share_kernel(
        spot_ref, cases, FIRST_PLACES, weight_refs, out_refs, sums_ref, table_ref, extra_ref, heads
    )


def last_shares_kernel(spot_ref, *refs, heads, experts):
    piece_refs, weight_refs, refs = refs[:4], refs[4:7], refs[7:]
    gain_ref, sums_in, table_in, extra_in, *refs = refs
    out_refs, refs = refs[4:8], refs[8:]
    gain_out, second_out, table_out, router_out, sums_ref, table_ref, extra_ref = refs
    step = pl.program_id(0)

    @pl.when(step == 0)
    def _():
        sums_ref[...] = sums_in[...]
        table_ref[...] = table_in[...]
        extra_ref[...] = extra_in[...]

    cases = [(piece_refs[0], piece_refs[1]), (piece_refs[2], piece_refs[3])]
    share_kernel(
        spot_ref, cases, LAST_PLACES, weight_refs, out_refs, sums_ref, table_ref, extra_ref, heads
    )

    @pl.when(step == pl.num_programs(0) - 1)
    def _():
        first = sums_ref[...].T[0:8] / row_of(gain_ref)
        second = extra_ref[experts : experts + 8, :]
        for lane in range(gain_out.shape[0]):
            gain_out[lane : lane + 1, :] = first[0:1, lane * 128 : (lane + 1) * 128]
            second_out[lane : lane + 1, :] = second[0:1, lane * 128 : (lane + 1) * 128]
        router_out[...] = extra_ref[:experts, :]
        for group in range(table_ref.shape[0]):
            table_out[group * heads : (group + 1) * heads, :] = table_ref[group][:heads]


def put_together(me, first, corners, weights, gain, heads, buckets, experts):
    model_width = weights[0].shape[0]
    groups, _, part, _ = first[0].shape

    def rows(places, breadth):
        return pl.BlockSpec(
            (2 * part, breadth), lambda i, me: (place_at(i, places) ^ me[0], 0)
        )

    square = shaped((model_width, model_width), WIDE)
    kept_shapes = [(groups, 8, buckets), (32, model_width)]
    *grads, sums, table, extra = run_with_scalar(
        functools.partial(first_shares_kernel, heads=heads),
        me,
        [square] * 4 + [shaped((model_width, 128), WIDE)] + [shaped(x, WIDE) for x in kept_shapes],
        (*(loose(x) for x in first), *weights),
        "first_shares",
        grid=(len(FIRST_PLACES),),
        in_specs=[fixed(x.shape) for x in first] + [rows(FIRST_PLACES, model_width)] * 3,
        out_specs=[rows(FIRST_PLACES, model_width)] * 4
        + [rows(FIRST_PLACES, 128)]
        + [fixed(x) for x in kept_shapes],
    )
    corners = [gate(array, (table,)) for array in corners]
    last = (*corners, *(swap(array, "dp", 1) for array in corners))
    operands = (*(loose(x) for x in last), *weights, gain, sums, table, extra, *grads)
    vectors = [(model_width // 128, 128)] * 2 + [(groups * heads, buckets), (experts, model_width)]
    count = len(last)
    *grads, shares, second, table, router = run_with_scalar(
        functools.partial(last_shares_kernel, heads=heads, experts=experts),
        me,
        [square] * 4 + [shaped(x, WIDE) for x in vectors],
        operands,
        "last_shares",
        grid=(len(LAST_PLACES),),
        in_specs=[fixed(x.shape) for x in last]
        + [rows(LAST_PLACES, model_width)] * 3
        + [fixed(x.shape) for x in operands[count + 3 : count + 7]]
        + [pl.BlockSpec(memory_space=pltpu.HBM)] * 4,
        out_specs=[rows(LAST_PLACES, model_width)] * 4 + [fixed(x) for x in vectors],
        scratch=[pltpu.VMEM((model_width, 128), WIDE)] + [pltpu.VMEM(x, WIDE) for x in kept_shapes],
        aliases={count + 8 + i: i for i in range(4)},
    )
    query_grad, key_grad, value_grad, output_grad = grads
    return (
        query_grad,
        key_grad,
        value_grad,
        shares.reshape(-1),
        table.T,
        output_grad,
        router.T,
        second.reshape(-1),
    )


def take_half_kernel(values_ref, out_ref):
    out_ref[...] = values_ref[...]


def take_half(values, half):
    groups, _, *rest = values.shape
    return pl.pallas_call(
        take_half_kernel,
        out_shape=pltpu.HBM((groups, 1, *rest), values.dtype),
        grid=(groups,),
        in_specs=[pl.BlockSpec((1, 1, *rest), lambda i: (i, half, 0, 0))],
        out_specs=pl.BlockSpec((1, 1, *rest), lambda i: (i, 0, 0, 0)),
        compiler_params=pltpu.CompilerParams(vmem_limit_bytes=VMEM_BYTES),
        name="take_half",
    )(values)


def weight_sums(
    turned, query_backs, home, diagonals, bucket_rows, buckets, weights, gain, experts, packed, middle, late
):
    groups, model_width, _ = turned.shape
    width = query_backs[0].shape[1]
    heads = width // HEAD_DIM
    tiles = len(diagonals)
    cube = is_cube()
    columns = side(width)
    dp, blk = lax.axis_index("dp"), lax.axis_index("blk")
    count = 2 if cube else 1
    pieces = run(
        functools.partial(pieces_kernel, parts=len(query_backs), tiles=tiles, buckets=buckets),
        [shaped((model_width // count, columns), LOW if cube else WIDE)] * count,
        (
            ((dp & 1) * (count - 1)).astype(jnp.int32)[None],
            near(turned),
            *query_backs,
            *received_loose(home),
            *diagonals,
            *bucket_rows,
        ),
        "projection_pieces",
        flops=6 * turned.size * width,
        in_specs=[SMEM] + [VMEM] * (1 + len(query_backs) + 3 * tiles),
        scratch=[pltpu.VMEM(home[0].shape, LOW), pltpu.VMEM((model_width, columns), WIDE)],
    )
    if not cube:
        sums = lax.psum(pieces[0], ("blk", "dp"))
        table = lax.all_gather(
            sums[:heads, 3 * width : 3 * width + buckets], "head", axis=0, tiled=True
        )
        grads = sums[:, : 3 * width].reshape(model_width, 3, width)
        grads = lax.all_gather(grads, "head", axis=2, tiled=True)
        grads = [grads[:, i] for i in range(3)]
        shares = sum(jnp.sum(x * y.astype(WIDE), axis=1) for x, y in zip(grads, weights))
        rest = packed[model_width:]
        shares = shares / gain.reshape(-1).astype(WIDE)
        packed = packed[:model_width], rest[:experts].T, rest[experts]
        return pieces, *grads, shares, table.T, *packed
    part = model_width // 16
    copies = run(
        join_kernel,
        [shaped((groups, 2, part, columns + 256), LOW)],
        tuple(loose(x) for x in (*cross(*pieces, "projection_core", middle), *packed)),
        "join",
        flops=0,
        after=late,
    )[0]
    own = blocks_over(copies, "head")
    across, along = swap(own, "blk", 1), swap(own, "dp", 2)
    corners = (
        swap(take_half(across, 0), "dp", 2),
        swap(take_half(along, 1), "blk", 1),
    )
    near_ones = (own, along, across)
    first = (*near_ones, *(swap(array, "dp", 1) for array in near_ones))
    me = ((dp & 1) * 4 + blk * 2 + dp // 2).astype(jnp.int32)[None]
    return pieces, *put_together(me, first, corners, weights, gain, heads, buckets, experts)


def body(
    tokens,
    first_gain,
    query_weight,
    key_weight,
    value_weight,
    output_weight,
    bias_table,
    second_gain,
    router_weight,
    inner_weight,
    outer_weight,
    expert_index,
    capacity_slot,
    bucket_of_offset,
    upstream,
):
    _, token_rows, model_width = tokens.shape
    groups = lax.axis_size("head")
    cycle = lax.axis_size("blk")
    shares = lax.axis_size("dp")
    width = model_width // groups
    heads = width // HEAD_DIM
    local_rows = groups * token_rows
    length = local_rows * cycle
    buckets = bias_table.shape[0]
    experts = router_weight.shape[1]
    capacity = max(2, 2 * token_rows // experts)
    slots = experts * capacity
    token_values, upstream_values = tokens[0], upstream[0]
    gain_one, gain_two = first_gain.reshape(-1, 128), second_gain.reshape(-1, 128)
    chosen = expert_index[0]
    place = chosen * capacity + capacity_slot[0]
    place_row, place_column, chosen_column = place[None], place[:, None], chosen[:, None]
    router = jnp.pad(router_weight, ((0, 0), (0, 128 - experts)))

    inner_shards, outer_shards = [inner_weight[0]], [outer_weight[0]]
    for held in (outer_shards, inner_shards):
        for bit in range(1, shares.bit_length() - 1):
            held += [swap(values, "dp", 1 << bit) for values in held]
    far_inner, far_outer = inner_shards[1:], outer_shards[1:]
    for held in (outer_shards, inner_shards):
        held[:] = [x for values in held for x in (values, swap(values, "dp", 1))]

    square = model_width * model_width
    pairs, normed_one = run(
        project_pairs_kernel,
        [
            shaped((groups, 2, width, token_rows), LOW),
            shaped((token_rows, model_width), LOW),
        ],
        (token_values, gain_one, key_weight, value_weight),
        "project_pairs",
        flops=4 * token_rows * square,
    )
    pairs = blocks_over(pairs, "head")
    head_start = (lax.axis_index("head") * heads).astype(jnp.int32)[None]
    table_rows = jnp.pad(bias_table.T, ((0, -(groups * heads) % 8), (0, 0)))
    bucket_line = jnp.pad(bucket_of_offset, (0, 1))[None]
    blk = lax.axis_index("blk")
    tile_buckets, tile_strips = [], []
    for step in range(cycle):
        number = lax.rem(blk + cycle - step, cycle)
        start = length + (number - blk - 1) * local_rows
        tile_buckets.append(lax.dynamic_slice_in_dim(bucket_line, start, 2 * local_rows, 1))
    tile_pairs = [pairs] + [turn(pairs, "blk", step) for step in range(1, cycle)]
    up_slots = run(
        scatter_kernel,
        [shaped((slots, model_width), LOW)],
        (place_row, upstream_values),
        "scatter_up",
        flops=2 * slots * token_rows * model_width,
        after=(normed_one,),
    )[0]
    turned = run(
        turn_kernel,
        [shaped((groups, model_width, token_rows), LOW)],
        (normed_one,),
        "turn",
        flops=0,
    )[0]
    queries = run(
        project_queries_kernel,
        [shaped((groups, width, token_rows), LOW)],
        (normed_one, query_weight),
        "project_queries",
        flops=2 * token_rows * square,
        after=(up_slots, turned),
    )[0]
    queries = blocks_over(gate(queries, (loose(pairs),)), "head")
    up_rows = blocks_over(up_slots, ("head", "blk"))
    for step in range(0, cycle, 2):
        tile_strips += make_strips(
            head_start, table_rows, tile_buckets[step : step + 2], heads, (queries,)
        )
    tile_weights, before = [], ()
    for step in range(0, cycle, 2):
        tiles = slice(step, step + 2)
        last = step + 2 >= cycle
        results = attend(queries, tile_pairs[tiles], tile_strips[tiles], before, last)
        tile_weights += results[: len(tile_pairs[tiles])]
        total, attended, *rest = results[len(tile_pairs[tiles]) :]
        before = (attended, total)
    attended_low = gate(rest[0], (loose(up_rows),))
    att_tok = blocks_over(attended_low, "head").reshape(model_width, token_rows)
    hidden = inner_shards[0].shape[1]
    full_hidden = shares * hidden
    product = 2 * slots * model_width * full_hidden
    hidden_block = pl.BlockSpec((slots, hidden), lambda i: (0, i))
    turned_block = pl.BlockSpec((slots, hidden), lambda i: (0, shard_at(i, shares)))
    raw = run(
        raw_back_kernel,
        [shaped((slots, full_hidden), LOW)],
        (near(up_rows), *outer_shards),
        "raw_back",
        flops=product,
        grid=(shares,),
        in_specs=[fixed(up_rows.shape)] + shard_places(outer_shards),
        out_specs=[hidden_block],
        scratch=shard_scratch(outer_shards),
    )[0]
    residual_mid, normed_two, normed_slots = run(
        middle_kernel,
        [
            shaped((token_rows, model_width), WIDE),
            shaped((token_rows, model_width), LOW),
            shaped((slots, model_width), LOW),
        ],
        (near(att_tok), token_values, output_weight, gain_two, place_row),
        "middle",
        flops=2 * token_rows * square + 2 * slots * token_rows * model_width,
        after=(raw, router, *far_inner),
    )
    expert_rows = blocks_over(normed_slots, ("head", "blk"))
    own_expert = (lax.axis_index("head") * cycle + blk).astype(jnp.int32)[None]
    hidden_act, pre_back, home_slots, out_back, logit_back = run(
        functools.partial(expert_kernel, experts=experts),
        [
            shaped((slots, full_hidden), LOW),
            shaped((slots, full_hidden), LOW),
            shaped((slots, model_width), LOW),
            shaped((slots, model_width), LOW),
            shaped((slots, 128), LOW),
        ],
        (own_expert, near(expert_rows), near(up_rows), router, raw, *inner_shards),
        "expert",
        flops=2 * product,
        grid=(shares,),
        in_specs=[
            SMEM,
            fixed(expert_rows.shape),
            fixed(up_rows.shape),
            fixed(router.shape),
            hidden_block,
            *shard_places(inner_shards),
        ],
        out_specs=[
            hidden_block,
            hidden_block,
            fixed((slots, model_width)),
            fixed((slots, model_width)),
            fixed((slots, 128)),
        ],
        scratch=[
            pltpu.VMEM((slots, 128), WIDE),
            pltpu.VMEM((slots, model_width), WIDE),
            pltpu.VMEM((slots, 128), WIDE),
            pltpu.VMEM((slots, 128), WIDE),
            *shard_scratch(inner_shards),
        ],
    )
    home_rows = blocks_over(home_slots, ("head", "blk"))
    inner_shape, outer_shape = (model_width, hidden), (hidden, model_width)
    inner_keep, inner_send, router_back = run(
        inner_grads_kernel,
        [shaped((shares // 2, *inner_shape), LOW)] * 2 + [shaped((experts, model_width), WIDE)],
        (near(expert_rows), pre_back, logit_back),
        "inner_grads",
        flops=product,
        grid=(shares,),
        in_specs=[fixed(expert_rows.shape), turned_block, fixed(logit_back.shape)],
        out_specs=[
            keep_spec(inner_shape, shares),
            send_spec(inner_shape, shares),
            fixed((experts, model_width)),
        ],
    )
    turned_shards = outer_shards[1::2] + outer_shards[0::2]
    outer_keep, outer_send, expert_out = run(
        outer_grads_kernel,
        [shaped((shares // 2, *outer_shape), LOW)] * 2 + [shaped((slots, model_width), LOW)],
        (hidden_act, out_back, *turned_shards),
        "outer_grads",
        flops=2 * product,
        grid=(shares,),
        in_specs=[turned_block, fixed(out_back.shape)] + shard_places(outer_shards),
        out_specs=[
            keep_spec(outer_shape, shares),
            send_spec(outer_shape, shares),
            fixed((slots, model_width)),
        ],
        scratch=[pltpu.VMEM((slots, model_width), WIDE)] + shard_scratch(outer_shards),
    )
    att_back, residual_back, branch_back, gain_back = run(
        after_kernel,
        [
            shaped((model_width, token_rows), LOW),
            shaped((token_rows, model_width), WIDE),
            shaped((token_rows, model_width), LOW),
            shaped((8, model_width), WIDE),
        ],
        (near(home_rows), place_column, residual_mid, gain_two, upstream_values, output_weight),
        "after",
        flops=2 * token_rows * square + 2 * slots * token_rows * model_width,
        after=(router_back, expert_out),
    )
    head_back = blocks_over(att_back.reshape(groups, width, token_rows), "head")
    packed_core, packed_sum, packed_shares = output_pieces(
        att_tok, branch_back, router_back, gain_back
    )
    *inner_parts, inner_gone = gather_shards(inner_keep, gate(inner_send, (att_back,)))
    *outer_parts, outer_gone = gather_shards(outer_keep, gate(outer_send, (att_back,)))
    turned = gate(turned, (head_back, *packed_core, inner_gone, outer_gone))
    turned_all = blocks_over(turned, "head")

    before, diagonals, home, query_backs = (), [], [], []
    for step in range(1, cycle):
        query_back, pairs_part, diagonal = attend_back(
            queries,
            head_back,
            attended,
            total,
            tile_weights[step],
            tile_pairs[step],
            before,
            False,
            0,
            groups,
            (),
        )
        before = (query_back,)
        diagonals.append(diagonal)
        home.append(turn(pairs_part, "blk", cycle - step))
    cut = groups - 1
    for begin, count, after in (
        (0, cut, packed_sum),
        (cut, groups - cut, tuple(loose(x) for x in (turned_all, *home[:1], *inner_parts[1]))),
    ):
        query_back, pairs_part, diagonal = attend_back(
            queries,
            head_back,
            attended,
            total,
            tile_weights[0],
            tile_pairs[0],
            before,
            True,
            begin,
            count,
            after,
        )
        query_backs.append(query_back)
        if begin == 0:
            out_rows = blocks_over(gate(expert_out, (loose(turned_all), query_back)), ("head", "blk"))
        diagonals.append(diagonal)
        home.append(pairs_part)
    diagonal_buckets = [*tile_buckets[1:], tile_buckets[0], tile_buckets[0]]
    layer_output = run(
        functools.partial(output_kernel, experts=experts),
        [shaped((token_rows, model_width), LOW)],
        (residual_mid, normed_two, router, chosen_column, place_column, loose(out_rows)),
        "layer_output",
        flops=2 * slots * token_rows * model_width,
    )[0]
    (
        pieces,
        query_grad,
        key_grad,
        value_grad,
        first_gain_grad,
        table_grad,
        output_grad,
        router_grad,
        second_gain_grad,
    ) = weight_sums(
        turned_all,
        query_backs,
        home,
        diagonals,
        diagonal_buckets,
        buckets,
        (query_weight, key_weight, value_weight),
        gain_one,
        experts,
        packed_shares,
        (loose(out_rows),),
        (*(loose(x) for x in outer_parts[1]), layer_output),
    )
    inner_part, inner_mark = finish_shards(*inner_parts)
    outer_part, outer_mark = finish_shards(*outer_parts)
    triples = run(
        functools.partial(triples_kernel, parts=len(query_backs)),
        [shaped((groups, 3, width, token_rows), LOW)],
        (*query_backs, *received_loose(home)),
        "triples",
        flops=0,
        after=(pieces[0], inner_mark, outer_mark),
    )[0]
    triples_tok = blocks_over(triples, "head")
    tokens_grad = run(
        tokens_grad_kernel,
        [shaped((token_rows, model_width), LOW)],
        (
            loose(triples_tok),
            query_weight,
            key_weight,
            value_weight,
            token_values,
            gain_one,
            residual_back,
        ),
        "tokens_grad",
        flops=6 * token_rows * square,
    )[0]
    return (
        layer_output[None],
        tokens_grad[None],
        first_gain_grad,
        query_grad,
        key_grad,
        value_grad,
        output_grad,
        table_grad,
        second_gain_grad,
        router_grad,
        inner_part[None],
        outer_part[None],
    )


def solution(mesh):
    return jax.shard_map(
        body,
        mesh=mesh,
        in_specs=(
            P("dp", ("blk", "head"), None),
            P(),
            P(),
            P(),
            P(),
            P(),
            P(),
            P(),
            P(),
            P(("head", "blk"), None, "dp"),
            P(("head", "blk"), "dp", None),
            P("dp", ("blk", "head")),
            P("dp", ("blk", "head")),
            P(),
            P("dp", ("blk", "head"), None),
        ),
        out_specs=(
            P("dp", ("blk", "head"), None),
            P("dp", ("blk", "head"), None),
            P(),
            P(),
            P(),
            P(),
            P(),
            P(),
            P(),
            P(),
            P(("head", "blk"), None, "dp"),
            P(("head", "blk"), "dp", None),
        ),
        check_vma=False,
    )
```

```python
import functools
import math

import jax
import jax.numpy as jnp
from jax import lax
from jax.experimental import pallas as pl
from jax.experimental.pallas import tpu as pltpu
from jax.sharding import PartitionSpec as P

HEAD_DIM = 64
EPSILON = 1e-06
STRIP = 128
VMEM_BYTES = 28 * 2**20
LOW = jnp.bfloat16
WIDE = jnp.float32


def dot_nt(former, latter):
    return lax.dot_general(former, latter, (((1,), (1,)), ((), ())), preferred_element_type=WIDE)


def dot_nn(former, latter):
    return lax.dot_general(former, latter, (((1,), (0,)), ((), ())), preferred_element_type=WIDE)


def dot_tn(former, latter):
    return lax.dot_general(former, latter, (((0,), (0,)), ((), ())), preferred_element_type=WIDE)


def shaped(shape, kind):
    return pltpu.HBM(tuple(shape), kind)


def kept(shape, kind):
    return pltpu.VMEM(tuple(shape), kind)


class Near:
    def __init__(self, values):
        self.values, self.shape, self.dtype = values, values.shape, values.dtype


def near(values):
    return Near(values)


class Loose(Near):
    pass


def loose(values):
    return Loose(values)


def fixed(shape):
    return pl.BlockSpec(tuple(shape), lambda *_: (0,) * len(shape), pipeline_mode=pl.Buffered(1))


def received_loose(home):
    return [loose(x) if x.dtype == LOW else x for x in home]


def placed(values):
    if isinstance(values, Loose):
        return values.values
    if isinstance(values, Near):
        return pltpu.with_memory_space_constraint(values.values, pltpu.VMEM)
    return pltpu.with_memory_space_constraint(values, pltpu.HBM)


def unread(values):
    return pl.BlockSpec(memory_space=pl.ANY if isinstance(values, Loose) else pltpu.HBM)


def run(
    kernel, outs, operands, name, flops, grid=None, in_specs=None, out_specs=None, scratch=(), after=()
):
    moved = sum(math.prod(x.shape) * jnp.dtype(x.dtype).itemsize for x in (*operands, *outs))
    count, skipped = len(operands), len(after)
    if grid is None:
        grid = (1,)
        out_specs = [fixed(x.shape) for x in outs]
    if in_specs is None:
        in_specs = [VMEM] * count
    in_specs = [fixed(x.shape) if spec is VMEM else spec for x, spec in zip(operands, in_specs)]

    def body(*refs):
        kernel(*refs[:count], *refs[count + skipped :])

    return pl.pallas_call(
        body,
        out_shape=list(outs),
        grid=grid,
        in_specs=in_specs + [unread(x) for x in after],
        out_specs=out_specs,
        scratch_shapes=list(scratch),
        compiler_params=pltpu.CompilerParams(vmem_limit_bytes=VMEM_BYTES),
        cost_estimate=pl.CostEstimate(flops=flops, bytes_accessed=moved, transcendentals=0),
        name=name,
    )(
        *(x if spec is SMEM else placed(x) for x, spec in zip(operands, in_specs)),
        *(placed(x) for x in after),
    )


def run_with_scalar(
    kernel, scalar, outs, operands, name, grid, in_specs, out_specs, scratch=(), aliases=None
):
    return pl.pallas_call(
        kernel,
        out_shape=list(outs),
        grid_spec=pltpu.PrefetchScalarGridSpec(
            num_scalar_prefetch=1,
            grid=grid,
            in_specs=in_specs,
            out_specs=out_specs,
            scratch_shapes=list(scratch),
        ),
        compiler_params=pltpu.CompilerParams(vmem_limit_bytes=VMEM_BYTES),
        input_output_aliases=aliases or {},
        name=name,
    )(scalar, *(placed(x) for x in operands))


SMEM = pl.BlockSpec(memory_space=pltpu.SMEM)
VMEM = pl.BlockSpec(memory_space=pltpu.VMEM)


def swap(values, axis, bit):
    return lax.ppermute(values, axis, [(i, i ^ bit) for i in range(lax.axis_size(axis))])


def turn(values, axis, step):
    size = lax.axis_size(axis)
    return lax.ppermute(values, axis, [(i, (i + step) % size) for i in range(size)])


def blocks_over(values, axis):
    return lax.all_to_all(values, axis, split_axis=0, concat_axis=0, tiled=True)


def row_of(ref):
    values = ref[...].astype(WIDE)
    return jnp.concatenate([values[at : at + 1] for at in range(values.shape[0])], 1)


def project_pairs_kernel(tokens_ref, gain_ref, key_ref, value_ref, pairs_ref, normed_ref):
    values = tokens_ref[...].astype(WIDE)
    scale = lax.rsqrt(jnp.mean(values * values, axis=-1, keepdims=True) + EPSILON)
    normed = (values * scale * row_of(gain_ref)).astype(LOW)
    normed_ref[...] = normed
    groups, _, width, _ = pairs_ref.shape
    for kind, weight_ref in enumerate((key_ref, value_ref)):
        rows = dot_nn(normed, weight_ref[...]).T
        for group in range(groups):
            pairs_ref[group, kind] = rows[group * width : (group + 1) * width].astype(LOW)


def project_queries_kernel(normed_ref, weight_ref, out_ref):
    rows = dot_nn(normed_ref[...], weight_ref[...]).T
    groups, width, _ = out_ref.shape
    for group in range(groups):
        out_ref[group] = rows[group * width : (group + 1) * width].astype(LOW)


def turn_kernel(normed_ref, out_ref):
    turned = normed_ref[...].astype(WIDE).T.astype(LOW)
    for copy in range(out_ref.shape[0]):
        out_ref[copy] = turned


def strips_kernel(start_ref, table_ref, *refs):
    tiles = (len(refs) - 1) // 2
    bucket_refs, strips_refs, rows_ref = refs[:tiles], refs[tiles : 2 * tiles], refs[-1]
    buckets = table_ref.shape[1]
    for bucket_ref, strips_ref in zip(bucket_refs, strips_refs):
        heads, _, span = strips_ref.shape
        breadth = bucket_ref.shape[1]
        hot = lax.broadcasted_iota(jnp.int32, (buckets, breadth), 0) == bucket_ref[...]
        rows_ref[...] = dot_nn(table_ref[...], hot.astype(WIDE).astype(LOW))
        for head in range(heads):
            row = rows_ref[pl.ds(start_ref[0] + head, 1), :]
            spread = jnp.broadcast_to(row, (STRIP, breadth))
            turned = pltpu.roll(spread, breadth - (STRIP - 1), 1, stride=1, stride_axis=0)
            strips_ref[head] = turned[:, :span]


def make_strips(head_start, table_rows, buckets, heads, after):
    breadth = buckets[0].shape[1]
    return run(
        strips_kernel,
        [kept((heads, STRIP, breadth - STRIP), WIDE)] * len(buckets),
        (head_start, table_rows, *buckets),
        "bias_strips",
        flops=2 * 12 * 32 * breadth,
        in_specs=[SMEM] + [VMEM] * (1 + len(buckets)),
        scratch=[pltpu.VMEM((table_rows.shape[0], breadth), WIDE)],
        after=after,
    )


def head_mask(shape, head):
    lane = lax.broadcasted_iota(jnp.int32, shape, 1)
    return (lane >= head * HEAD_DIM) & (lane < (head + 1) * HEAD_DIM)


def side_by_side(pairs_ref, kind):
    return jnp.concatenate([pairs_ref[group, kind] for group in range(pairs_ref.shape[0])], 1)


def attend_kernel(*refs, heads, rows, tiles, first, last):
    query_ref = refs[0]
    pairs_refs, strips_refs, refs = refs[1 : 1 + tiles], refs[1 + tiles : 1 + 2 * tiles], refs[1 + 2 * tiles :]
    if not first:
        numer_in, total_in = refs[:2]
        refs = refs[2:]
    weight_refs, (total_ref, out_ref) = refs[:tiles], refs[tiles : tiles + 2]
    tile = query_ref.shape[2]
    groups = pairs_refs[0].shape[0]
    step = pl.program_id(0)
    queries = (query_ref[0] * jnp.asarray(0.125, LOW)).astype(WIDE).T.astype(LOW)
    out = jnp.zeros(queries.shape, WIDE)
    sums = jnp.zeros(queries.shape, WIDE)
    for head in range(heads):
        mask = head_mask(queries.shape, head)
        masked = jnp.where(mask, queries, jnp.zeros_like(queries))
        lanes = jnp.zeros((tile, 128), WIDE)
        numerator = jnp.zeros(queries.shape, WIDE)
        for pairs_ref, strips_ref, weight_ref in zip(pairs_refs, strips_refs, weight_refs):
            keys = jnp.concatenate([pairs_ref[group, 0] for group in range(groups)], 1)
            values = jnp.concatenate([pairs_ref[group, 1] for group in range(groups)], 1)
            scores = dot_nn(masked, keys)
            parts = []
            for sub in range(tile // STRIP):
                start = pl.multiple_of(rows - STRIP - (step * tile + sub * STRIP), STRIP)
                parts.append(
                    jnp.exp(
                        scores[sub * STRIP : (sub + 1) * STRIP, :]
                        + strips_ref[head, :, pl.ds(start, rows)]
                    )
                )
            weights = jnp.concatenate(parts, 0)
            for lane in range(rows // 128):
                lanes = lanes + weights[:, lane * 128 : (lane + 1) * 128]
            low = weights.astype(LOW)
            weight_ref[head] = low
            numerator = numerator + dot_nt(low, values)
        total = jnp.sum(lanes, axis=1, keepdims=True)
        out = jnp.where(mask, numerator, out)
        sums = jnp.where(mask, total, sums)
    out, sums = out.T, sums.T
    if not first:
        out = out + numer_in[0]
        sums = sums + total_in[0]
    total_ref[0] = sums
    if last:
        out = out / sums
        refs[-1][0] = out.astype(LOW)
    out_ref[0] = out


def gate(values, after):
    return pl.pallas_call(
        lambda *refs: None,
        out_shape=jax.ShapeDtypeStruct(values.shape, values.dtype),
        in_specs=[pl.BlockSpec(memory_space=pl.ANY)] + [unread(x) for x in after],
        out_specs=pl.BlockSpec(memory_space=pl.ANY),
        input_output_aliases={0: 0},
        name="gate",
    )(values, *(placed(x) for x in after))


def attend(queries, pairs, strips, before, last):
    groups, width, tile = queries.shape
    rows = groups * tile
    heads = width // HEAD_DIM
    tiles = len(pairs)
    block = pl.BlockSpec((1, width, tile), lambda i: (i, 0, 0))
    weight_block = pl.BlockSpec((heads, tile, rows), lambda i: (0, i, 0))
    operands = (queries, *(loose(x) for x in pairs), *(near(x) for x in strips), *before)
    return run(
        functools.partial(attend_kernel, heads=heads, rows=rows, tiles=tiles, first=not before, last=last),
        [shaped((heads, rows, rows), LOW)] * tiles
        + [shaped(queries.shape, WIDE)] * 2
        + [shaped(queries.shape, LOW)] * last,
        operands,
        "attend",
        flops=16 * width * rows * rows * tiles,
        grid=(groups,),
        in_specs=[block]
        + [fixed(x.shape) for x in pairs]
        + [fixed(x.shape) for x in strips]
        + [block] * len(before),
        out_specs=[weight_block] * tiles + [block] * (2 + last),
    )


def attend_back_kernel(*refs, heads, rows, first, last, begin):
    query_ref, grad_ref, att_ref, total_ref, weight_ref, pairs_ref = refs[:6]
    refs = refs[6:]
    if not first:
        query_in = refs[0]
        refs = refs[1:]
    query_back_ref, pairs_back_ref, diagonal_ref, strips_ref, key_acc, value_acc = refs
    tile = query_ref.shape[2]
    groups, _, width, chunk = pairs_back_ref.shape
    span = strips_ref.shape[2]
    step = pl.program_id(0)
    block = step + begin

    @pl.when(step == 0)
    def _():
        strips_ref[...] = jnp.zeros_like(strips_ref)
        key_acc[...] = jnp.zeros_like(key_acc)
        value_acc[...] = jnp.zeros_like(value_acc)

    query_turned = query_ref[0] * jnp.asarray(0.125, LOW)
    grads = grad_ref[0].astype(WIDE)
    inverse = 1.0 / total_ref[0]
    numer_wide = grads * inverse
    numer_turned = numer_wide.astype(LOW)
    products = -(numer_wide * att_ref[0]).T
    numer_back = numer_turned.astype(WIDE).T.astype(LOW)
    out = jnp.zeros(numer_back.shape, WIDE)
    keys = side_by_side(pairs_ref, 0)
    values = side_by_side(pairs_ref, 1)
    for head in range(heads):
        mask = head_mask(numer_back.shape, head)
        masked = jnp.where(mask, numer_back, jnp.zeros_like(numer_back))
        denom_back = jnp.sum(jnp.where(mask, products, 0.0), axis=1, keepdims=True)
        here = slice(head * HEAD_DIM, (head + 1) * HEAD_DIM)
        query_here = query_turned[here]
        numer_here = numer_turned[here]
        weight_back = dot_nn(masked, values)
        weights = weight_ref[head]
        score_back = weights.astype(WIDE) * (weight_back + denom_back)
        low = score_back.astype(LOW)
        for sub in range(tile // STRIP):
            start = pl.multiple_of(rows - STRIP - (block * tile + sub * STRIP), STRIP)
            strips_ref[head, :, pl.ds(start, rows)] += score_back[sub * STRIP : (sub + 1) * STRIP, :]
        key_acc[here, :] += dot_nn(query_here, low)
        value_acc[here, :] += dot_nn(numer_here, weights)
        query_back = dot_nt(low, keys)
        out = jnp.where(mask, query_back * 0.125, out)
    out = out.T
    if not first:
        out = out + query_in[0]
    query_back_ref[0] = out.astype(query_back_ref.dtype)

    @pl.when(step == pl.num_programs(0) - 1)
    def _():
        for group in range(groups):
            at = group * chunk
            pairs_back_ref[group, 0] = key_acc[:, at : at + chunk].astype(pairs_back_ref.dtype)
            pairs_back_ref[group, 1] = value_acc[:, at : at + chunk].astype(pairs_back_ref.dtype)
        diagonal_ref[...] = jnp.zeros_like(diagonal_ref)
        for head in range(heads):
            folded = strips_ref[head]
            size = STRIP
            while size > 8:
                size //= 2
                folded = folded[:size] + pltpu.roll(folded[size:], span - size, 1)
            row = folded[0:1]
            for place in range(1, 8):
                row = row + pltpu.roll(folded[place : place + 1], span - place, 1)
            diagonal_ref[head : head + 1, :] = pltpu.roll(row, STRIP - 1, 1)

def attend_back(
    queries, grads, attended, total, weights, pairs, before, last, begin, count, after
):
    groups, width, tile = queries.shape
    rows = groups * tile
    heads = width // HEAD_DIM
    span = 2 * rows
    block = pl.BlockSpec((1, width, tile), lambda i: (i + begin, 0, 0))
    out_block = pl.BlockSpec((1, width, tile), lambda i: (i, 0, 0))
    operands = (queries, grads, attended, total, weights, pairs, *before)
    return run(
        functools.partial(attend_back_kernel, heads=heads, rows=rows, first=not before, last=last, begin=begin),
        [
            shaped((count, width, tile), LOW if last else WIDE),
            shaped(pairs.shape, WIDE if last else LOW),
            shaped((8, span), WIDE),
        ],
        operands,
        "attend_back",
        flops=8 * width * rows * rows * count,
        grid=(count,),
        in_specs=[block, block, block, block]
        + [pl.BlockSpec((heads, tile, rows), lambda i: (0, i + begin, 0)), fixed(pairs.shape)]
        + [block] * len(before),
        out_specs=[out_block, fixed(pairs.shape), fixed((8, span))],
        scratch=[pltpu.VMEM((heads, STRIP, span), WIDE), pltpu.VMEM((width, rows), WIDE), pltpu.VMEM((width, rows), WIDE)], after=after)


def hot_rows(place_row, slots):
    tokens = place_row.shape[1]
    hot = lax.broadcasted_iota(jnp.int32, (slots, tokens), 0) == place_row
    return hot.astype(WIDE).astype(LOW)


def hot_columns(place_column, slots):
    tokens = place_column.shape[0]
    hot = lax.broadcasted_iota(jnp.int32, (tokens, slots), 1) == place_column
    return hot.astype(WIDE).astype(LOW)


def scatter_kernel(place_ref, rows_ref, slots_ref):
    hot = hot_rows(place_ref[...], slots_ref.shape[0])
    slots_ref[...] = dot_nn(hot, rows_ref[...]).astype(LOW)


def middle_kernel(
    att_ref, tokens_ref, weight_ref, gain_ref, place_ref, residual_ref, normed_ref, slots_ref
):
    residual = tokens_ref[...].astype(WIDE) + dot_tn(att_ref[...], weight_ref[...])
    residual_ref[...] = residual
    scale = lax.rsqrt(jnp.mean(residual * residual, axis=-1, keepdims=True) + EPSILON)
    normed = (residual * scale * row_of(gain_ref)).astype(LOW)
    normed_ref[...] = normed
    hot = hot_rows(place_ref[...], slots_ref.shape[0])
    slots_ref[...] = dot_nn(hot, normed).astype(LOW)


def route(normed, router, experts):
    logits = dot_nn(normed, router)
    lane = lax.broadcasted_iota(jnp.int32, logits.shape, 1)
    logits = jnp.where(lane < experts, logits, -jnp.inf)
    powers = jnp.exp(logits - jnp.max(logits, axis=-1, keepdims=True))
    return powers / jnp.sum(powers, axis=-1, keepdims=True), lane


def shard_copy(weight_refs, buffer_ref, semaphores, at):
    return pltpu.make_async_copy(weight_refs[at], buffer_ref.at[at % 2], semaphores.at[at % 2])


def take_shard(weight_refs, buffer_ref, semaphores):
    step = pl.program_id(0)

    @pl.when(step == 0)
    def _():
        for at in range(min(2, len(weight_refs))):
            shard_copy(weight_refs, buffer_ref, semaphores, at).start()

    for at in range(len(weight_refs)):

        @pl.when(step == at)
        def _(at=at):
            shard_copy(weight_refs, buffer_ref, semaphores, at).wait()

    return lax.rem(step, 2)


def next_shard(weight_refs, buffer_ref, semaphores):
    for at in range(len(weight_refs) - 2):

        @pl.when(pl.program_id(0) == at)
        def _(at=at):
            shard_copy(weight_refs, buffer_ref, semaphores, at + 2).start()


def shard_scratch(weights):
    return [pltpu.VMEM((2, *weights[0].shape), LOW), pltpu.SemaphoreType.DMA((2,))]


def shard_places(weights):
    return [pl.BlockSpec(memory_space=pltpu.HBM)] * len(weights)


def raw_back_kernel(up_ref, *refs):
    *weight_refs, raw_ref, buffer_ref, semaphores = refs
    slot = take_shard(weight_refs, buffer_ref, semaphores)
    raw_ref[...] = dot_nt(up_ref[...], buffer_ref[slot]).astype(LOW)
    next_shard(weight_refs, buffer_ref, semaphores)


def expert_kernel(own_ref, rows_ref, up_ref, router_ref, raw_ref, *refs, experts):
    *weight_refs, act_ref, pre_ref, home_ref, out_back_ref, logit_ref = refs[:-5]
    back_acc, gate_acc, gate_ref, buffer_ref, semaphores = refs[-5:]
    slot = take_shard(weight_refs, buffer_ref, semaphores)
    step = pl.program_id(0)
    rows = rows_ref[...]

    @pl.when(step == 0)
    def _():
        probs, lane = route(rows, router_ref[...], experts)
        hot = (lane == own_ref[0]).astype(WIDE)
        gate = jnp.sum(probs * hot, axis=-1, keepdims=True)
        gate_ref[...] = jnp.broadcast_to(gate, gate_ref.shape)
        out_back_ref[...] = (gate * up_ref[...].astype(WIDE)).astype(LOW)
        back_acc[...] = jnp.zeros_like(back_acc)
        gate_acc[...] = jnp.zeros_like(gate_acc)

    gate = gate_ref[:, 0:1]
    lanes = gate_acc[...]
    back = back_acc[...]
    root = 0.7978845608028654
    hidden = buffer_ref.shape[2]
    size = 256 if hidden % 256 == 0 else 128
    count = hidden // size
    following = dot_nn(rows, buffer_ref[slot, :, 0:size])
    for piece in range(count):
        here = slice(piece * size, (piece + 1) * size)
        value = following
        if piece + 1 < count:
            following = dot_nn(rows, buffer_ref[slot, :, (piece + 1) * size : (piece + 2) * size])
        squared = value * value
        tilted = jnp.tanh(value * (root + (root * 0.044715) * squared))
        share = 0.5 + 0.5 * tilted
        wide = value * share
        act = wide.astype(LOW)
        slope = share + wide * (1.0 - share) * (2.0 * root + (6.0 * root * 0.044715) * squared)
        raw = raw_ref[:, here].astype(WIDE)
        pre = (gate * raw * slope).astype(LOW)
        act_ref[:, here] = act
        pre_ref[:, here] = pre
        back = back + dot_nt(pre, buffer_ref[slot, :, here])
        shares = act.astype(WIDE) * raw
        for lane in range(size // 128):
            lanes = lanes + shares[:, lane * 128 : (lane + 1) * 128]
    gate_acc[...] = lanes
    back_acc[...] = back
    next_shard(weight_refs, buffer_ref, semaphores)

    @pl.when(step == pl.num_programs(0) - 1)
    def _():
        probs, lane = route(rows, router_ref[...], experts)
        hot = (lane == own_ref[0]).astype(WIDE)
        gate = jnp.sum(probs * hot, axis=-1, keepdims=True)
        gate_back = jnp.sum(gate_acc[...], axis=-1, keepdims=True)
        logit_back = (probs * gate_back * (hot - gate)).astype(LOW)
        logit_ref[...] = logit_back
        home_ref[...] = (dot_nt(logit_back, router_ref[...]) + back_acc[...]).astype(LOW)


def store_half(former_ref, latter_ref, keep_ref, send_ref):
    count = pl.num_programs(0) // 2

    @pl.when(pl.program_id(0) < count)
    def _():
        send_ref[0] = dot_tn(former_ref[...], latter_ref[...]).astype(LOW)

    @pl.when(pl.program_id(0) >= count)
    def _():
        keep_ref[0] = dot_tn(former_ref[...], latter_ref[...]).astype(LOW)


def shard_at(i, shares):
    count = shares // 2
    return jnp.where(i < count, 2 * i + 1, 2 * (i - count))


def keep_spec(shape, shares):
    return pl.BlockSpec((1, *shape), lambda i: (jnp.maximum(i - shares // 2, 0), 0, 0))


def send_spec(shape, shares):
    return pl.BlockSpec((1, *shape), lambda i: (jnp.minimum(i, shares // 2 - 1), 0, 0))


def inner_grads_kernel(rows_ref, pre_ref, logit_ref, keep_ref, send_ref, router_ref):
    store_half(rows_ref, pre_ref, keep_ref, send_ref)

    @pl.when(pl.program_id(0) == 0)
    def _():
        router_ref[...] = dot_tn(logit_ref[...], rows_ref[...])[: router_ref.shape[0]]


def outer_grads_kernel(act_ref, out_back_ref, *refs):
    *weight_refs, keep_ref, send_ref, out_ref, total_ref, buffer_ref, semaphores = refs
    step = pl.program_id(0)
    slot = take_shard(weight_refs, buffer_ref, semaphores)

    @pl.when(step == 0)
    def _():
        total_ref[...] = jnp.zeros_like(total_ref)

    store_half(act_ref, out_back_ref, keep_ref, send_ref)
    total_ref[...] += dot_nn(act_ref[...], buffer_ref[slot])
    next_shard(weight_refs, buffer_ref, semaphores)

    @pl.when(step == pl.num_programs(0) - 1)
    def _():
        out_ref[...] = total_ref[...].astype(LOW)


def add_shards_kernel(*refs, count):
    operands, outs = refs[:count], refs[count:]
    total = operands[0][0].astype(WIDE)
    for operand in operands[1:]:
        total += operand[0].astype(WIDE)
    if len(outs) == 1:
        outs[0][0] = total.astype(outs[0].dtype)
        return
    half = pl.num_programs(1) // 2
    for place, out_ref in enumerate(outs):

        @pl.when(pl.program_id(1) // half == place)
        def _(out_ref=out_ref):
            out_ref[0] = total.astype(out_ref.dtype)


def add_shards(operands, start, count, kind, parts, name, after=()):
    _, rows, columns = operands[0].shape
    tile = rows // 2 if rows % 32 == 0 else rows
    steps = rows // tile
    parts = parts if steps % 2 == 0 else 1
    half = steps // parts
    block = pl.BlockSpec((1, tile, columns), lambda i, j: (start + i, j, 0))

    def out_block(place):
        last = half - 1
        return pl.BlockSpec(
            (1, tile, columns), lambda i, j: (i, jnp.clip(j - place * half, 0, last), 0)
        )

    return run(
        functools.partial(add_shards_kernel, count=len(operands)),
        [shaped((count, rows // parts, columns), kind)] * parts,
        (operands[0], *(loose(x) for x in operands[1:])),
        name,
        flops=0,
        grid=(count, steps),
        in_specs=[block] * len(operands),
        out_specs=[out_block(place) for place in range(parts)],
        after=after,
    )


def gather_shards(keep, send):
    operands = [keep, swap(send, "dp", 1)]
    size = keep.shape[0]
    while size > 2:
        half = size // 2
        gone = add_shards(operands, half, half, LOW, 1, "add_shards")
        operands.append(swap(gone[0], "dp", 2 * half))
        size = half
    gone = add_shards(operands, 1, 1, LOW, 1, "add_shards")
    return operands, [swap(part, "dp", 2) for part in gone], gone[0]


def finish_kernel(*refs, count, steps):
    former_refs, came_refs, (out_ref, mark_ref) = refs[:count], refs[count:-2], refs[-2:]
    total = former_refs[0][0].astype(WIDE)
    for former_ref in former_refs[1:]:
        total += former_ref[0].astype(WIDE)
    half = steps // len(came_refs)
    for place, came_ref in enumerate(came_refs):

        @pl.when(pl.program_id(0) // half == place)
        def _(came_ref=came_ref):
            out_ref[...] = total + came_ref[0].astype(WIDE)

    mark_ref[...] = jnp.zeros_like(mark_ref)


def finish_shards(formers, came):
    _, rows, columns = formers[0].shape
    tile = rows // 2 if rows % 32 == 0 else rows
    steps = rows // tile
    half = steps // len(came)
    block = pl.BlockSpec((1, tile, columns), lambda i: (0, i, 0))
    parts = [
        pl.BlockSpec(
            (1, tile, columns), lambda i, place=place: (0, jnp.clip(i - place * half, 0, half - 1), 0)
        )
        for place in range(len(came))
    ]
    return run(
        functools.partial(finish_kernel, count=len(formers), steps=steps),
        [shaped((rows, columns), WIDE), shaped((8, 128), WIDE)],
        (formers[0], *(loose(x) for x in (*formers[1:], *came))),
        "finish_shards",
        flops=0,
        grid=(steps,),
        in_specs=[block] * len(formers) + parts,
        out_specs=[pl.BlockSpec((tile, columns), lambda i: (i, 0)), fixed((8, 128))],
    )


def after_kernel(
    home_ref,
    place_ref,
    residual_ref,
    gain_ref,
    upstream_ref,
    weight_ref,
    att_back_ref,
    residual_back_ref,
    branch_ref,
    gain_back_ref,
):
    hot = hot_columns(place_ref[...], home_ref.shape[0])
    normed_back = dot_nn(hot, home_ref[...])
    residual = residual_ref[...]
    scale = lax.rsqrt(jnp.mean(residual * residual, axis=-1, keepdims=True) + EPSILON)
    spread = residual * scale
    gained = row_of(gain_ref) * normed_back
    inner = jnp.mean(gained * spread, axis=-1, keepdims=True)
    back = upstream_ref[...].astype(WIDE) + scale * (gained - spread * inner)
    residual_back_ref[...] = back
    branch = back.astype(LOW)
    branch_ref[...] = branch
    gain_back_ref[...] = jnp.broadcast_to(
        jnp.sum(normed_back * spread, axis=0, keepdims=True), gain_back_ref.shape
    )
    att_back_ref[...] = dot_nt(weight_ref[...], branch).astype(LOW)


def output_pieces_kernel(core_ref, att_ref, branch_ref, router_ref, gain_ref, *refs, owners):
    *out_refs, full_ref = refs
    grad = dot_nn(att_ref[...], branch_ref[...])
    own = grad.shape[0] // owners
    height = full_ref.shape[0] // owners
    full_ref[...] = jnp.zeros_like(full_ref)
    for owner in range(owners):
        full_ref[owner * height : owner * height + own, :] = grad[owner * own : (owner + 1) * own]
    at = own + router_ref.shape[0]
    full_ref[own:at, :] = router_ref[...]
    full_ref[at : at + 8, :] = gain_ref[...]
    for place, out_ref in enumerate(out_refs):
        height = out_ref.shape[0]
        start = pl.multiple_of(jnp.bitwise_xor(core_ref[0], place) * height, height)
        out_ref[...] = full_ref[pl.ds(start, height), :].astype(out_ref.dtype)


def is_cube():
    return [lax.axis_size(name) for name in ("head", "blk", "dp")] == [4, 2, 4]


def sums_kernel(me_ref, *refs, count):
    operands, outs = refs[: len(refs) - count], refs[len(refs) - count :]
    for place, out_ref in enumerate(outs):
        height = out_ref.shape[0]
        start = pl.multiple_of(jnp.bitwise_xor(me_ref[0], place) * height, height)
        total = operands[0][pl.ds(start, height), :].astype(WIDE)
        for operand in operands[1:]:
            total += operand[pl.ds(start, height), :].astype(WIDE)
        out_ref[...] = total.astype(out_ref.dtype)


def sums(me, operands, count, name, after=()):
    height, breadth = operands[0].shape
    return run(
        functools.partial(sums_kernel, count=count),
        [shaped((height // count, breadth), LOW)] * count,
        (me[None].astype(jnp.int32), operands[0], *(loose(x) for x in operands[1:])),
        name,
        flops=0,
        in_specs=[SMEM] + [VMEM] * len(operands),
        after=after,
    )


def cross(mine, other, name, after=()):
    spot = lax.axis_index("blk") * 2 + lax.axis_index("dp") // 2
    own, along, across, corner = sums(spot, (mine, swap(other, "dp", 1)), 4, name, after)
    diagonal = [(b * 4 + d, (1 - b) * 4 + (d ^ 2)) for b in range(2) for d in range(4)]
    return [
        own,
        swap(across, "blk", 1),
        swap(along, "dp", 2),
        lax.ppermute(corner, ("blk", "dp"), diagonal),
    ]


def output_pieces(att_tok, branch_back, router_back, gain_back):
    model_width, experts = branch_back.shape[1], router_back.shape[0]
    cube = is_cube()
    owners = 8 if cube else 1
    height = owners * -(-(model_width // owners + experts + 8) // 128) * 128
    dp = lax.axis_index("dp")
    count = 2 if cube else 1
    outs = run(
        functools.partial(output_pieces_kernel, owners=owners),
        [shaped((height // count, model_width), LOW if cube else WIDE)] * count,
        (
            ((dp & 1) * (count - 1)).astype(jnp.int32)[None],
            att_tok,
            branch_back,
            router_back,
            gain_back,
        ),
        "output_pieces",
        flops=2 * att_tok.size * model_width,
        in_specs=[SMEM] + [VMEM] * 4,
        scratch=[pltpu.VMEM((height, model_width), WIDE)],
    )
    if not cube:
        return (), (), lax.psum(outs[0], ("head", "blk", "dp"))
    own, *came = cross(*outs, "output_core")
    shares = sums(lax.axis_index("head"), (own, *came), 4, "output_sum")
    arrived = [shares[0]] + [swap(shares[step], "head", step) for step in range(1, 4)]
    return (own,), (shares[0],), arrived


def output_kernel(
    residual_ref, normed_ref, router_ref, chosen_ref, place_ref, slots_ref, out_ref, *, experts
):
    probs, lane = route(normed_ref[...], router_ref[...], experts)
    hot = (lane == chosen_ref[...]).astype(WIDE)
    gate = jnp.sum(probs * hot, axis=-1, keepdims=True)
    expert_out = dot_nn(hot_columns(place_ref[...], slots_ref.shape[0]), slots_ref[...])
    out_ref[...] = (residual_ref[...] + gate * expert_out).astype(LOW)


def tokens_grad_kernel(
    triples_ref,
    query_weight_ref,
    key_weight_ref,
    value_weight_ref,
    tokens_ref,
    gain_ref,
    residual_back_ref,
    out_ref,
):
    groups = triples_ref.shape[0]
    weight_refs = (query_weight_ref, key_weight_ref, value_weight_ref)
    normed_back = jnp.zeros(out_ref.shape[::-1], WIDE)
    for kind, weight_ref in enumerate(weight_refs):
        rows = jnp.concatenate([triples_ref[group, kind] for group in range(groups)], 0)
        normed_back += dot_nn(weight_ref[...], rows)
    normed_back = normed_back.T
    values = tokens_ref[...].astype(WIDE)
    scale = lax.rsqrt(jnp.mean(values * values, axis=-1, keepdims=True) + EPSILON)
    spread = values * scale
    gained = row_of(gain_ref) * normed_back
    inner = jnp.mean(gained * spread, axis=-1, keepdims=True)
    out_ref[...] = (residual_back_ref[...] + scale * (gained - spread * inner)).astype(LOW)


def bucket_sums(diagonal, bucket_row, buckets):
    breadth = bucket_row.shape[1]
    hot = lax.broadcasted_iota(jnp.int32, (buckets, breadth), 0) == bucket_row
    hot = hot.astype(WIDE).astype(LOW)
    high = diagonal.astype(LOW)
    rest = diagonal - high.astype(WIDE)
    middle = rest.astype(LOW)
    small = (rest - middle.astype(WIDE)).astype(LOW)
    return dot_nt(high, hot) + dot_nt(middle, hot) + dot_nt(small, hot)


def side(grads):
    return -(-3 * grads // 128) * 128


def blocks_of(refs):
    return [ref[place] for ref in refs for place in range(ref.shape[0])]


def projection_grads(turned_ref, query_refs, pairs_ref):
    _, width, tokens = query_refs[0].shape
    queries = blocks_of(query_refs)
    groups = len(queries)
    spare = jnp.zeros((side(width) - 3 * width, tokens), LOW)
    total = None
    for group in range(groups):
        rows = [queries[group], pairs_ref[group, 0], pairs_ref[group, 1], spare]
        part = dot_nt(turned_ref[group], jnp.concatenate(rows, 0))
        total = part if total is None else total + part
    return total


def table_sums(diagonal_refs, bucket_refs, buckets):
    table = bucket_sums(diagonal_refs[0][...], bucket_refs[0][...], buckets)
    for diagonal_ref, bucket_ref in zip(diagonal_refs[1:], bucket_refs[1:]):
        table += bucket_sums(diagonal_ref[...], bucket_ref[...], buckets)
    return table


def add_pairs(home_refs):
    total = home_refs[0][...].astype(WIDE)
    for home_ref in home_refs[1:]:
        total += home_ref[...].astype(WIDE)
    return total.astype(LOW)


def triples_kernel(*refs, parts):
    pairs = add_pairs(refs[parts:-1])
    for group, queries in enumerate(blocks_of(refs[:parts])):
        refs[-1][group, 0] = queries
        refs[-1][group, 1] = pairs[group, 0]
        refs[-1][group, 2] = pairs[group, 1]


def pieces_kernel(core_ref, turned_ref, *refs, parts, tiles, buckets):
    query_refs, refs = refs[:parts], refs[parts:]
    home_refs, refs = refs[:tiles], refs[tiles:]
    diagonal_refs, bucket_refs = refs[:tiles], refs[tiles : 2 * tiles]
    *out_refs, pairs_ref, full_ref = refs[2 * tiles :]
    width = query_refs[0].shape[1]
    pairs_ref[...] = add_pairs(home_refs)
    full_ref[...] = projection_grads(turned_ref, query_refs, pairs_ref)
    table = table_sums(diagonal_refs, bucket_refs, buckets)
    full_ref[0:8, 3 * width : 3 * width + buckets] = table
    for place, out_ref in enumerate(out_refs):
        height = out_ref.shape[0]
        start = pl.multiple_of(jnp.bitwise_xor(core_ref[0], place) * height, height)
        out_ref[...] = full_ref[pl.ds(start, height), :].astype(out_ref.dtype)


def join_kernel(*refs):
    *refs, out_ref = refs
    copies, halves, part, _ = out_ref.shape
    count = len(refs) // 2
    columns = refs[0].shape[1]
    total, packed = (
        functools.reduce(jnp.add, [ref[...].astype(WIDE) for ref in group])
        for group in (refs[:count], refs[count:])
    )
    height = packed.shape[0] // halves
    for half in range(halves):
        former = total[half * part : (half + 1) * part].astype(LOW)
        rows = packed[half * height : (half + 1) * height]
        blocks = [rows[:, at : at + 256] for at in range(0, rows.shape[1], 256)]
        latter = jnp.concatenate(blocks, 0).astype(LOW)
        for copy in range(copies):
            out_ref[copy, half, :, :columns] = former
            out_ref[copy, half, :, columns:] = latter


def share_kernel(spot_ref, cases, places, weight_refs, out_refs, sums_ref, table_ref, extra_ref, heads):
    step = pl.program_id(0)
    owner = jnp.bitwise_xor(spot_ref[0], places[0] if len(places) == 1 else place_at(step, places))
    part = out_refs[0].shape[0] // 2
    width = heads * HEAD_DIM
    columns = side(width)
    buckets = table_ref.shape[2]
    for case, pair in enumerate(cases):

        @pl.when(step == case)
        def _(pair=pair):
            for half in range(2):
                ref = pair[half]
                groups = ref.shape[0]
                at = half if ref.shape[1] == 2 else 0
                rows = slice(half * part, (half + 1) * part)

                def tile(group, place, ref=ref, at=at):
                    return ref[group, at, :, place * 128 : (place + 1) * 128].astype(WIDE)

                def turned(group, place, tile=tile):
                    return pltpu.roll(tile(group, place), 64, 1)

                lower = lax.broadcasted_iota(jnp.int32, (part, 128), 1) < 64
                for one in range(0, groups, 2):
                    two = one + 1
                    for kind in range(3):
                        if kind == 1:
                            middle = turned(one, 2)
                            parts = (
                                jnp.where(lower, turned(one, 1), middle),
                                jnp.where(lower, middle, tile(two, 1)),
                                tile(two, 2),
                            )
                        else:
                            place = 3 * kind // 2
                            first = turned(two, place)
                            parts = (
                                tile(one, place),
                                jnp.where(lower, tile(one, place + 1), first),
                                jnp.where(lower, first, turned(two, place + 1)),
                            )
                        for number, values in enumerate(parts):
                            lane = one * width + number * 128
                            out_refs[kind][rows, lane : lane + 128] = values
                for group in range(groups):
                    packed = ref[group, at, :, columns:].astype(WIDE)
                    start = group * 32 + half * 16
                    for number in range(part // 16):
                        lane = number * 256
                        values = packed[number * 16 : (number + 1) * 16]
                        if group + 1 < groups:
                            out_refs[3][start : start + 16, lane : lane + 256] = values
                        else:

                            @pl.when(owner == 0)
                            def _(values=values, half=half, lane=lane):
                                extra_ref[half * 16 : half * 16 + 16, lane : lane + 256] = values

                    if half == 0:

                        @pl.when(owner == 0)
                        def _(group=group, tile=tile):
                            table_ref[group] = tile(group, 4)[:8, 64 : 64 + buckets]

    shares = jnp.zeros((2 * part, 1), WIDE)
    for kind in range(3):
        shares += jnp.sum(
            out_refs[kind][...] * weight_refs[kind][...].astype(WIDE), axis=1, keepdims=True
        )
    shares = jnp.broadcast_to(shares, (2 * part, 128))
    if sums_ref.shape[0] == 2 * part:
        sums_ref[...] = shares
    else:
        sums_ref[pl.ds(owner * 2 * part, 2 * part), :] = shares


def place_at(step, places):
    return sum(jnp.where(step == at, place, 0) for at, place in enumerate(places))


FIRST_PLACES, LAST_PLACES = (0, 1, 2, 4, 5, 6), (3, 7)


def first_shares_kernel(spot_ref, *refs, heads):
    piece_refs, weight_refs, refs = refs[:6], refs[6:9], refs[9:]
    out_refs, (sums_ref, table_ref, extra_ref) = refs[:4], refs[4:]

    @pl.when(pl.program_id(0) == 0)
    def _():
        table_ref[...] = jnp.zeros_like(table_ref)
        extra_ref[...] = jnp.zeros_like(extra_ref)

    cases = [(ref, ref) for ref in piece_refs]
    share_kernel(
        spot_ref, cases, FIRST_PLACES, weight_refs, out_refs, sums_ref, table_ref, extra_ref, heads
    )


def last_shares_kernel(spot_ref, *refs, heads, experts):
    piece_refs, weight_refs, refs = refs[:4], refs[4:7], refs[7:]
    gain_ref, sums_in, table_in, extra_in, *refs = refs
    out_refs, refs = refs[4:8], refs[8:]
    gain_out, second_out, table_out, router_out, sums_ref, table_ref, extra_ref = refs
    step = pl.program_id(0)

    @pl.when(step == 0)
    def _():
        sums_ref[...] = sums_in[...]
        table_ref[...] = table_in[...]
        extra_ref[...] = extra_in[...]

    cases = [(piece_refs[0], piece_refs[1]), (piece_refs[2], piece_refs[3])]
    share_kernel(
        spot_ref, cases, LAST_PLACES, weight_refs, out_refs, sums_ref, table_ref, extra_ref, heads
    )

    @pl.when(step == pl.num_programs(0) - 1)
    def _():
        first = sums_ref[...].T[0:8] / row_of(gain_ref)
        second = extra_ref[experts : experts + 8, :]
        for lane in range(gain_out.shape[0]):
            gain_out[lane : lane + 1, :] = first[0:1, lane * 128 : (lane + 1) * 128]
            second_out[lane : lane + 1, :] = second[0:1, lane * 128 : (lane + 1) * 128]
        router_out[...] = extra_ref[:experts, :]
        for group in range(table_ref.shape[0]):
            table_out[group * heads : (group + 1) * heads, :] = table_ref[group][:heads]


def put_together(me, first, corners, weights, gain, heads, buckets, experts):
    model_width = weights[0].shape[0]
    groups, _, part, _ = first[0].shape

    def rows(places, breadth):
        return pl.BlockSpec(
            (2 * part, breadth), lambda i, me: (place_at(i, places) ^ me[0], 0)
        )

    square = shaped((model_width, model_width), WIDE)
    kept_shapes = [(groups, 8, buckets), (32, model_width)]
    *grads, sums, table, extra = run_with_scalar(
        functools.partial(first_shares_kernel, heads=heads),
        me,
        [square] * 4 + [shaped((model_width, 128), WIDE)] + [shaped(x, WIDE) for x in kept_shapes],
        (*(loose(x) for x in first), *weights),
        "first_shares",
        grid=(len(FIRST_PLACES),),
        in_specs=[fixed(x.shape) for x in first] + [rows(FIRST_PLACES, model_width)] * 3,
        out_specs=[rows(FIRST_PLACES, model_width)] * 4
        + [rows(FIRST_PLACES, 128)]
        + [fixed(x) for x in kept_shapes],
    )
    corners = [gate(array, (table,)) for array in corners]
    last = (*corners, *(swap(array, "dp", 1) for array in corners))
    operands = (*(loose(x) for x in last), *weights, gain, sums, table, extra, *grads)
    vectors = [(model_width // 128, 128)] * 2 + [(groups * heads, buckets), (experts, model_width)]
    count = len(last)
    *grads, shares, second, table, router = run_with_scalar(
        functools.partial(last_shares_kernel, heads=heads, experts=experts),
        me,
        [square] * 4 + [shaped(x, WIDE) for x in vectors],
        operands,
        "last_shares",
        grid=(len(LAST_PLACES),),
        in_specs=[fixed(x.shape) for x in last]
        + [rows(LAST_PLACES, model_width)] * 3
        + [fixed(x.shape) for x in operands[count + 3 : count + 7]]
        + [pl.BlockSpec(memory_space=pltpu.HBM)] * 4,
        out_specs=[rows(LAST_PLACES, model_width)] * 4 + [fixed(x) for x in vectors],
        scratch=[pltpu.VMEM((model_width, 128), WIDE)] + [pltpu.VMEM(x, WIDE) for x in kept_shapes],
        aliases={count + 8 + i: i for i in range(4)},
    )
    query_grad, key_grad, value_grad, output_grad = grads
    return (
        query_grad,
        key_grad,
        value_grad,
        shares.reshape(-1),
        table.T,
        output_grad,
        router.T,
        second.reshape(-1),
    )


def take_half_kernel(values_ref, out_ref):
    out_ref[...] = values_ref[...]


def take_half(values, half):
    groups, _, *rest = values.shape
    return pl.pallas_call(
        take_half_kernel,
        out_shape=pltpu.HBM((groups, 1, *rest), values.dtype),
        grid=(groups,),
        in_specs=[pl.BlockSpec((1, 1, *rest), lambda i: (i, half, 0, 0))],
        out_specs=pl.BlockSpec((1, 1, *rest), lambda i: (i, 0, 0, 0)),
        compiler_params=pltpu.CompilerParams(vmem_limit_bytes=VMEM_BYTES),
        name="take_half",
    )(values)


def weight_sums(
    turned, query_backs, home, diagonals, bucket_rows, buckets, weights, gain, experts, packed, middle, late
):
    groups, model_width, _ = turned.shape
    width = query_backs[0].shape[1]
    heads = width // HEAD_DIM
    tiles = len(diagonals)
    cube = is_cube()
    columns = side(width)
    dp, blk = lax.axis_index("dp"), lax.axis_index("blk")
    count = 2 if cube else 1
    pieces = run(
        functools.partial(pieces_kernel, parts=len(query_backs), tiles=tiles, buckets=buckets),
        [shaped((model_width // count, columns), LOW if cube else WIDE)] * count,
        (
            ((dp & 1) * (count - 1)).astype(jnp.int32)[None],
            near(turned),
            *query_backs,
            *received_loose(home),
            *diagonals,
            *bucket_rows,
        ),
        "projection_pieces",
        flops=6 * turned.size * width,
        in_specs=[SMEM] + [VMEM] * (1 + len(query_backs) + 3 * tiles),
        scratch=[pltpu.VMEM(home[0].shape, LOW), pltpu.VMEM((model_width, columns), WIDE)],
    )
    if not cube:
        sums = lax.psum(pieces[0], ("blk", "dp"))
        table = lax.all_gather(
            sums[:heads, 3 * width : 3 * width + buckets], "head", axis=0, tiled=True
        )
        grads = sums[:, : 3 * width].reshape(model_width, 3, width)
        grads = lax.all_gather(grads, "head", axis=2, tiled=True)
        grads = [grads[:, i] for i in range(3)]
        shares = sum(jnp.sum(x * y.astype(WIDE), axis=1) for x, y in zip(grads, weights))
        rest = packed[model_width:]
        shares = shares / gain.reshape(-1).astype(WIDE)
        packed = packed[:model_width], rest[:experts].T, rest[experts]
        return pieces, *grads, shares, table.T, *packed
    part = model_width // 16
    copies = run(
        join_kernel,
        [shaped((groups, 2, part, columns + 256), LOW)],
        tuple(loose(x) for x in (*cross(*pieces, "projection_core", middle), *packed)),
        "join",
        flops=0,
        after=late,
    )[0]
    own = blocks_over(copies, "head")
    across, along = swap(own, "blk", 1), swap(own, "dp", 2)
    corners = (
        swap(take_half(across, 0), "dp", 2),
        swap(take_half(along, 1), "blk", 1),
    )
    near_ones = (own, along, across)
    first = (*near_ones, *(swap(array, "dp", 1) for array in near_ones))
    me = ((dp & 1) * 4 + blk * 2 + dp // 2).astype(jnp.int32)[None]
    return pieces, *put_together(me, first, corners, weights, gain, heads, buckets, experts)


def body(
    tokens,
    first_gain,
    query_weight,
    key_weight,
    value_weight,
    output_weight,
    bias_table,
    second_gain,
    router_weight,
    inner_weight,
    outer_weight,
    expert_index,
    capacity_slot,
    bucket_of_offset,
    upstream,
):
    _, token_rows, model_width = tokens.shape
    groups = lax.axis_size("head")
    cycle = lax.axis_size("blk")
    shares = lax.axis_size("dp")
    width = model_width // groups
    heads = width // HEAD_DIM
    local_rows = groups * token_rows
    length = local_rows * cycle
    buckets = bias_table.shape[0]
    experts = router_weight.shape[1]
    capacity = max(2, 2 * token_rows // experts)
    slots = experts * capacity
    token_values, upstream_values = tokens[0], upstream[0]
    gain_one, gain_two = first_gain.reshape(-1, 128), second_gain.reshape(-1, 128)
    chosen = expert_index[0]
    place = chosen * capacity + capacity_slot[0]
    place_row, place_column, chosen_column = place[None], place[:, None], chosen[:, None]
    router = jnp.pad(router_weight, ((0, 0), (0, 128 - experts)))

    inner_shards, outer_shards = [inner_weight[0]], [outer_weight[0]]
    for held in (outer_shards, inner_shards):
        for bit in range(1, shares.bit_length() - 1):
            held += [swap(values, "dp", 1 << bit) for values in held]
    far_inner, far_outer = inner_shards[1:], outer_shards[1:]
    for held in (outer_shards, inner_shards):
        held[:] = [x for values in held for x in (values, swap(values, "dp", 1))]

    square = model_width * model_width
    pairs, normed_one = run(
        project_pairs_kernel,
        [
            shaped((groups, 2, width, token_rows), LOW),
            shaped((token_rows, model_width), LOW),
        ],
        (token_values, gain_one, key_weight, value_weight),
        "project_pairs",
        flops=4 * token_rows * square,
    )
    pairs = blocks_over(pairs, "head")
    head_start = (lax.axis_index("head") * heads).astype(jnp.int32)[None]
    table_rows = jnp.pad(bias_table.T, ((0, -(groups * heads) % 8), (0, 0)))
    bucket_line = jnp.pad(bucket_of_offset, (0, 1))[None]
    blk = lax.axis_index("blk")
    tile_buckets, tile_strips = [], []
    for step in range(cycle):
        number = lax.rem(blk + cycle - step, cycle)
        start = length + (number - blk - 1) * local_rows
        tile_buckets.append(lax.dynamic_slice_in_dim(bucket_line, start, 2 * local_rows, 1))
    tile_pairs = [pairs] + [turn(pairs, "blk", step) for step in range(1, cycle)]
    up_slots = run(
        scatter_kernel,
        [shaped((slots, model_width), LOW)],
        (place_row, upstream_values),
        "scatter_up",
        flops=2 * slots * token_rows * model_width,
        after=(normed_one,),
    )[0]
    turned = run(
        turn_kernel,
        [shaped((groups, model_width, token_rows), LOW)],
        (normed_one,),
        "turn",
        flops=0,
    )[0]
    queries = run(
        project_queries_kernel,
        [shaped((groups, width, token_rows), LOW)],
        (normed_one, query_weight),
        "project_queries",
        flops=2 * token_rows * square,
        after=(up_slots, turned),
    )[0]
    queries = blocks_over(gate(queries, (loose(pairs),)), "head")
    up_rows = blocks_over(up_slots, ("head", "blk"))
    for step in range(0, cycle, 2):
        tile_strips += make_strips(
            head_start, table_rows, tile_buckets[step : step + 2], heads, (queries,)
        )
    tile_weights, before = [], ()
    for step in range(0, cycle, 2):
        tiles = slice(step, step + 2)
        last = step + 2 >= cycle
        results = attend(queries, tile_pairs[tiles], tile_strips[tiles], before, last)
        tile_weights += results[: len(tile_pairs[tiles])]
        total, attended, *rest = results[len(tile_pairs[tiles]) :]
        before = (attended, total)
    attended_low = gate(rest[0], (loose(up_rows),))
    att_tok = blocks_over(attended_low, "head").reshape(model_width, token_rows)
    hidden = inner_shards[0].shape[1]
    full_hidden = shares * hidden
    product = 2 * slots * model_width * full_hidden
    hidden_block = pl.BlockSpec((slots, hidden), lambda i: (0, i))
    turned_block = pl.BlockSpec((slots, hidden), lambda i: (0, shard_at(i, shares)))
    raw = run(
        raw_back_kernel,
        [shaped((slots, full_hidden), LOW)],
        (near(up_rows), *outer_shards),
        "raw_back",
        flops=product,
        grid=(shares,),
        in_specs=[fixed(up_rows.shape)] + shard_places(outer_shards),
        out_specs=[hidden_block],
        scratch=shard_scratch(outer_shards),
    )[0]
    residual_mid, normed_two, normed_slots = run(
        middle_kernel,
        [
            shaped((token_rows, model_width), WIDE),
            shaped((token_rows, model_width), LOW),
            shaped((slots, model_width), LOW),
        ],
        (near(att_tok), token_values, output_weight, gain_two, place_row),
        "middle",
        flops=2 * token_rows * square + 2 * slots * token_rows * model_width,
        after=(raw, router, *far_inner),
    )
    expert_rows = blocks_over(normed_slots, ("head", "blk"))
    own_expert = (lax.axis_index("head") * cycle + blk).astype(jnp.int32)[None]
    hidden_act, pre_back, home_slots, out_back, logit_back = run(
        functools.partial(expert_kernel, experts=experts),
        [
            shaped((slots, full_hidden), LOW),
            shaped((slots, full_hidden), LOW),
            shaped((slots, model_width), LOW),
            shaped((slots, model_width), LOW),
            shaped((slots, 128), LOW),
        ],
        (own_expert, near(expert_rows), near(up_rows), router, raw, *inner_shards),
        "expert",
        flops=2 * product,
        grid=(shares,),
        in_specs=[
            SMEM,
            fixed(expert_rows.shape),
            fixed(up_rows.shape),
            fixed(router.shape),
            hidden_block,
            *shard_places(inner_shards),
        ],
        out_specs=[
            hidden_block,
            hidden_block,
            fixed((slots, model_width)),
            fixed((slots, model_width)),
            fixed((slots, 128)),
        ],
        scratch=[
            pltpu.VMEM((slots, model_width), WIDE),
            pltpu.VMEM((slots, 128), WIDE),
            pltpu.VMEM((slots, 128), WIDE),
            *shard_scratch(inner_shards),
        ],
    )
    home_rows = blocks_over(home_slots, ("head", "blk"))
    inner_shape, outer_shape = (model_width, hidden), (hidden, model_width)
    inner_keep, inner_send, router_back = run(
        inner_grads_kernel,
        [shaped((shares // 2, *inner_shape), LOW)] * 2 + [shaped((experts, model_width), WIDE)],
        (near(expert_rows), pre_back, logit_back),
        "inner_grads",
        flops=product,
        grid=(shares,),
        in_specs=[fixed(expert_rows.shape), turned_block, fixed(logit_back.shape)],
        out_specs=[
            keep_spec(inner_shape, shares),
            send_spec(inner_shape, shares),
            fixed((experts, model_width)),
        ],
    )
    turned_shards = outer_shards[1::2] + outer_shards[0::2]
    outer_keep, outer_send, expert_out = run(
        outer_grads_kernel,
        [shaped((shares // 2, *outer_shape), LOW)] * 2 + [shaped((slots, model_width), LOW)],
        (hidden_act, out_back, *turned_shards),
        "outer_grads",
        flops=2 * product,
        grid=(shares,),
        in_specs=[turned_block, fixed(out_back.shape)] + shard_places(outer_shards),
        out_specs=[
            keep_spec(outer_shape, shares),
            send_spec(outer_shape, shares),
            fixed((slots, model_width)),
        ],
        scratch=[pltpu.VMEM((slots, model_width), WIDE)] + shard_scratch(outer_shards),
    )
    att_back, residual_back, branch_back, gain_back = run(
        after_kernel,
        [
            shaped((model_width, token_rows), LOW),
            shaped((token_rows, model_width), WIDE),
            shaped((token_rows, model_width), LOW),
            shaped((8, model_width), WIDE),
        ],
        (near(home_rows), place_column, residual_mid, gain_two, upstream_values, output_weight),
        "after",
        flops=2 * token_rows * square + 2 * slots * token_rows * model_width,
        after=(router_back, expert_out),
    )
    head_back = blocks_over(att_back.reshape(groups, width, token_rows), "head")
    packed_core, packed_sum, packed_shares = output_pieces(
        att_tok, branch_back, router_back, gain_back
    )
    *inner_parts, inner_gone = gather_shards(inner_keep, gate(inner_send, (att_back,)))
    *outer_parts, outer_gone = gather_shards(outer_keep, gate(outer_send, (att_back,)))
    turned = gate(turned, (head_back, *packed_core, inner_gone, outer_gone))
    turned_all = blocks_over(turned, "head")

    before, diagonals, home, query_backs = (), [], [], []
    for step in range(1, cycle):
        query_back, pairs_part, diagonal = attend_back(
            queries,
            head_back,
            attended,
            total,
            tile_weights[step],
            tile_pairs[step],
            before,
            False,
            0,
            groups,
            (),
        )
        before = (query_back,)
        diagonals.append(diagonal)
        home.append(turn(pairs_part, "blk", cycle - step))
    cut = groups - 1
    for begin, count, after in (
        (0, cut, packed_sum),
        (cut, groups - cut, tuple(loose(x) for x in (turned_all, *home[:1], *inner_parts[1]))),
    ):
        query_back, pairs_part, diagonal = attend_back(
            queries,
            head_back,
            attended,
            total,
            tile_weights[0],
            tile_pairs[0],
            before,
            True,
            begin,
            count,
            after,
        )
        query_backs.append(query_back)
        if begin == 0:
            out_rows = blocks_over(gate(expert_out, (loose(turned_all), query_back)), ("head", "blk"))
        diagonals.append(diagonal)
        home.append(pairs_part)
    diagonal_buckets = [*tile_buckets[1:], tile_buckets[0], tile_buckets[0]]
    layer_output = run(
        functools.partial(output_kernel, experts=experts),
        [shaped((token_rows, model_width), LOW)],
        (residual_mid, normed_two, router, chosen_column, place_column, loose(out_rows)),
        "layer_output",
        flops=2 * slots * token_rows * model_width,
    )[0]
    (
        pieces,
        query_grad,
        key_grad,
        value_grad,
        first_gain_grad,
        table_grad,
        output_grad,
        router_grad,
        second_gain_grad,
    ) = weight_sums(
        turned_all,
        query_backs,
        home,
        diagonals,
        diagonal_buckets,
        buckets,
        (query_weight, key_weight, value_weight),
        gain_one,
        experts,
        packed_shares,
        (loose(out_rows),),
        (*(loose(x) for x in outer_parts[1]), layer_output),
    )
    inner_part, inner_mark = finish_shards(*inner_parts)
    outer_part, outer_mark = finish_shards(*outer_parts)
    triples = run(
        functools.partial(triples_kernel, parts=len(query_backs)),
        [shaped((groups, 3, width, token_rows), LOW)],
        (*query_backs, *received_loose(home)),
        "triples",
        flops=0,
        after=(pieces[0], inner_mark, outer_mark),
    )[0]
    triples_tok = blocks_over(triples, "head")
    tokens_grad = run(
        tokens_grad_kernel,
        [shaped((token_rows, model_width), LOW)],
        (
            loose(triples_tok),
            query_weight,
            key_weight,
            value_weight,
            token_values,
            gain_one,
            residual_back,
        ),
        "tokens_grad",
        flops=6 * token_rows * square,
    )[0]
    return (
        layer_output[None],
        tokens_grad[None],
        first_gain_grad,
        query_grad,
        key_grad,
        value_grad,
        output_grad,
        table_grad,
        second_gain_grad,
        router_grad,
        inner_part[None],
        outer_part[None],
    )


def solution(mesh):
    return jax.shard_map(
        body,
        mesh=mesh,
        in_specs=(
            P("dp", ("blk", "head"), None),
            P(),
            P(),
            P(),
            P(),
            P(),
            P(),
            P(),
            P(),
            P(("head", "blk"), None, "dp"),
            P(("head", "blk"), "dp", None),
            P("dp", ("blk", "head")),
            P("dp", ("blk", "head")),
            P(),
            P("dp", ("blk", "head"), None),
        ),
        out_specs=(
            P("dp", ("blk", "head"), None),
            P("dp", ("blk", "head"), None),
            P(),
            P(),
            P(),
            P(),
            P(),
            P(),
            P(),
            P(),
            P(("head", "blk"), None, "dp"),
            P(("head", "blk"), "dp", None),
        ),
        check_vma=False,
    )
```

```python
import functools
import math

import jax
import jax.numpy as jnp
from jax import lax
from jax.experimental import pallas as pl
from jax.experimental.pallas import tpu as pltpu
from jax.sharding import PartitionSpec as P

HEAD_DIM = 64
EPSILON = 1e-06
STRIP = 128
VMEM_BYTES = 28 * 2**20
LOW = jnp.bfloat16
WIDE = jnp.float32


def dot_nt(former, latter):
    return lax.dot_general(former, latter, (((1,), (1,)), ((), ())), preferred_element_type=WIDE)


def dot_nn(former, latter):
    return lax.dot_general(former, latter, (((1,), (0,)), ((), ())), preferred_element_type=WIDE)


def dot_tn(former, latter):
    return lax.dot_general(former, latter, (((0,), (0,)), ((), ())), preferred_element_type=WIDE)


def shaped(shape, kind):
    return pltpu.HBM(tuple(shape), kind)


def kept(shape, kind):
    return pltpu.VMEM(tuple(shape), kind)


class Near:
    def __init__(self, values):
        self.values, self.shape, self.dtype = values, values.shape, values.dtype


def near(values):
    return Near(values)


class Loose(Near):
    pass


def loose(values):
    return Loose(values)


def fixed(shape):
    return pl.BlockSpec(tuple(shape), lambda *_: (0,) * len(shape), pipeline_mode=pl.Buffered(1))


def received_loose(home):
    return [loose(x) if x.dtype == LOW else x for x in home]


def placed(values):
    if isinstance(values, Loose):
        return values.values
    if isinstance(values, Near):
        return pltpu.with_memory_space_constraint(values.values, pltpu.VMEM)
    return pltpu.with_memory_space_constraint(values, pltpu.HBM)


def unread(values):
    return pl.BlockSpec(memory_space=pl.ANY if isinstance(values, Loose) else pltpu.HBM)


def run(
    kernel, outs, operands, name, flops, grid=None, in_specs=None, out_specs=None, scratch=(), after=()
):
    moved = sum(math.prod(x.shape) * jnp.dtype(x.dtype).itemsize for x in (*operands, *outs))
    count, skipped = len(operands), len(after)
    if grid is None:
        grid = (1,)
        out_specs = [fixed(x.shape) for x in outs]
    if in_specs is None:
        in_specs = [VMEM] * count
    in_specs = [fixed(x.shape) if spec is VMEM else spec for x, spec in zip(operands, in_specs)]

    def body(*refs):
        kernel(*refs[:count], *refs[count + skipped :])

    return pl.pallas_call(
        body,
        out_shape=list(outs),
        grid=grid,
        in_specs=in_specs + [unread(x) for x in after],
        out_specs=out_specs,
        scratch_shapes=list(scratch),
        compiler_params=pltpu.CompilerParams(vmem_limit_bytes=VMEM_BYTES),
        cost_estimate=pl.CostEstimate(flops=flops, bytes_accessed=moved, transcendentals=0),
        name=name,
    )(
        *(x if spec is SMEM else placed(x) for x, spec in zip(operands, in_specs)),
        *(placed(x) for x in after),
    )


def run_with_scalar(
    kernel, scalar, outs, operands, name, grid, in_specs, out_specs, scratch=(), aliases=None
):
    return pl.pallas_call(
        kernel,
        out_shape=list(outs),
        grid_spec=pltpu.PrefetchScalarGridSpec(
            num_scalar_prefetch=1,
            grid=grid,
            in_specs=in_specs,
            out_specs=out_specs,
            scratch_shapes=list(scratch),
        ),
        compiler_params=pltpu.CompilerParams(vmem_limit_bytes=VMEM_BYTES),
        input_output_aliases=aliases or {},
        name=name,
    )(scalar, *(placed(x) for x in operands))


SMEM = pl.BlockSpec(memory_space=pltpu.SMEM)
VMEM = pl.BlockSpec(memory_space=pltpu.VMEM)


def swap(values, axis, bit):
    return lax.ppermute(values, axis, [(i, i ^ bit) for i in range(lax.axis_size(axis))])


def turn(values, axis, step):
    size = lax.axis_size(axis)
    return lax.ppermute(values, axis, [(i, (i + step) % size) for i in range(size)])


def blocks_over(values, axis):
    return lax.all_to_all(values, axis, split_axis=0, concat_axis=0, tiled=True)


def row_of(ref):
    values = ref[...].astype(WIDE)
    return jnp.concatenate([values[at : at + 1] for at in range(values.shape[0])], 1)


def project_pairs_kernel(tokens_ref, gain_ref, key_ref, value_ref, pairs_ref, normed_ref):
    values = tokens_ref[...].astype(WIDE)
    scale = lax.rsqrt(jnp.mean(values * values, axis=-1, keepdims=True) + EPSILON)
    normed = (values * scale * row_of(gain_ref)).astype(LOW)
    normed_ref[...] = normed
    groups, _, width, _ = pairs_ref.shape
    for kind, weight_ref in enumerate((key_ref, value_ref)):
        rows = dot_nn(normed, weight_ref[...]).T
        for group in range(groups):
            pairs_ref[group, kind] = rows[group * width : (group + 1) * width].astype(LOW)


def project_queries_kernel(normed_ref, weight_ref, out_ref):
    rows = dot_nn(normed_ref[...], weight_ref[...]).T
    groups, width, _ = out_ref.shape
    for group in range(groups):
        out_ref[group] = rows[group * width : (group + 1) * width].astype(LOW)


def turn_kernel(normed_ref, out_ref):
    turned = normed_ref[...].astype(WIDE).T.astype(LOW)
    for copy in range(out_ref.shape[0]):
        out_ref[copy] = turned


def strips_kernel(start_ref, table_ref, *refs):
    tiles = (len(refs) - 1) // 2
    bucket_refs, strips_refs, rows_ref = refs[:tiles], refs[tiles : 2 * tiles], refs[-1]
    buckets = table_ref.shape[1]
    for bucket_ref, strips_ref in zip(bucket_refs, strips_refs):
        heads, _, span = strips_ref.shape
        breadth = bucket_ref.shape[1]
        hot = lax.broadcasted_iota(jnp.int32, (buckets, breadth), 0) == bucket_ref[...]
        rows_ref[...] = dot_nn(table_ref[...], hot.astype(WIDE).astype(LOW))
        for head in range(heads):
            row = rows_ref[pl.ds(start_ref[0] + head, 1), :]
            spread = jnp.broadcast_to(row, (STRIP, breadth))
            turned = pltpu.roll(spread, breadth - (STRIP - 1), 1, stride=1, stride_axis=0)
            strips_ref[head] = turned[:, :span]


def make_strips(head_start, table_rows, buckets, heads, after):
    breadth = buckets[0].shape[1]
    return run(
        strips_kernel,
        [kept((heads, STRIP, breadth - STRIP), WIDE)] * len(buckets),
        (head_start, table_rows, *buckets),
        "bias_strips",
        flops=2 * 12 * 32 * breadth,
        in_specs=[SMEM] + [VMEM] * (1 + len(buckets)),
        scratch=[pltpu.VMEM((table_rows.shape[0], breadth), WIDE)],
        after=after,
    )


def head_mask(shape, head):
    lane = lax.broadcasted_iota(jnp.int32, shape, 1)
    return (lane >= head * HEAD_DIM) & (lane < (head + 1) * HEAD_DIM)


def side_by_side(pairs_ref, kind):
    return jnp.concatenate([pairs_ref[group, kind] for group in range(pairs_ref.shape[0])], 1)


def attend_kernel(*refs, heads, rows, tiles, first, last):
    query_ref = refs[0]
    pairs_refs, strips_refs, refs = refs[1 : 1 + tiles], refs[1 + tiles : 1 + 2 * tiles], refs[1 + 2 * tiles :]
    if not first:
        numer_in, total_in = refs[:2]
        refs = refs[2:]
    weight_refs, (total_ref, out_ref) = refs[:tiles], refs[tiles : tiles + 2]
    tile = query_ref.shape[2]
    groups = pairs_refs[0].shape[0]
    step = pl.program_id(0)
    queries = (query_ref[0] * jnp.asarray(0.125, LOW)).astype(WIDE).T.astype(LOW)
    out = jnp.zeros(queries.shape, WIDE)
    sums = jnp.zeros(queries.shape, WIDE)
    for head in range(heads):
        mask = head_mask(queries.shape, head)
        masked = jnp.where(mask, queries, jnp.zeros_like(queries))
        lanes = jnp.zeros((tile, 128), WIDE)
        numerator = jnp.zeros(queries.shape, WIDE)
        for pairs_ref, strips_ref, weight_ref in zip(pairs_refs, strips_refs, weight_refs):
            keys = jnp.concatenate([pairs_ref[group, 0] for group in range(groups)], 1)
            values = jnp.concatenate([pairs_ref[group, 1] for group in range(groups)], 1)
            scores = dot_nn(masked, keys)
            parts = []
            for sub in range(tile // STRIP):
                start = pl.multiple_of(rows - STRIP - (step * tile + sub * STRIP), STRIP)
                parts.append(
                    jnp.exp(
                        scores[sub * STRIP : (sub + 1) * STRIP, :]
                        + strips_ref[head, :, pl.ds(start, rows)]
                    )
                )
            weights = jnp.concatenate(parts, 0)
            for lane in range(rows // 128):
                lanes = lanes + weights[:, lane * 128 : (lane + 1) * 128]
            low = weights.astype(LOW)
            weight_ref[head] = low
            numerator = numerator + dot_nt(low, values)
        total = jnp.sum(lanes, axis=1, keepdims=True)
        out = jnp.where(mask, numerator, out)
        sums = jnp.where(mask, total, sums)
    out, sums = out.T, sums.T
    if not first:
        out = out + numer_in[0]
        sums = sums + total_in[0]
    total_ref[0] = sums
    if last:
        out = out / sums
        refs[-1][0] = out.astype(LOW)
    out_ref[0] = out


def gate(values, after):
    return pl.pallas_call(
        lambda *refs: None,
        out_shape=jax.ShapeDtypeStruct(values.shape, values.dtype),
        in_specs=[pl.BlockSpec(memory_space=pl.ANY)] + [unread(x) for x in after],
        out_specs=pl.BlockSpec(memory_space=pl.ANY),
        input_output_aliases={0: 0},
        name="gate",
    )(values, *(placed(x) for x in after))


def attend(queries, pairs, strips, before, last):
    groups, width, tile = queries.shape
    rows = groups * tile
    heads = width // HEAD_DIM
    tiles = len(pairs)
    block = pl.BlockSpec((1, width, tile), lambda i: (i, 0, 0))
    weight_block = pl.BlockSpec((heads, tile, rows), lambda i: (0, i, 0))
    operands = (queries, *(loose(x) for x in pairs), *(near(x) for x in strips), *before)
    return run(
        functools.partial(attend_kernel, heads=heads, rows=rows, tiles=tiles, first=not before, last=last),
        [shaped((heads, rows, rows), LOW)] * tiles
        + [shaped(queries.shape, WIDE)] * 2
        + [shaped(queries.shape, LOW)] * last,
        operands,
        "attend",
        flops=16 * width * rows * rows * tiles,
        grid=(groups,),
        in_specs=[block]
        + [fixed(x.shape) for x in pairs]
        + [fixed(x.shape) for x in strips]
        + [block] * len(before),
        out_specs=[weight_block] * tiles + [block] * (2 + last),
    )


def attend_back_kernel(*refs, heads, rows, first, last, begin):
    query_ref, grad_ref, att_ref, total_ref, weight_ref, pairs_ref = refs[:6]
    refs = refs[6:]
    if not first:
        query_in = refs[0]
        refs = refs[1:]
    query_back_ref, pairs_back_ref, diagonal_ref, strips_ref, key_acc, value_acc = refs
    tile = query_ref.shape[2]
    groups, _, width, chunk = pairs_back_ref.shape
    span = strips_ref.shape[2]
    step = pl.program_id(0)
    block = step + begin

    @pl.when(step == 0)
    def _():
        strips_ref[...] = jnp.zeros_like(strips_ref)
        key_acc[...] = jnp.zeros_like(key_acc)
        value_acc[...] = jnp.zeros_like(value_acc)

    query_turned = query_ref[0] * jnp.asarray(0.125, LOW)
    grads = grad_ref[0].astype(WIDE)
    inverse = 1.0 / total_ref[0]
    numer_wide = grads * inverse
    numer_turned = numer_wide.astype(LOW)
    products = -(numer_wide * att_ref[0]).T
    numer_back = numer_turned.astype(WIDE).T.astype(LOW)
    out = jnp.zeros(numer_back.shape, WIDE)
    keys = side_by_side(pairs_ref, 0)
    values = side_by_side(pairs_ref, 1)
    for head in range(heads):
        mask = head_mask(numer_back.shape, head)
        masked = jnp.where(mask, numer_back, jnp.zeros_like(numer_back))
        denom_back = jnp.sum(jnp.where(mask, products, 0.0), axis=1, keepdims=True)
        here = slice(head * HEAD_DIM, (head + 1) * HEAD_DIM)
        query_here = query_turned[here]
        numer_here = numer_turned[here]
        weight_back = dot_nn(masked, values)
        weights = weight_ref[head]
        score_back = weights.astype(WIDE) * (weight_back + denom_back)
        low = score_back.astype(LOW)
        for sub in range(tile // STRIP):
            start = pl.multiple_of(rows - STRIP - (block * tile + sub * STRIP), STRIP)
            strips_ref[head, :, pl.ds(start, rows)] += score_back[sub * STRIP : (sub + 1) * STRIP, :]
        key_acc[here, :] += dot_nn(query_here, low)
        value_acc[here, :] += dot_nn(numer_here, weights)
        query_back = dot_nt(low, keys)
        out = jnp.where(mask, query_back * 0.125, out)
    out = out.T
    if not first:
        out = out + query_in[0]
    query_back_ref[0] = out.astype(query_back_ref.dtype)

    @pl.when(step == pl.num_programs(0) - 1)
    def _():
        for group in range(groups):
            at = group * chunk
            pairs_back_ref[group, 0] = key_acc[:, at : at + chunk].astype(pairs_back_ref.dtype)
            pairs_back_ref[group, 1] = value_acc[:, at : at + chunk].astype(pairs_back_ref.dtype)
        diagonal_ref[...] = jnp.zeros_like(diagonal_ref)
        for head in range(heads):
            folded = strips_ref[head]
            size = STRIP
            while size > 8:
                size //= 2
                folded = folded[:size] + pltpu.roll(folded[size:], span - size, 1)
            row = folded[0:1]
            for place in range(1, 8):
                row = row + pltpu.roll(folded[place : place + 1], span - place, 1)
            diagonal_ref[head : head + 1, :] = pltpu.roll(row, STRIP - 1, 1)

def attend_back(
    queries, grads, attended, total, weights, pairs, before, last, begin, count, after
):
    groups, width, tile = queries.shape
    rows = groups * tile
    heads = width // HEAD_DIM
    span = 2 * rows
    block = pl.BlockSpec((1, width, tile), lambda i: (i + begin, 0, 0))
    out_block = pl.BlockSpec((1, width, tile), lambda i: (i, 0, 0))
    operands = (queries, grads, attended, total, weights, pairs, *before)
    return run(
        functools.partial(attend_back_kernel, heads=heads, rows=rows, first=not before, last=last, begin=begin),
        [
            shaped((count, width, tile), LOW if last else WIDE),
            shaped(pairs.shape, WIDE if last else LOW),
            shaped((8, span), WIDE),
        ],
        operands,
        "attend_back",
        flops=8 * width * rows * rows * count,
        grid=(count,),
        in_specs=[block, block, block, block]
        + [pl.BlockSpec((heads, tile, rows), lambda i: (0, i + begin, 0)), fixed(pairs.shape)]
        + [block] * len(before),
        out_specs=[out_block, fixed(pairs.shape), fixed((8, span))],
        scratch=[pltpu.VMEM((heads, STRIP, span), WIDE), pltpu.VMEM((width, rows), WIDE), pltpu.VMEM((width, rows), WIDE)], after=after)


def hot_rows(place_row, slots):
    tokens = place_row.shape[1]
    hot = lax.broadcasted_iota(jnp.int32, (slots, tokens), 0) == place_row
    return hot.astype(WIDE).astype(LOW)


def hot_columns(place_column, slots):
    tokens = place_column.shape[0]
    hot = lax.broadcasted_iota(jnp.int32, (tokens, slots), 1) == place_column
    return hot.astype(WIDE).astype(LOW)


def scatter_kernel(place_ref, rows_ref, slots_ref):
    hot = hot_rows(place_ref[...], slots_ref.shape[0])
    slots_ref[...] = dot_nn(hot, rows_ref[...]).astype(LOW)


def middle_kernel(
    att_ref, tokens_ref, weight_ref, gain_ref, place_ref, residual_ref, normed_ref, slots_ref
):
    residual = tokens_ref[...].astype(WIDE) + dot_tn(att_ref[...], weight_ref[...])
    residual_ref[...] = residual
    scale = lax.rsqrt(jnp.mean(residual * residual, axis=-1, keepdims=True) + EPSILON)
    normed = (residual * scale * row_of(gain_ref)).astype(LOW)
    normed_ref[...] = normed
    hot = hot_rows(place_ref[...], slots_ref.shape[0])
    slots_ref[...] = dot_nn(hot, normed).astype(LOW)


def route(normed, router, experts):
    logits = dot_nn(normed, router)
    lane = lax.broadcasted_iota(jnp.int32, logits.shape, 1)
    logits = jnp.where(lane < experts, logits, -jnp.inf)
    powers = jnp.exp(logits - jnp.max(logits, axis=-1, keepdims=True))
    return powers / jnp.sum(powers, axis=-1, keepdims=True), lane


def shard_copy(weight_refs, buffer_ref, semaphores, at):
    return pltpu.make_async_copy(weight_refs[at], buffer_ref.at[at % 2], semaphores.at[at % 2])


def take_shard(weight_refs, buffer_ref, semaphores):
    step = pl.program_id(0)

    @pl.when(step == 0)
    def _():
        for at in range(min(2, len(weight_refs))):
            shard_copy(weight_refs, buffer_ref, semaphores, at).start()

    for at in range(len(weight_refs)):

        @pl.when(step == at)
        def _(at=at):
            shard_copy(weight_refs, buffer_ref, semaphores, at).wait()

    return lax.rem(step, 2)


def next_shard(weight_refs, buffer_ref, semaphores):
    for at in range(len(weight_refs) - 2):

        @pl.when(pl.program_id(0) == at)
        def _(at=at):
            shard_copy(weight_refs, buffer_ref, semaphores, at + 2).start()


def shard_scratch(weights):
    return [pltpu.VMEM((2, *weights[0].shape), LOW), pltpu.SemaphoreType.DMA((2,))]


def shard_places(weights):
    return [pl.BlockSpec(memory_space=pltpu.HBM)] * len(weights)


def raw_back_kernel(up_ref, *refs):
    *weight_refs, raw_ref, buffer_ref, semaphores = refs
    slot = take_shard(weight_refs, buffer_ref, semaphores)
    raw_ref[...] = dot_nt(up_ref[...], buffer_ref[slot]).astype(LOW)
    next_shard(weight_refs, buffer_ref, semaphores)


def expert_kernel(own_ref, rows_ref, up_ref, router_ref, raw_ref, *refs, experts):
    *weight_refs, act_ref, pre_ref, home_ref, out_back_ref, logit_ref = refs[:-6]
    probs_ref, back_acc, gate_acc, gate_ref, buffer_ref, semaphores = refs[-6:]
    slot = take_shard(weight_refs, buffer_ref, semaphores)
    step = pl.program_id(0)
    rows = rows_ref[...]

    @pl.when(step == 0)
    def _():
        probs, lane = route(rows, router_ref[...], experts)
        probs_ref[...] = probs
        hot = (lane == own_ref[0]).astype(WIDE)
        gate = jnp.sum(probs * hot, axis=-1, keepdims=True)
        gate_ref[...] = jnp.broadcast_to(gate, gate_ref.shape)
        out_back_ref[...] = (gate * up_ref[...].astype(WIDE)).astype(LOW)
        back_acc[...] = jnp.zeros_like(back_acc)
        gate_acc[...] = jnp.zeros_like(gate_acc)

    gate = gate_ref[:, 0:1]
    lanes = gate_acc[...]
    back = back_acc[...]
    root = 0.7978845608028654
    hidden = buffer_ref.shape[2]
    size = 256 if hidden % 256 == 0 else 128
    count = hidden // size
    following = dot_nn(rows, buffer_ref[slot, :, 0:size])
    for piece in range(count):
        here = slice(piece * size, (piece + 1) * size)
        value = following
        if piece + 1 < count:
            following = dot_nn(rows, buffer_ref[slot, :, (piece + 1) * size : (piece + 2) * size])
        squared = value * value
        tilted = jnp.tanh(value * (root + (root * 0.044715) * squared))
        share = 0.5 + 0.5 * tilted
        wide = value * share
        act = wide.astype(LOW)
        slope = share + wide * (1.0 - share) * (2.0 * root + (6.0 * root * 0.044715) * squared)
        raw = raw_ref[:, here].astype(WIDE)
        pre = (gate * raw * slope).astype(LOW)
        act_ref[:, here] = act
        pre_ref[:, here] = pre
        back = back + dot_nt(pre, buffer_ref[slot, :, here])
        shares = act.astype(WIDE) * raw
        for lane in range(size // 128):
            lanes = lanes + shares[:, lane * 128 : (lane + 1) * 128]
    gate_acc[...] = lanes
    back_acc[...] = back
    next_shard(weight_refs, buffer_ref, semaphores)

    @pl.when(step == pl.num_programs(0) - 1)
    def _():
        probs = probs_ref[...]
        hot = (lax.broadcasted_iota(jnp.int32, probs.shape, 1) == own_ref[0]).astype(WIDE)
        gate_back = jnp.sum(gate_acc[...], axis=-1, keepdims=True)
        logit_back = (probs * gate_back * (hot - gate_ref[...])).astype(LOW)
        logit_ref[...] = logit_back
        home_ref[...] = (dot_nt(logit_back, router_ref[...]) + back_acc[...]).astype(LOW)


def store_half(former_ref, latter_ref, keep_ref, send_ref):
    count = pl.num_programs(0) // 2

    @pl.when(pl.program_id(0) < count)
    def _():
        send_ref[0] = dot_tn(former_ref[...], latter_ref[...]).astype(LOW)

    @pl.when(pl.program_id(0) >= count)
    def _():
        keep_ref[0] = dot_tn(former_ref[...], latter_ref[...]).astype(LOW)


def shard_at(i, shares):
    count = shares // 2
    return jnp.where(i < count, 2 * i + 1, 2 * (i - count))


def keep_spec(shape, shares):
    return pl.BlockSpec((1, *shape), lambda i: (jnp.maximum(i - shares // 2, 0), 0, 0))


def send_spec(shape, shares):
    return pl.BlockSpec((1, *shape), lambda i: (jnp.minimum(i, shares // 2 - 1), 0, 0))


def inner_grads_kernel(rows_ref, pre_ref, logit_ref, keep_ref, send_ref, router_ref):
    store_half(rows_ref, pre_ref, keep_ref, send_ref)

    @pl.when(pl.program_id(0) == 0)
    def _():
        router_ref[...] = dot_tn(logit_ref[...], rows_ref[...])[: router_ref.shape[0]]


def outer_grads_kernel(act_ref, out_back_ref, *refs):
    *weight_refs, keep_ref, send_ref, out_ref, total_ref, buffer_ref, semaphores = refs
    step = pl.program_id(0)
    slot = take_shard(weight_refs, buffer_ref, semaphores)

    @pl.when(step == 0)
    def _():
        total_ref[...] = jnp.zeros_like(total_ref)

    store_half(act_ref, out_back_ref, keep_ref, send_ref)
    total_ref[...] += dot_nn(act_ref[...], buffer_ref[slot])
    next_shard(weight_refs, buffer_ref, semaphores)

    @pl.when(step == pl.num_programs(0) - 1)
    def _():
        out_ref[...] = total_ref[...].astype(LOW)


def add_shards_kernel(*refs, count):
    operands, outs = refs[:count], refs[count:]
    total = operands[0][0].astype(WIDE)
    for operand in operands[1:]:
        total += operand[0].astype(WIDE)
    if len(outs) == 1:
        outs[0][0] = total.astype(outs[0].dtype)
        return
    half = pl.num_programs(1) // 2
    for place, out_ref in enumerate(outs):

        @pl.when(pl.program_id(1) // half == place)
        def _(out_ref=out_ref):
            out_ref[0] = total.astype(out_ref.dtype)


def add_shards(operands, start, count, kind, parts, name, after=()):
    _, rows, columns = operands[0].shape
    tile = rows // 2 if rows % 32 == 0 else rows
    steps = rows // tile
    parts = parts if steps % 2 == 0 else 1
    half = steps // parts
    block = pl.BlockSpec((1, tile, columns), lambda i, j: (start + i, j, 0))

    def out_block(place):
        last = half - 1
        return pl.BlockSpec(
            (1, tile, columns), lambda i, j: (i, jnp.clip(j - place * half, 0, last), 0)
        )

    return run(
        functools.partial(add_shards_kernel, count=len(operands)),
        [shaped((count, rows // parts, columns), kind)] * parts,
        (operands[0], *(loose(x) for x in operands[1:])),
        name,
        flops=0,
        grid=(count, steps),
        in_specs=[block] * len(operands),
        out_specs=[out_block(place) for place in range(parts)],
        after=after,
    )


def gather_shards(keep, send):
    operands = [keep, swap(send, "dp", 1)]
    size = keep.shape[0]
    while size > 2:
        half = size // 2
        gone = add_shards(operands, half, half, LOW, 1, "add_shards")
        operands.append(swap(gone[0], "dp", 2 * half))
        size = half
    gone = add_shards(operands, 1, 1, LOW, 1, "add_shards")
    return operands, [swap(part, "dp", 2) for part in gone], gone[0]


def finish_kernel(*refs, count, steps):
    former_refs, came_refs, (out_ref, mark_ref) = refs[:count], refs[count:-2], refs[-2:]
    total = former_refs[0][0].astype(WIDE)
    for former_ref in former_refs[1:]:
        total += former_ref[0].astype(WIDE)
    half = steps // len(came_refs)
    for place, came_ref in enumerate(came_refs):

        @pl.when(pl.program_id(0) // half == place)
        def _(came_ref=came_ref):
            out_ref[...] = total + came_ref[0].astype(WIDE)

    mark_ref[...] = jnp.zeros_like(mark_ref)


def finish_shards(formers, came):
    _, rows, columns = formers[0].shape
    tile = rows // 2 if rows % 32 == 0 else rows
    steps = rows // tile
    half = steps // len(came)
    block = pl.BlockSpec((1, tile, columns), lambda i: (0, i, 0))
    parts = [
        pl.BlockSpec(
            (1, tile, columns), lambda i, place=place: (0, jnp.clip(i - place * half, 0, half - 1), 0)
        )
        for place in range(len(came))
    ]
    return run(
        functools.partial(finish_kernel, count=len(formers), steps=steps),
        [shaped((rows, columns), WIDE), shaped((8, 128), WIDE)],
        (formers[0], *(loose(x) for x in (*formers[1:], *came))),
        "finish_shards",
        flops=0,
        grid=(steps,),
        in_specs=[block] * len(formers) + parts,
        out_specs=[pl.BlockSpec((tile, columns), lambda i: (i, 0)), fixed((8, 128))],
    )


def after_kernel(
    home_ref,
    place_ref,
    residual_ref,
    gain_ref,
    upstream_ref,
    weight_ref,
    att_back_ref,
    residual_back_ref,
    branch_ref,
    gain_back_ref,
):
    hot = hot_columns(place_ref[...], home_ref.shape[0])
    normed_back = dot_nn(hot, home_ref[...])
    residual = residual_ref[...]
    scale = lax.rsqrt(jnp.mean(residual * residual, axis=-1, keepdims=True) + EPSILON)
    spread = residual * scale
    gained = row_of(gain_ref) * normed_back
    inner = jnp.mean(gained * spread, axis=-1, keepdims=True)
    back = upstream_ref[...].astype(WIDE) + scale * (gained - spread * inner)
    residual_back_ref[...] = back
    branch = back.astype(LOW)
    branch_ref[...] = branch
    gain_back_ref[...] = jnp.broadcast_to(
        jnp.sum(normed_back * spread, axis=0, keepdims=True), gain_back_ref.shape
    )
    att_back_ref[...] = dot_nt(weight_ref[...], branch).astype(LOW)


def output_pieces_kernel(core_ref, att_ref, branch_ref, router_ref, gain_ref, *refs, owners):
    *out_refs, full_ref = refs
    grad = dot_nn(att_ref[...], branch_ref[...])
    own = grad.shape[0] // owners
    height = full_ref.shape[0] // owners
    full_ref[...] = jnp.zeros_like(full_ref)
    for owner in range(owners):
        full_ref[owner * height : owner * height + own, :] = grad[owner * own : (owner + 1) * own]
    at = own + router_ref.shape[0]
    full_ref[own:at, :] = router_ref[...]
    full_ref[at : at + 8, :] = gain_ref[...]
    for place, out_ref in enumerate(out_refs):
        height = out_ref.shape[0]
        start = pl.multiple_of(jnp.bitwise_xor(core_ref[0], place) * height, height)
        out_ref[...] = full_ref[pl.ds(start, height), :].astype(out_ref.dtype)


def is_cube():
    return [lax.axis_size(name) for name in ("head", "blk", "dp")] == [4, 2, 4]


def sums_kernel(me_ref, *refs, count):
    operands, outs = refs[: len(refs) - count], refs[len(refs) - count :]
    for place, out_ref in enumerate(outs):
        height = out_ref.shape[0]
        start = pl.multiple_of(jnp.bitwise_xor(me_ref[0], place) * height, height)
        total = operands[0][pl.ds(start, height), :].astype(WIDE)
        for operand in operands[1:]:
            total += operand[pl.ds(start, height), :].astype(WIDE)
        out_ref[...] = total.astype(out_ref.dtype)


def sums(me, operands, count, name, after=()):
    height, breadth = operands[0].shape
    return run(
        functools.partial(sums_kernel, count=count),
        [shaped((height // count, breadth), LOW)] * count,
        (me[None].astype(jnp.int32), operands[0], *(loose(x) for x in operands[1:])),
        name,
        flops=0,
        in_specs=[SMEM] + [VMEM] * len(operands),
        after=after,
    )


def cross(mine, other, name, after=()):
    spot = lax.axis_index("blk") * 2 + lax.axis_index("dp") // 2
    own, along, across, corner = sums(spot, (mine, swap(other, "dp", 1)), 4, name, after)
    diagonal = [(b * 4 + d, (1 - b) * 4 + (d ^ 2)) for b in range(2) for d in range(4)]
    return [
        own,
        swap(across, "blk", 1),
        swap(along, "dp", 2),
        lax.ppermute(corner, ("blk", "dp"), diagonal),
    ]


def output_pieces(att_tok, branch_back, router_back, gain_back):
    model_width, experts = branch_back.shape[1], router_back.shape[0]
    cube = is_cube()
    owners = 8 if cube else 1
    height = owners * -(-(model_width // owners + experts + 8) // 128) * 128
    dp = lax.axis_index("dp")
    count = 2 if cube else 1
    outs = run(
        functools.partial(output_pieces_kernel, owners=owners),
        [shaped((height // count, model_width), LOW if cube else WIDE)] * count,
        (
            ((dp & 1) * (count - 1)).astype(jnp.int32)[None],
            att_tok,
            branch_back,
            router_back,
            gain_back,
        ),
        "output_pieces",
        flops=2 * att_tok.size * model_width,
        in_specs=[SMEM] + [VMEM] * 4,
        scratch=[pltpu.VMEM((height, model_width), WIDE)],
    )
    if not cube:
        return (), (), lax.psum(outs[0], ("head", "blk", "dp"))
    own, *came = cross(*outs, "output_core")
    shares = sums(lax.axis_index("head"), (own, *came), 4, "output_sum")
    arrived = [shares[0]] + [swap(shares[step], "head", step) for step in range(1, 4)]
    return (own,), (shares[0],), arrived


def output_kernel(
    residual_ref, normed_ref, router_ref, chosen_ref, place_ref, slots_ref, out_ref, *, experts
):
    probs, lane = route(normed_ref[...], router_ref[...], experts)
    hot = (lane == chosen_ref[...]).astype(WIDE)
    gate = jnp.sum(probs * hot, axis=-1, keepdims=True)
    expert_out = dot_nn(hot_columns(place_ref[...], slots_ref.shape[0]), slots_ref[...])
    out_ref[...] = (residual_ref[...] + gate * expert_out).astype(LOW)


def tokens_grad_kernel(
    triples_ref,
    query_weight_ref,
    key_weight_ref,
    value_weight_ref,
    tokens_ref,
    gain_ref,
    residual_back_ref,
    out_ref,
):
    groups = triples_ref.shape[0]
    weight_refs = (query_weight_ref, key_weight_ref, value_weight_ref)
    normed_back = jnp.zeros(out_ref.shape[::-1], WIDE)
    for kind, weight_ref in enumerate(weight_refs):
        rows = jnp.concatenate([triples_ref[group, kind] for group in range(groups)], 0)
        normed_back += dot_nn(weight_ref[...], rows)
    normed_back = normed_back.T
    values = tokens_ref[...].astype(WIDE)
    scale = lax.rsqrt(jnp.mean(values * values, axis=-1, keepdims=True) + EPSILON)
    spread = values * scale
    gained = row_of(gain_ref) * normed_back
    inner = jnp.mean(gained * spread, axis=-1, keepdims=True)
    out_ref[...] = (residual_back_ref[...] + scale * (gained - spread * inner)).astype(LOW)


def bucket_sums(diagonal, bucket_row, buckets):
    breadth = bucket_row.shape[1]
    hot = lax.broadcasted_iota(jnp.int32, (buckets, breadth), 0) == bucket_row
    hot = hot.astype(WIDE).astype(LOW)
    high = diagonal.astype(LOW)
    rest = diagonal - high.astype(WIDE)
    middle = rest.astype(LOW)
    small = (rest - middle.astype(WIDE)).astype(LOW)
    return dot_nt(high, hot) + dot_nt(middle, hot) + dot_nt(small, hot)


def side(grads):
    return -(-3 * grads // 128) * 128


def blocks_of(refs):
    return [ref[place] for ref in refs for place in range(ref.shape[0])]


def projection_grads(turned_ref, query_refs, pairs_ref):
    _, width, tokens = query_refs[0].shape
    queries = blocks_of(query_refs)
    groups = len(queries)
    spare = jnp.zeros((side(width) - 3 * width, tokens), LOW)
    total = None
    for group in range(groups):
        rows = [queries[group], pairs_ref[group, 0], pairs_ref[group, 1], spare]
        part = dot_nt(turned_ref[group], jnp.concatenate(rows, 0))
        total = part if total is None else total + part
    return total


def table_sums(diagonal_refs, bucket_refs, buckets):
    table = bucket_sums(diagonal_refs[0][...], bucket_refs[0][...], buckets)
    for diagonal_ref, bucket_ref in zip(diagonal_refs[1:], bucket_refs[1:]):
        table += bucket_sums(diagonal_ref[...], bucket_ref[...], buckets)
    return table


def add_pairs(home_refs):
    total = home_refs[0][...].astype(WIDE)
    for home_ref in home_refs[1:]:
        total += home_ref[...].astype(WIDE)
    return total.astype(LOW)


def triples_kernel(*refs, parts):
    pairs = add_pairs(refs[parts:-1])
    for group, queries in enumerate(blocks_of(refs[:parts])):
        refs[-1][group, 0] = queries
        refs[-1][group, 1] = pairs[group, 0]
        refs[-1][group, 2] = pairs[group, 1]


def pieces_kernel(core_ref, turned_ref, *refs, parts, tiles, buckets):
    query_refs, refs = refs[:parts], refs[parts:]
    home_refs, refs = refs[:tiles], refs[tiles:]
    diagonal_refs, bucket_refs = refs[:tiles], refs[tiles : 2 * tiles]
    *out_refs, pairs_ref, full_ref = refs[2 * tiles :]
    width = query_refs[0].shape[1]
    pairs_ref[...] = add_pairs(home_refs)
    full_ref[...] = projection_grads(turned_ref, query_refs, pairs_ref)
    table = table_sums(diagonal_refs, bucket_refs, buckets)
    full_ref[0:8, 3 * width : 3 * width + buckets] = table
    for place, out_ref in enumerate(out_refs):
        height = out_ref.shape[0]
        start = pl.multiple_of(jnp.bitwise_xor(core_ref[0], place) * height, height)
        out_ref[...] = full_ref[pl.ds(start, height), :].astype(out_ref.dtype)


def join_kernel(*refs):
    *refs, out_ref = refs
    copies, halves, part, _ = out_ref.shape
    count = len(refs) // 2
    columns = refs[0].shape[1]
    total, packed = (
        functools.reduce(jnp.add, [ref[...].astype(WIDE) for ref in group])
        for group in (refs[:count], refs[count:])
    )
    height = packed.shape[0] // halves
    for half in range(halves):
        former = total[half * part : (half + 1) * part].astype(LOW)
        rows = packed[half * height : (half + 1) * height]
        blocks = [rows[:, at : at + 256] for at in range(0, rows.shape[1], 256)]
        latter = jnp.concatenate(blocks, 0).astype(LOW)
        for copy in range(copies):
            out_ref[copy, half, :, :columns] = former
            out_ref[copy, half, :, columns:] = latter


def share_kernel(spot_ref, cases, places, weight_refs, out_refs, sums_ref, table_ref, extra_ref, heads):
    step = pl.program_id(0)
    owner = jnp.bitwise_xor(spot_ref[0], places[0] if len(places) == 1 else place_at(step, places))
    part = out_refs[0].shape[0] // 2
    width = heads * HEAD_DIM
    columns = side(width)
    buckets = table_ref.shape[2]
    for case, pair in enumerate(cases):

        @pl.when(step == case)
        def _(pair=pair):
            for half in range(2):
                ref = pair[half]
                groups = ref.shape[0]
                at = half if ref.shape[1] == 2 else 0
                rows = slice(half * part, (half + 1) * part)

                def tile(group, place, ref=ref, at=at):
                    return ref[group, at, :, place * 128 : (place + 1) * 128].astype(WIDE)

                def turned(group, place, tile=tile):
                    return pltpu.roll(tile(group, place), 64, 1)

                lower = lax.broadcasted_iota(jnp.int32, (part, 128), 1) < 64
                for one in range(0, groups, 2):
                    two = one + 1
                    for kind in range(3):
                        if kind == 1:
                            middle = turned(one, 2)
                            parts = (
                                jnp.where(lower, turned(one, 1), middle),
                                jnp.where(lower, middle, tile(two, 1)),
                                tile(two, 2),
                            )
                        else:
                            place = 3 * kind // 2
                            first = turned(two, place)
                            parts = (
                                tile(one, place),
                                jnp.where(lower, tile(one, place + 1), first),
                                jnp.where(lower, first, turned(two, place + 1)),
                            )
                        for number, values in enumerate(parts):
                            lane = one * width + number * 128
                            out_refs[kind][rows, lane : lane + 128] = values
                for group in range(groups):
                    packed = ref[group, at, :, columns:].astype(WIDE)
                    start = group * 32 + half * 16
                    for number in range(part // 16):
                        lane = number * 256
                        values = packed[number * 16 : (number + 1) * 16]
                        if group + 1 < groups:
                            out_refs[3][start : start + 16, lane : lane + 256] = values
                        else:

                            @pl.when(owner == 0)
                            def _(values=values, half=half, lane=lane):
                                extra_ref[half * 16 : half * 16 + 16, lane : lane + 256] = values

                    if half == 0:

                        @pl.when(owner == 0)
                        def _(group=group, tile=tile):
                            table_ref[group] = tile(group, 4)[:8, 64 : 64 + buckets]

    shares = jnp.zeros((2 * part, 1), WIDE)
    for kind in range(3):
        shares += jnp.sum(
            out_refs[kind][...] * weight_refs[kind][...].astype(WIDE), axis=1, keepdims=True
        )
    shares = jnp.broadcast_to(shares, (2 * part, 128))
    if sums_ref.shape[0] == 2 * part:
        sums_ref[...] = shares
    else:
        sums_ref[pl.ds(owner * 2 * part, 2 * part), :] = shares


def place_at(step, places):
    return sum(jnp.where(step == at, place, 0) for at, place in enumerate(places))


FIRST_PLACES, LAST_PLACES = (0, 1, 2, 4, 5, 6), (3, 7)


def first_shares_kernel(spot_ref, *refs, heads):
    piece_refs, weight_refs, refs = refs[:6], refs[6:9], refs[9:]
    out_refs, (sums_ref, table_ref, extra_ref) = refs[:4], refs[4:]

    @pl.when(pl.program_id(0) == 0)
    def _():
        table_ref[...] = jnp.zeros_like(table_ref)
        extra_ref[...] = jnp.zeros_like(extra_ref)

    cases = [(ref, ref) for ref in piece_refs]
    share_kernel(
        spot_ref, cases, FIRST_PLACES, weight_refs, out_refs, sums_ref, table_ref, extra_ref, heads
    )


def last_shares_kernel(spot_ref, *refs, heads, experts):
    piece_refs, weight_refs, refs = refs[:4], refs[4:7], refs[7:]
    gain_ref, sums_in, table_in, extra_in, *refs = refs
    out_refs, refs = refs[4:8], refs[8:]
    gain_out, second_out, table_out, router_out, sums_ref, table_ref, extra_ref = refs
    step = pl.program_id(0)

    @pl.when(step == 0)
    def _():
        sums_ref[...] = sums_in[...]
        table_ref[...] = table_in[...]
        extra_ref[...] = extra_in[...]

    cases = [(piece_refs[0], piece_refs[1]), (piece_refs[2], piece_refs[3])]
    share_kernel(
        spot_ref, cases, LAST_PLACES, weight_refs, out_refs, sums_ref, table_ref, extra_ref, heads
    )

    @pl.when(step == pl.num_programs(0) - 1)
    def _():
        first = sums_ref[...].T[0:8] / row_of(gain_ref)
        second = extra_ref[experts : experts + 8, :]
        for lane in range(gain_out.shape[0]):
            gain_out[lane : lane + 1, :] = first[0:1, lane * 128 : (lane + 1) * 128]
            second_out[lane : lane + 1, :] = second[0:1, lane * 128 : (lane + 1) * 128]
        router_out[...] = extra_ref[:experts, :]
        for group in range(table_ref.shape[0]):
            table_out[group * heads : (group + 1) * heads, :] = table_ref[group][:heads]


def put_together(me, first, corners, weights, gain, heads, buckets, experts):
    model_width = weights[0].shape[0]
    groups, _, part, _ = first[0].shape

    def rows(places, breadth):
        return pl.BlockSpec(
            (2 * part, breadth), lambda i, me: (place_at(i, places) ^ me[0], 0)
        )

    square = shaped((model_width, model_width), WIDE)
    kept_shapes = [(groups, 8, buckets), (32, model_width)]
    *grads, sums, table, extra = run_with_scalar(
        functools.partial(first_shares_kernel, heads=heads),
        me,
        [square] * 4 + [shaped((model_width, 128), WIDE)] + [shaped(x, WIDE) for x in kept_shapes],
        (*(loose(x) for x in first), *weights),
        "first_shares",
        grid=(len(FIRST_PLACES),),
        in_specs=[fixed(x.shape) for x in first] + [rows(FIRST_PLACES, model_width)] * 3,
        out_specs=[rows(FIRST_PLACES, model_width)] * 4
        + [rows(FIRST_PLACES, 128)]
        + [fixed(x) for x in kept_shapes],
    )
    corners = [gate(array, (table,)) for array in corners]
    last = (*corners, *(swap(array, "dp", 1) for array in corners))
    operands = (*(loose(x) for x in last), *weights, gain, sums, table, extra, *grads)
    vectors = [(model_width // 128, 128)] * 2 + [(groups * heads, buckets), (experts, model_width)]
    count = len(last)
    *grads, shares, second, table, router = run_with_scalar(
        functools.partial(last_shares_kernel, heads=heads, experts=experts),
        me,
        [square] * 4 + [shaped(x, WIDE) for x in vectors],
        operands,
        "last_shares",
        grid=(len(LAST_PLACES),),
        in_specs=[fixed(x.shape) for x in last]
        + [rows(LAST_PLACES, model_width)] * 3
        + [fixed(x.shape) for x in operands[count + 3 : count + 7]]
        + [pl.BlockSpec(memory_space=pltpu.HBM)] * 4,
        out_specs=[rows(LAST_PLACES, model_width)] * 4 + [fixed(x) for x in vectors],
        scratch=[pltpu.VMEM((model_width, 128), WIDE)] + [pltpu.VMEM(x, WIDE) for x in kept_shapes],
        aliases={count + 8 + i: i for i in range(4)},
    )
    query_grad, key_grad, value_grad, output_grad = grads
    return (
        query_grad,
        key_grad,
        value_grad,
        shares.reshape(-1),
        table.T,
        output_grad,
        router.T,
        second.reshape(-1),
    )


def take_half_kernel(values_ref, out_ref):
    out_ref[...] = values_ref[...]


def take_half(values, half):
    groups, _, *rest = values.shape
    return pl.pallas_call(
        take_half_kernel,
        out_shape=pltpu.HBM((groups, 1, *rest), values.dtype),
        grid=(groups,),
        in_specs=[pl.BlockSpec((1, 1, *rest), lambda i: (i, half, 0, 0))],
        out_specs=pl.BlockSpec((1, 1, *rest), lambda i: (i, 0, 0, 0)),
        compiler_params=pltpu.CompilerParams(vmem_limit_bytes=VMEM_BYTES),
        name="take_half",
    )(values)


def weight_sums(
    turned, query_backs, home, diagonals, bucket_rows, buckets, weights, gain, experts, packed, middle, late
):
    groups, model_width, _ = turned.shape
    width = query_backs[0].shape[1]
    heads = width // HEAD_DIM
    tiles = len(diagonals)
    cube = is_cube()
    columns = side(width)
    dp, blk = lax.axis_index("dp"), lax.axis_index("blk")
    count = 2 if cube else 1
    pieces = run(
        functools.partial(pieces_kernel, parts=len(query_backs), tiles=tiles, buckets=buckets),
        [shaped((model_width // count, columns), LOW if cube else WIDE)] * count,
        (
            ((dp & 1) * (count - 1)).astype(jnp.int32)[None],
            near(turned),
            *query_backs,
            *received_loose(home),
            *diagonals,
            *bucket_rows,
        ),
        "projection_pieces",
        flops=6 * turned.size * width,
        in_specs=[SMEM] + [VMEM] * (1 + len(query_backs) + 3 * tiles),
        scratch=[pltpu.VMEM(home[0].shape, LOW), pltpu.VMEM((model_width, columns), WIDE)],
    )
    if not cube:
        sums = lax.psum(pieces[0], ("blk", "dp"))
        table = lax.all_gather(
            sums[:heads, 3 * width : 3 * width + buckets], "head", axis=0, tiled=True
        )
        grads = sums[:, : 3 * width].reshape(model_width, 3, width)
        grads = lax.all_gather(grads, "head", axis=2, tiled=True)
        grads = [grads[:, i] for i in range(3)]
        shares = sum(jnp.sum(x * y.astype(WIDE), axis=1) for x, y in zip(grads, weights))
        rest = packed[model_width:]
        shares = shares / gain.reshape(-1).astype(WIDE)
        packed = packed[:model_width], rest[:experts].T, rest[experts]
        return pieces, *grads, shares, table.T, *packed
    part = model_width // 16
    copies = run(
        join_kernel,
        [shaped((groups, 2, part, columns + 256), LOW)],
        tuple(loose(x) for x in (*cross(*pieces, "projection_core", middle), *packed)),
        "join",
        flops=0,
        after=late,
    )[0]
    own = blocks_over(copies, "head")
    across, along = swap(own, "blk", 1), swap(own, "dp", 2)
    corners = (
        swap(take_half(across, 0), "dp", 2),
        swap(take_half(along, 1), "blk", 1),
    )
    near_ones = (own, along, across)
    first = (*near_ones, *(swap(array, "dp", 1) for array in near_ones))
    me = ((dp & 1) * 4 + blk * 2 + dp // 2).astype(jnp.int32)[None]
    return pieces, *put_together(me, first, corners, weights, gain, heads, buckets, experts)


def body(
    tokens,
    first_gain,
    query_weight,
    key_weight,
    value_weight,
    output_weight,
    bias_table,
    second_gain,
    router_weight,
    inner_weight,
    outer_weight,
    expert_index,
    capacity_slot,
    bucket_of_offset,
    upstream,
):
    _, token_rows, model_width = tokens.shape
    groups = lax.axis_size("head")
    cycle = lax.axis_size("blk")
    shares = lax.axis_size("dp")
    width = model_width // groups
    heads = width // HEAD_DIM
    local_rows = groups * token_rows
    length = local_rows * cycle
    buckets = bias_table.shape[0]
    experts = router_weight.shape[1]
    capacity = max(2, 2 * token_rows // experts)
    slots = experts * capacity
    token_values, upstream_values = tokens[0], upstream[0]
    gain_one, gain_two = first_gain.reshape(-1, 128), second_gain.reshape(-1, 128)
    chosen = expert_index[0]
    place = chosen * capacity + capacity_slot[0]
    place_row, place_column, chosen_column = place[None], place[:, None], chosen[:, None]
    router = jnp.pad(router_weight, ((0, 0), (0, 128 - experts)))

    inner_shards, outer_shards = [inner_weight[0]], [outer_weight[0]]
    for held in (outer_shards, inner_shards):
        for bit in range(1, shares.bit_length() - 1):
            held += [swap(values, "dp", 1 << bit) for values in held]
    far_inner, far_outer = inner_shards[1:], outer_shards[1:]
    for held in (outer_shards, inner_shards):
        held[:] = [x for values in held for x in (values, swap(values, "dp", 1))]

    square = model_width * model_width
    pairs, normed_one = run(
        project_pairs_kernel,
        [
            shaped((groups, 2, width, token_rows), LOW),
            shaped((token_rows, model_width), LOW),
        ],
        (token_values, gain_one, key_weight, value_weight),
        "project_pairs",
        flops=4 * token_rows * square,
    )
    pairs = blocks_over(pairs, "head")
    head_start = (lax.axis_index("head") * heads).astype(jnp.int32)[None]
    table_rows = jnp.pad(bias_table.T, ((0, -(groups * heads) % 8), (0, 0)))
    bucket_line = jnp.pad(bucket_of_offset, (0, 1))[None]
    blk = lax.axis_index("blk")
    tile_buckets, tile_strips = [], []
    for step in range(cycle):
        number = lax.rem(blk + cycle - step, cycle)
        start = length + (number - blk - 1) * local_rows
        tile_buckets.append(lax.dynamic_slice_in_dim(bucket_line, start, 2 * local_rows, 1))
    tile_pairs = [pairs] + [turn(pairs, "blk", step) for step in range(1, cycle)]
    up_slots = run(
        scatter_kernel,
        [shaped((slots, model_width), LOW)],
        (place_row, upstream_values),
        "scatter_up",
        flops=2 * slots * token_rows * model_width,
        after=(normed_one,),
    )[0]
    turned = run(
        turn_kernel,
        [shaped((groups, model_width, token_rows), LOW)],
        (normed_one,),
        "turn",
        flops=0,
    )[0]
    queries = run(
        project_queries_kernel,
        [shaped((groups, width, token_rows), LOW)],
        (normed_one, query_weight),
        "project_queries",
        flops=2 * token_rows * square,
        after=(up_slots, turned),
    )[0]
    queries = blocks_over(gate(queries, (loose(pairs),)), "head")
    up_rows = blocks_over(up_slots, ("head", "blk"))
    for step in range(0, cycle, 2):
        tile_strips += make_strips(
            head_start, table_rows, tile_buckets[step : step + 2], heads, (queries,)
        )
    tile_weights, before = [], ()
    for step in range(0, cycle, 2):
        tiles = slice(step, step + 2)
        last = step + 2 >= cycle
        results = attend(queries, tile_pairs[tiles], tile_strips[tiles], before, last)
        tile_weights += results[: len(tile_pairs[tiles])]
        total, attended, *rest = results[len(tile_pairs[tiles]) :]
        before = (attended, total)
    attended_low = gate(rest[0], (loose(up_rows),))
    att_tok = blocks_over(attended_low, "head").reshape(model_width, token_rows)
    hidden = inner_shards[0].shape[1]
    full_hidden = shares * hidden
    product = 2 * slots * model_width * full_hidden
    hidden_block = pl.BlockSpec((slots, hidden), lambda i: (0, i))
    turned_block = pl.BlockSpec((slots, hidden), lambda i: (0, shard_at(i, shares)))
    raw = run(
        raw_back_kernel,
        [shaped((slots, full_hidden), LOW)],
        (near(up_rows), *outer_shards),
        "raw_back",
        flops=product,
        grid=(shares,),
        in_specs=[fixed(up_rows.shape)] + shard_places(outer_shards),
        out_specs=[hidden_block],
        scratch=shard_scratch(outer_shards),
    )[0]
    residual_mid, normed_two, normed_slots = run(
        middle_kernel,
        [
            shaped((token_rows, model_width), WIDE),
            shaped((token_rows, model_width), LOW),
            shaped((slots, model_width), LOW),
        ],
        (near(att_tok), token_values, output_weight, gain_two, place_row),
        "middle",
        flops=2 * token_rows * square + 2 * slots * token_rows * model_width,
        after=(raw, router, *far_inner),
    )
    expert_rows = blocks_over(normed_slots, ("head", "blk"))
    own_expert = (lax.axis_index("head") * cycle + blk).astype(jnp.int32)[None]
    hidden_act, pre_back, home_slots, out_back, logit_back = run(
        functools.partial(expert_kernel, experts=experts),
        [
            shaped((slots, full_hidden), LOW),
            shaped((slots, full_hidden), LOW),
            shaped((slots, model_width), LOW),
            shaped((slots, model_width), LOW),
            shaped((slots, 128), LOW),
        ],
        (own_expert, near(expert_rows), near(up_rows), router, raw, *inner_shards),
        "expert",
        flops=2 * product,
        grid=(shares,),
        in_specs=[
            SMEM,
            fixed(expert_rows.shape),
            fixed(up_rows.shape),
            fixed(router.shape),
            hidden_block,
            *shard_places(inner_shards),
        ],
        out_specs=[
            hidden_block,
            hidden_block,
            fixed((slots, model_width)),
            fixed((slots, model_width)),
            fixed((slots, 128)),
        ],
        scratch=[
            pltpu.VMEM((slots, 128), WIDE),
            pltpu.VMEM((slots, model_width), WIDE),
            pltpu.VMEM((slots, 128), WIDE),
            pltpu.VMEM((slots, 128), WIDE),
            *shard_scratch(inner_shards),
        ],
    )
    home_rows = blocks_over(home_slots, ("head", "blk"))
    inner_shape, outer_shape = (model_width, hidden), (hidden, model_width)
    inner_keep, inner_send, router_back = run(
        inner_grads_kernel,
        [shaped((shares // 2, *inner_shape), LOW)] * 2 + [shaped((experts, model_width), WIDE)],
        (near(expert_rows), pre_back, logit_back),
        "inner_grads",
        flops=product,
        grid=(shares,),
        in_specs=[fixed(expert_rows.shape), turned_block, fixed(logit_back.shape)],
        out_specs=[
            keep_spec(inner_shape, shares),
            send_spec(inner_shape, shares),
            fixed((experts, model_width)),
        ],
    )
    turned_shards = outer_shards[1::2] + outer_shards[0::2]
    outer_keep, outer_send, expert_out = run(
        outer_grads_kernel,
        [shaped((shares // 2, *outer_shape), LOW)] * 2 + [shaped((slots, model_width), LOW)],
        (hidden_act, out_back, *turned_shards),
        "outer_grads",
        flops=2 * product,
        grid=(shares,),
        in_specs=[turned_block, fixed(out_back.shape)] + shard_places(outer_shards),
        out_specs=[
            keep_spec(outer_shape, shares),
            send_spec(outer_shape, shares),
            fixed((slots, model_width)),
        ],
        scratch=[pltpu.VMEM((slots, model_width), WIDE)] + shard_scratch(outer_shards),
    )
    att_back, residual_back, branch_back, gain_back = run(
        after_kernel,
        [
            shaped((model_width, token_rows), LOW),
            shaped((token_rows, model_width), WIDE),
            shaped((token_rows, model_width), LOW),
            shaped((8, model_width), WIDE),
        ],
        (near(home_rows), place_column, residual_mid, gain_two, upstream_values, output_weight),
        "after",
        flops=2 * token_rows * square + 2 * slots * token_rows * model_width,
        after=(router_back, expert_out),
    )
    head_back = blocks_over(att_back.reshape(groups, width, token_rows), "head")
    packed_core, packed_sum, packed_shares = output_pieces(
        att_tok, branch_back, router_back, gain_back
    )
    *inner_parts, inner_gone = gather_shards(inner_keep, gate(inner_send, (att_back,)))
    *outer_parts, outer_gone = gather_shards(outer_keep, gate(outer_send, (att_back,)))
    turned = gate(turned, (head_back, *packed_core, inner_gone, outer_gone))
    turned_all = blocks_over(turned, "head")

    before, diagonals, home, query_backs = (), [], [], []
    for step in range(1, cycle):
        query_back, pairs_part, diagonal = attend_back(
            queries,
            head_back,
            attended,
            total,
            tile_weights[step],
            tile_pairs[step],
            before,
            False,
            0,
            groups,
            (),
        )
        before = (query_back,)
        diagonals.append(diagonal)
        home.append(turn(pairs_part, "blk", cycle - step))
    cut = groups - 1
    for begin, count, after in (
        (0, cut, packed_sum),
        (cut, groups - cut, tuple(loose(x) for x in (turned_all, *home[:1], *inner_parts[1]))),
    ):
        query_back, pairs_part, diagonal = attend_back(
            queries,
            head_back,
            attended,
            total,
            tile_weights[0],
            tile_pairs[0],
            before,
            True,
            begin,
            count,
            after,
        )
        query_backs.append(query_back)
        if begin == 0:
            out_rows = blocks_over(gate(expert_out, (loose(turned_all), query_back)), ("head", "blk"))
        diagonals.append(diagonal)
        home.append(pairs_part)
    diagonal_buckets = [*tile_buckets[1:], tile_buckets[0], tile_buckets[0]]
    layer_output = run(
        functools.partial(output_kernel, experts=experts),
        [shaped((token_rows, model_width), LOW)],
        (residual_mid, normed_two, router, chosen_column, place_column, loose(out_rows)),
        "layer_output",
        flops=2 * slots * token_rows * model_width,
    )[0]
    (
        pieces,
        query_grad,
        key_grad,
        value_grad,
        first_gain_grad,
        table_grad,
        output_grad,
        router_grad,
        second_gain_grad,
    ) = weight_sums(
        turned_all,
        query_backs,
        home,
        diagonals,
        diagonal_buckets,
        buckets,
        (query_weight, key_weight, value_weight),
        gain_one,
        experts,
        packed_shares,
        (loose(out_rows),),
        (*(loose(x) for x in outer_parts[1]), layer_output),
    )
    inner_part, inner_mark = finish_shards(*inner_parts)
    outer_part, outer_mark = finish_shards(*outer_parts)
    triples = run(
        functools.partial(triples_kernel, parts=len(query_backs)),
        [shaped((groups, 3, width, token_rows), LOW)],
        (*query_backs, *received_loose(home)),
        "triples",
        flops=0,
        after=(pieces[0], inner_mark, outer_mark),
    )[0]
    triples_tok = blocks_over(triples, "head")
    tokens_grad = run(
        tokens_grad_kernel,
        [shaped((token_rows, model_width), LOW)],
        (
            loose(triples_tok),
            query_weight,
            key_weight,
            value_weight,
            token_values,
            gain_one,
            residual_back,
        ),
        "tokens_grad",
        flops=6 * token_rows * square,
    )[0]
    return (
        layer_output[None],
        tokens_grad[None],
        first_gain_grad,
        query_grad,
        key_grad,
        value_grad,
        output_grad,
        table_grad,
        second_gain_grad,
        router_grad,
        inner_part[None],
        outer_part[None],
    )


def solution(mesh):
    return jax.shard_map(
        body,
        mesh=mesh,
        in_specs=(
            P("dp", ("blk", "head"), None),
            P(),
            P(),
            P(),
            P(),
            P(),
            P(),
            P(),
            P(),
            P(("head", "blk"), None, "dp"),
            P(("head", "blk"), "dp", None),
            P("dp", ("blk", "head")),
            P("dp", ("blk", "head")),
            P(),
            P("dp", ("blk", "head"), None),
        ),
        out_specs=(
            P("dp", ("blk", "head"), None),
            P("dp", ("blk", "head"), None),
            P(),
            P(),
            P(),
            P(),
            P(),
            P(),
            P(),
            P(),
            P(("head", "blk"), None, "dp"),
            P(("head", "blk"), "dp", None),
        ),
        check_vma=False,
    )
```
